128 devices in a mesh: px: 8 (over x, core), py: 16 (over y, z).
Axes of the slice: x: 4, y: 4, z: 4, core: 2. Of those that a mesh axis runs over, the one named last changes fastest.
Arguments:
- horiz_div: float32 [128, 1024, 1024], P('py', 'px'), may hold values from -6 to 6
- w_star: float32 [128, 1024, 1024], P('py', 'px'), may hold values from -6 to 6
- air_temp: bfloat16 [128, 1024, 1024], P('py', 'px'), may hold values from -6 to 6
- roof_level: int32 [1024, 1024], P('px'), may hold values from 0 to 63
- facet_cells: int32 [128, 4096], P(('px', 'py')), may hold values from -1 to 1048575, as said below
- facet_temp: float32 [128, 4096], P(('px', 'py')), may hold values from -6 to 6
- net_radiation: float32 [128, 4096], P(('px', 'py')), may hold values from -6 to 6
- heat_capacity: float32 [128, 4096], P(('px', 'py')), may hold values from 1 to 4
- drag_coef: float32 [128, 4096], P(('px', 'py')), may hold values from 0.05 to 0.5
- heat_coef: float32 [128, 4096], P(('px', 'py')), may hold values from 0.05 to 0.5
Outputs:
- w_new: float32 [128, 1024, 1024], P('py', 'px')
- theta_new: bfloat16 [128, 1024, 1024], P('py', 'px')
- facet_temp_new: float32 [128, 4096], P(('px', 'py'))
The draws below stay inside these ranges and needn't reach their ends.
Inputs may be any that keep to these rules, and one draw needn't show every extreme that they name: `facet_cells`: in each block of 32 rows the non-empty rows come first. For every device one owner's block is full, the same owner for all devices.
All inputs are finite; a program needn't handle non-finite values.
Results may differ from the reference program's by a relative error of at most 0.001.
Values sent between devices are 32-bit elements; how exact they have to be, the bound alone decides.
No kernel may reach another device: no remote copies, remote signals or barrier semaphores. Data moves between devices by JAX's collectives and lax.ppermute only.
A program may use at most 128 MiB of HBM per device.

```python
import math
import jax
import jax.numpy as jnp
from jax import lax

NX = 1024
NY = 1024
NZ = 128
SLOT = 32
CELLS_DEV = 1048576
N_PX = 8
N_PY = 16
DEVICES = 128


def draw_facet_cells(key, part):
    key_counts, key_busy, key_cells = jax.random.split(jax.random.fold_in(key, 11), 3)
    counts = jax.random.randint(key_counts, (DEVICES, DEVICES), SLOT // 4, SLOT + 1)
    busy_owner = jax.random.randint(key_busy, (), 0, DEVICES)
    owner_ids = jnp.arange(DEVICES, dtype=jnp.int32)
    counts = jnp.where(owner_ids[None, :] == busy_owner, SLOT, counts)
    slot_ids = jnp.arange(SLOT, dtype=jnp.int32)
    is_live = slot_ids[None, None, :] < counts[:, :, None]
    cell_ids = jax.random.randint(key_cells, (DEVICES, DEVICES, SLOT), 0, CELLS_DEV)
    cell_ids = cell_ids.at[0, busy_owner, 0].set(CELLS_DEV - 1)
    return jnp.where(is_live, cell_ids, -1).reshape(DEVICES, DEVICES * SLOT).astype(jnp.int32)


def touch_ends(result, stream_key, least, high):
    longest = result.shape.index(max(result.shape))
    spots = []
    for shift in (0, 1):
        where = [jax.random.randint(jax.random.fold_in(stream_key, axis), (), 0, length) for axis, length in enumerate(result.shape)]
        where[longest] = (where[longest] + shift) % result.shape[longest]
        spots.append(tuple(where))
    return result.at[spots[0]].set(least).at[spots[1]].set(high)


def block_levels(own_key, shape, cuts, least, high):
    def one(axis_at, shards_of):
        steps = jax.random.uniform(jax.random.fold_in(jax.random.fold_in(own_key, 6), axis_at), (shards_of,), jnp.float32, least / len(cuts), high / len(cuts))
        return jnp.repeat(jnp.exp(steps), shape[axis_at] // shards_of).reshape((-1,) + (1,) * (len(shape) - axis_at - 1))

    loudness = one(*cuts[0])
    for cut in cuts[1:]:
        loudness = loudness * one(*cut)
    return loudness


def gaussian(stream_key, shape, width, limit, cuts=(), kind=jnp.bfloat16):
    array = width * jax.random.normal(stream_key, shape, jnp.float32)
    if cuts:
        array = array * block_levels(stream_key, shape, cuts, -0.22, 0.18)
    return jnp.clip(array, -limit, limit).astype(kind)


def setup_inputs(seed: int = 0) -> dict:
    streams_of = jax.random.split(jax.random.key(seed), 11)
    return {
        "horiz_div": gaussian(streams_of[0], (NZ, NY, NX), 1.0, 6.0, ((0, 16), (1, 8)), jnp.float32),
        "w_star": gaussian(streams_of[1], (NZ, NY, NX), 1.0, 6.0, ((0, 16), (1, 8)), jnp.float32),
        "air_temp": gaussian(streams_of[2], (NZ, NY, NX), 1.0, 6.0, ((0, 16), (1, 8))),
        "roof_level": touch_ends(jax.random.randint(streams_of[3], (NY, NX), 0, NZ // 2), jax.random.fold_in(streams_of[3], 1), 0, (NZ // 2) - 1).astype(jnp.int32),
        "facet_cells": draw_facet_cells(jax.random.fold_in(streams_of[10], 71), 0),
        "facet_temp": gaussian(streams_of[5], (DEVICES, DEVICES * SLOT), 1.0, 6.0, ((0, 128),), jnp.float32),
        "net_radiation": gaussian(streams_of[6], (DEVICES, DEVICES * SLOT), 1.0, 6.0, ((0, 128),), jnp.float32),
        "heat_capacity": jnp.clip(jnp.exp(math.log(4.0) - 1.3862944 * jax.random.uniform(streams_of[7], (DEVICES, DEVICES * SLOT), jnp.float32) ** block_levels(streams_of[7], (DEVICES, DEVICES * SLOT), ((0, 128),), -0.2, 0.2)), 1.0, 4.0),
        "drag_coef": jnp.clip(jnp.exp(math.log(0.5) - 2.3025851 * jax.random.uniform(streams_of[8], (DEVICES, DEVICES * SLOT), jnp.float32) ** block_levels(streams_of[8], (DEVICES, DEVICES * SLOT), ((0, 128),), -0.2, 0.2)), 0.05, 0.5),
        "heat_coef": jnp.clip(jnp.exp(math.log(0.5) - 2.3025851 * jax.random.uniform(streams_of[9], (DEVICES, DEVICES * SLOT), jnp.float32) ** block_levels(streams_of[9], (DEVICES, DEVICES * SLOT), ((0, 128),), -0.2, 0.2)), 0.05, 0.5),
    }


def to_devices(field):
    shaped = field.reshape(N_PY, NZ // N_PY, N_PX, NY // N_PX, NX)
    return shaped.transpose(2, 0, 1, 3, 4).reshape(DEVICES, -1)

def from_devices(device_rows):
    shaped = device_rows.reshape(N_PX, N_PY, NZ // N_PY, NY // N_PX, NX)
    return shaped.transpose(1, 2, 0, 3, 4).reshape(NZ, NY, NX)

def owner_major(values):
    return values.reshape(DEVICES, DEVICES, SLOT).transpose(1, 0, 2).reshape(DEVICES, DEVICES * SLOT)

def reference(horiz_div, w_star, air_temp, roof_level, facet_cells, facet_temp, net_radiation, heat_capacity, drag_coef, heat_coef):
    is_live = facet_cells >= 0
    safe_ids = jnp.maximum(facet_cells, 0).astype(jnp.int32)
    w_rows = to_devices(w_star)
    temp_rows = to_devices(air_temp.astype(jnp.float32))
    w_cell = jnp.where(is_live, jnp.take_along_axis(w_rows, safe_ids, axis=1), 0.0)
    temp_cell = jnp.where(is_live, jnp.take_along_axis(temp_rows, safe_ids, axis=1), 0.0)
    w_owner = owner_major(w_cell)
    temp_owner = owner_major(temp_cell)
    speeds = jnp.sqrt(w_owner * w_owner + 0.25)
    stress = drag_coef * speeds * w_owner
    heat_flux = heat_coef * speeds * (facet_temp - temp_owner)
    facet_temp_new = facet_temp + (net_radiation - heat_flux - 0.5 * facet_temp) / heat_capacity
    stress_src = jnp.where(is_live, owner_major(stress), 0.0)
    heat_src = jnp.where(is_live, owner_major(heat_flux), 0.0)
    device_ids = jnp.arange(DEVICES, dtype=jnp.int32)[:, None]
    w_rows = w_rows.at[device_ids, safe_ids].add(-stress_src)
    temp_rows = temp_rows.at[device_ids, safe_ids].add(heat_src)
    w_corr = from_devices(w_rows)
    theta_new = from_devices(temp_rows).astype(jnp.bfloat16)
    w_up = jnp.concatenate([w_corr[1:], jnp.zeros((1, NY, NX), jnp.float32)], axis=0)
    rhs = horiz_div + w_up - w_corr
    spectrum = jnp.fft.rfft2(rhs, axes=(1, 2))
    eigen_x = 2.0 * jnp.cos(2.0 * math.pi / NX * jnp.arange(NX // 2 + 1, dtype=jnp.float32)) - 2.0
    eigen_y = 2.0 * jnp.cos(2.0 * math.pi / NY * jnp.arange(NY, dtype=jnp.float32)) - 2.0
    stacked = jnp.stack([spectrum.real, spectrum.imag], axis=-1).transpose(1, 2, 0, 3)
    main_diag = jnp.full((NZ,), -2.0, jnp.float32).at[0].set(-1.0).at[NZ - 1].set(-3.0)
    lower_diag = jnp.ones((NZ,), jnp.float32).at[0].set(0.0)
    upper_diag = jnp.ones((NZ,), jnp.float32).at[NZ - 1].set(0.0)

    def solve_row(pieces):
        mode_row, shift_y = pieces
        diagonal = main_diag[None, :] + (shift_y + eigen_x)[:, None]
        lower_full = jnp.broadcast_to(lower_diag, diagonal.shape)
        upper_full = jnp.broadcast_to(upper_diag, diagonal.shape)
        return lax.linalg.tridiagonal_solve(lower_full, diagonal, upper_full, mode_row)
    solved = lax.map(solve_row, (stacked, eigen_y))
    spectrum_p = (solved[..., 0] + 1j * solved[..., 1]).transpose(2, 0, 1)
    potential = jnp.fft.irfft2(spectrum_p, s=(NY, NX), axes=(1, 2))
    slope = potential - jnp.concatenate([potential[:1], potential[:-1]], axis=0)
    level_ids = jnp.arange(NZ, dtype=jnp.int32)
    inside_solid = level_ids[:, None, None] < roof_level[None, :, :]
    w_new = jnp.where(inside_solid, 0.0, w_corr - slope).astype(w_corr.dtype)
    return (w_new, theta_new, facet_temp_new)
```

```python
import functools
import math

import jax
import jax.numpy as jnp
import numpy as np
from jax import lax
from jax.experimental import pallas as pl
from jax.experimental.pallas import tpu as pltpu
from jax.sharding import PartitionSpec as P

N = 1024
NPX, NPY = 8, 16
LEV, ROWS = 8, 128
OWNERS, SLOT = 128, 32
MIB = 1 << 20
F32, BF16 = jnp.float32, jnp.bfloat16


def mode_table():
    classes = [np.arange(0, 513, 4), np.arange(2, 513, 4), np.arange(1, 512, 2)]
    n = np.arange(N)
    cols, waves = [], []
    for ks in classes:
        for k in ks:
            edge = k == 0 or k == N // 2
            norm = math.sqrt((1.0 if edge else 2.0) / N)
            cols.append(norm * np.cos(2 * np.pi * ((n * k) % N) / N))
            waves.append(k)
        for k in ks:
            if k == 0 or k == N // 2:
                continue
            cols.append(math.sqrt(2.0 / N) * np.sin(2 * np.pi * ((n * k) % N) / N))
            waves.append(k)
    table = np.stack(cols, axis=1)
    eigen = -4.0 * np.sin(np.pi * np.array(waves) / N) ** 2
    return table, eigen


def split_np(a):
    a = a.astype(np.float32)
    hi = a.astype(jnp.bfloat16)
    lo = (a - hi.astype(np.float32)).astype(jnp.bfloat16)
    return hi, lo


TABLE, EIGEN = mode_table()
T_EE = TABLE[:256, :256]
T_EO = TABLE[:256, 256:512]
T_OD = TABLE[:512, 512:]


def split(v):
    hi = v.astype(BF16)
    return hi, (v - hi.astype(F32)).astype(BF16)


def dot3(ah, al, bh, bl):
    d = functools.partial(jnp.dot, preferred_element_type=F32)
    return d(ah, bh) + (d(al, bh) + d(ah, bl))


def params(mb, sem=None):
    return pltpu.CompilerParams(vmem_limit_bytes=mb * MIB)


VM = pl.BlockSpec(memory_space=pltpu.VMEM)
SM = pl.BlockSpec(memory_space=pltpu.SMEM)


def load_tiles(w_ref, a_ref, wt, tt):
    def one(i, c):
        for half in range(2):
            tr = 2 * i + half
            for ct in range(8):
                wt[pl.ds(pl.multiple_of(tr * 64 + ct * 8, 8), 8), :] = w_ref[
                    pl.ds(pl.multiple_of(tr * 8, 8), 8), ct * 128:(ct + 1) * 128]
        for ct in range(8):
            v = a_ref[pl.ds(pl.multiple_of(i * 16, 16), 16), ct * 128:(ct + 1) * 128].astype(F32)
            tt[pl.ds(pl.multiple_of(i * 128 + ct * 8, 8), 8), :] = v[:8]
            tt[pl.ds(pl.multiple_of(i * 128 + 64 + ct * 8, 8), 8), :] = v[8:]
        return c
    lax.fori_loop(0, 64, one, 0)


def gather_kernel(addr, ids_ref, w_ref, a_ref, wc_ref, tc_ref, wt, tt, gw, gt):
    load_tiles(w_ref, a_ref, wt, tt)

    def one(o, c):
        for s in range(SLOT):
            a = addr[o * SLOT + s]
            gw[pl.ds(s * OWNERS + o, 1), :] = wt[pl.ds(a, 1), :]
            gt[pl.ds(s * OWNERS + o, 1), :] = tt[pl.ds(a, 1), :]
        return c
    lax.fori_loop(0, OWNERS, one, 0)
    ids = ids_ref[...]
    lane = lax.broadcasted_iota(jnp.int32, (OWNERS, 128), 1)
    slot = lax.broadcasted_iota(jnp.int32, (OWNERS, SLOT), 1)
    wc = jnp.zeros((OWNERS, SLOT), F32)
    tc = jnp.zeros((OWNERS, SLOT), F32)
    for s in range(SLOT):
        col = ids[:, s:s + 1]
        hit = lane == jnp.where(col >= 0, col & 127, -1)
        rows = slice(s * OWNERS, (s + 1) * OWNERS)
        wv = jnp.sum(jnp.where(hit, gw[rows, :], 0.0), axis=1, keepdims=True)
        tv = jnp.sum(jnp.where(hit, gt[rows, :], 0.0), axis=1, keepdims=True)
        wc = jnp.where(slot == s, wv, wc)
        tc = jnp.where(slot == s, tv, tc)
    wc_ref[...] = wc
    tc_ref[...] = tc


def gather_cells(addr, ids, w2, a2):
    out = jax.ShapeDtypeStruct((OWNERS, SLOT), F32)
    return pl.pallas_call(
        gather_kernel, out_shape=(out, out), in_specs=[SM, VM, VM, VM], out_specs=(VM, VM),
        scratch_shapes=[pltpu.VMEM((8192, 128), F32), pltpu.VMEM((8192, 128), F32),
                        pltpu.VMEM((4096, 128), F32), pltpu.VMEM((4096, 128), F32)],
        compiler_params=params(40), name="facet_gather",
    )(addr, ids, w2, a2)


def scatter_kernel(addr, ids_ref, wc_ref, tc_ref, od_ref, w_ref, a_ref,
                   wo_ref, th_ref, heat_ref, wt, tt, cw, ct_):
    load_tiles(w_ref, a_ref, wt, tt)
    ids = ids_ref[...]
    wc, tc = wc_ref[...], tc_ref[...]
    ft, drag, heat = od_ref[:, 0:32], od_ref[:, 32:64], od_ref[:, 64:96]
    speed = jnp.sqrt(wc * wc + 0.25)
    stress = drag * speed * wc
    flux = heat * speed * (ft - tc)
    heat_ref[...] = flux
    lane = lax.broadcasted_iota(jnp.int32, (OWNERS, 128), 1)
    for s in range(SLOT):
        col = ids[:, s:s + 1]
        hit = lane == jnp.where(col >= 0, col & 127, -1)
        rows = slice(s * OWNERS, (s + 1) * OWNERS)
        cw[rows, :] = jnp.where(hit, -stress[:, s:s + 1], 0.0)
        ct_[rows, :] = jnp.where(hit, flux[:, s:s + 1], 0.0)

    def one(o, c):
        for s in range(SLOT):
            a = addr[o * SLOT + s]
            wt[pl.ds(a, 1), :] = wt[pl.ds(a, 1), :] + cw[pl.ds(s * OWNERS + o, 1), :]
            tt[pl.ds(a, 1), :] = tt[pl.ds(a, 1), :] + ct_[pl.ds(s * OWNERS + o, 1), :]
        return c
    lax.fori_loop(0, OWNERS, one, 0)

    def put(i, c):
        for half in range(2):
            tr = 2 * i + half
            for ct in range(8):
                wo_ref[pl.ds(pl.multiple_of(tr * 8, 8), 8), ct * 128:(ct + 1) * 128] = wt[
                    pl.ds(pl.multiple_of(tr * 64 + ct * 8, 8), 8), :]
        for ct in range(8):
            v0 = tt[pl.ds(pl.multiple_of(i * 128 + ct * 8, 8), 8), :]
            v1 = tt[pl.ds(pl.multiple_of(i * 128 + 64 + ct * 8, 8), 8), :]
            th_ref[pl.ds(pl.multiple_of(i * 16, 16), 16), ct * 128:(ct + 1) * 128] = (
                jnp.concatenate([v0, v1], axis=0).astype(BF16))
        return c
    lax.fori_loop(0, 64, put, 0)


def scatter_fluxes(addr, ids, wc, tc, od, w2, a2):
    return pl.pallas_call(
        scatter_kernel,
        out_shape=(jax.ShapeDtypeStruct((1024, 1024), F32), jax.ShapeDtypeStruct((1024, 1024), BF16),
                   jax.ShapeDtypeStruct((OWNERS, SLOT), F32)),
        in_specs=[SM, VM, VM, VM, VM, VM, VM], out_specs=(VM, VM, VM),
        scratch_shapes=[pltpu.VMEM((8192, 128), F32), pltpu.VMEM((8192, 128), F32),
                        pltpu.VMEM((4096, 128), F32), pltpu.VMEM((4096, 128), F32)],
        compiler_params=params(48), name="facet_scatter",
    )(addr, ids, wc, tc, od, w2, a2)


def x_forward_kernel(h_ref, w_ref, wn_ref, halo_ref, eh, el, oh, ol, dh, dl, out_ref):
    step = pl.program_id(0)
    up = jnp.where(step == 3, halo_ref[0], wn_ref[0])
    r0 = h_ref[0] + w_ref[1] - w_ref[0]
    r1 = h_ref[1] + up - w_ref[1]
    r = jnp.concatenate([r0, r1], axis=0)
    s, d = r[:, :512] + r[:, 512:], r[:, :512] - r[:, 512:]
    ee, eo = s[:, :256] + s[:, 256:], s[:, :256] - s[:, 256:]

    def put(res, b0):
        for b in range(res.shape[1] // 128):
            for l in range(2):
                out_ref[b0 + b, l] = res[l * 128:(l + 1) * 128, b * 128:(b + 1) * 128]
    put(dot3(*split(ee), eh[...], el[...]), 0)
    put(dot3(*split(eo), oh[...], ol[...]), 2)
    put(dot3(*split(d), dh[...], dl[...]), 4)


def table_specs():
    small = pl.BlockSpec((256, 256), lambda g: (0, 0))
    big = pl.BlockSpec((512, 512), lambda g: (0, 0))
    return [small] * 4 + [big] * 2


def tables(transposed):
    out = []
    for t in (T_EE, T_EO, T_OD):
        out += [jnp.asarray(v) for v in split_np(t.T if transposed else t)]
    return out


def x_forward(h, w, halo):
    return pl.pallas_call(
        x_forward_kernel, grid=(4,),
        out_shape=jax.ShapeDtypeStruct((NPX, LEV, ROWS, 128), F32),
        in_specs=[pl.BlockSpec((2, 128, 1024), lambda g: (g, 0, 0)),
                  pl.BlockSpec((2, 128, 1024), lambda g: (g, 0, 0)),
                  pl.BlockSpec((1, 128, 1024), lambda g: (jnp.minimum(2 * g + 2, 7), 0, 0)),
                  pl.BlockSpec((1, 128, 1024), lambda g: (0, 0, 0))] + table_specs(),
        out_specs=pl.BlockSpec((NPX, 2, ROWS, 128), lambda g: (0, g, 0, 0)),
        compiler_params=params(40), name="x_forward",
    )(h, w, w, halo, *tables(False))


def slab_polys(lam):
    phi = [None] * 9
    phi[8] = jnp.ones_like(lam)
    delta = -lam
    phi[7] = phi[8] + delta
    for k in range(6, -1, -1):
        delta = delta - lam * phi[k + 1]
        phi[k] = phi[k + 1] + delta
    theta = [jnp.ones_like(lam), 2.0 - lam]
    for k in range(2, 8):
        theta.append((2.0 - lam) * theta[k - 1] - theta[k - 2])
    return phi, theta, delta


def y_forward_kernel(x_ref, lam_ref, eh, el, oh, ol, dh, dl, r_ref, al_ref, keep):
    step = pl.program_id(0)
    x = jnp.concatenate([x_ref[:, 0], x_ref[:, 1]], axis=-1).reshape(1024, 256)
    s, d = x[:512] + x[512:], x[:512] - x[512:]
    ee, eo = s[:256] + s[256:], s[:256] - s[256:]

    def left(th, tl, v):
        vh, vl = split(v)
        return dot3(th, tl, vh, vl)

    def put(res, k0):
        for l in range(2):
            part = res[:, l * 128:(l + 1) * 128]
            r_ref[l, k0:k0 + res.shape[0], :] = part
            keep[2 * step + l, k0:k0 + res.shape[0], :] = part
    put(left(eh[...], el[...], ee), 0)
    put(left(oh[...], ol[...], eo), 256)
    put(left(dh[...], dl[...], d), 512)

    @pl.when(step == 3)
    def _():
        def one(t, c):
            rows = pl.ds(pl.multiple_of(t * 16, 16), 16)
            phi, theta, _ = slab_polys(lam_ref[rows, :])
            inv = -1.0 / phi[0]
            a0 = phi[1] * keep[0, rows, :]
            a7 = keep[0, rows, :]
            for k in range(1, 8):
                a0 = a0 + phi[k + 1] * keep[k, rows, :]
                a7 = a7 + theta[k] * keep[k, rows, :]
            inner = pl.ds(pl.multiple_of((t % 4) * 16, 16), 16)
            al_ref[t // 4, 0, inner, :] = a0 * inv
            al_ref[t // 4, 1, inner, :] = a7 * inv
            return c
        lax.fori_loop(0, 64, one, 0)


def y_forward(x, lam):
    whole = pl.BlockSpec((N, 128), lambda g: (0, 0))
    return pl.pallas_call(
        y_forward_kernel, grid=(4,),
        out_shape=(jax.ShapeDtypeStruct((LEV, N, 128), F32), jax.ShapeDtypeStruct((NPY, 2, 64, 128), F32)),
        in_specs=[pl.BlockSpec((NPX, 2, ROWS, 128), lambda g: (0, g, 0, 0)), whole] + table_specs(),
        out_specs=(pl.BlockSpec((2, N, 128), lambda g: (g, 0, 0)),
                   pl.BlockSpec((NPY, 2, 64, 128), lambda g: (0, 0, 0, 0))),
        scratch_shapes=[pltpu.VMEM((LEV, N, 128), F32)],
        compiler_params=params(40), name="y_forward",
    )(x, lam, *tables(True))


def ladder_kernel(al_ref, lam_ref, out_ref):
    for t in range(8):
        rows = slice(t * 8, (t + 1) * 8)
        phi, theta, delta = slab_polys(lam_ref[rows, :])
        inv = 1.0 / phi[0]
        n07, n77, c = inv, theta[7] * inv, delta * inv
        A = [None] * 17
        B = [None] * 17
        e = [None] * 17
        A[16] = jnp.zeros_like(inv)
        B[16] = jnp.full_like(inv, -2.0)
        for j in range(15, -1, -1):
            g, q = al_ref[j, 0, rows, :], al_ref[j, 1, rows, :]
            e[j + 1] = 1.0 / (1.0 - n77 * B[j + 1])
            be = B[j + 1] * e[j + 1]
            A[j] = g + n07 * (A[j + 1] + be * (q + n77 * A[j + 1]))
            B[j] = n07 * n07 * be - c
        p = -A[0] / B[0]
        for j in range(16):
            out_ref[j, 0, rows, :] = p
            p = (al_ref[j, 1, rows, :] + n77 * A[j + 1] + n07 * p) * e[j + 1]
            out_ref[j, 1, rows, :] = A[j + 1] + B[j + 1] * p


def ladder(al, lam):
    return pl.pallas_call(
        ladder_kernel, out_shape=jax.ShapeDtypeStruct((NPY, 2, 64, 128), F32),
        in_specs=[VM, VM], out_specs=VM, compiler_params=params(16), name="ladder",
    )(al, lam)


def y_inverse_kernel(r_ref, pu_ref, lam_ref, eh, el, oh, ol, dh, dl, out_ref, sh, sl):
    step = pl.program_id(0)

    @pl.when(step == 0)
    def _():
        def one(t, c):
            rows = pl.ds(pl.multiple_of(t * 16, 16), 16)
            inner = pl.ds(pl.multiple_of((t % 4) * 16, 16), 16)
            low = pu_ref[t // 4, 0, inner, :]
            top = pu_ref[t // 4, 1, inner, :]
            lam = lam_ref[rows, :]
            cs = [None] * 8
            fs = [None] * 8
            cs[7] = 1.0 / (1.0 - lam)
            fs[7] = top_f = -r_ref[7, rows, :] - (-top)
            for k in range(6, -1, -1):
                cs[k] = 1.0 / (2.0 - lam - cs[k + 1])
                f = -r_ref[k, rows, :]
                if k == 0:
                    f = f + low
                fs[k] = f + cs[k + 1] * fs[k + 1]
            prev = low
            for k in range(8):
                p = cs[k] * (fs[k] + prev) if k else cs[k] * fs[k]
                hi, lo = split(p - prev)
                sh[k // 2, rows, (k % 2) * 128:(k % 2 + 1) * 128] = hi
                sl[k // 2, rows, (k % 2) * 128:(k % 2 + 1) * 128] = lo
                prev = p
            return c
        lax.fori_loop(0, 64, one, 0)

    def left(th, tl, lo, hi):
        return dot3(th, tl, sh[step, lo:hi, :], sl[step, lo:hi, :])
    t0 = left(eh[...], el[...], 0, 256)
    t1 = left(oh[...], ol[...], 256, 512)
    d = left(dh[...], dl[...], 512, 1024)
    ev = (t0 + t1, t0 - t1)
    for i in range(4):
        base = ev[i // 2][(i % 2) * 128:(i % 2 + 1) * 128]
        odd = d[i * 128:(i + 1) * 128]
        for l in range(2):
            cols = slice(l * 128, (l + 1) * 128)
            out_ref[i, l] = base[:, cols] + odd[:, cols]
            out_ref[i + 4, l] = base[:, cols] - odd[:, cols]


def y_inverse(r, pu, lam):
    return pl.pallas_call(
        y_inverse_kernel, grid=(4,),
        out_shape=jax.ShapeDtypeStruct((NPX, LEV, ROWS, 128), F32),
        in_specs=[pl.BlockSpec((LEV, N, 128), lambda g: (0, 0, 0)),
                  pl.BlockSpec((NPY, 2, 64, 128), lambda g: (0, 0, 0, 0)),
                  pl.BlockSpec((N, 128), lambda g: (0, 0))] + table_specs(),
        out_specs=pl.BlockSpec((NPX, 2, ROWS, 128), lambda g: (0, g, 0, 0)),
        scratch_shapes=[pltpu.VMEM((4, N, 256), BF16), pltpu.VMEM((4, N, 256), BF16)],
        compiler_params=params(40), name="y_inverse",
    )(r, pu, lam, *tables(False))


def x_inverse_kernel(base_ref, y_ref, w_ref, roof_ref, eh, el, oh, ol, dh, dl, out_ref):
    step = pl.program_id(0)

    def cat(b0, b1):
        return jnp.concatenate(
            [jnp.concatenate([y_ref[b, l] for b in range(b0, b1)], axis=1) for l in range(2)], axis=0)
    t0 = dot3(*split(cat(0, 2)), eh[...], el[...])
    t1 = dot3(*split(cat(2, 4)), oh[...], ol[...])
    d = dot3(*split(cat(4, 8)), dh[...], dl[...])
    s = jnp.concatenate([t0 + t1, t0 - t1], axis=1)
    for half, slope in ((0, s + d), (1, s - d)):
        cols = slice(half * 512, (half + 1) * 512)
        for l in range(2):
            level = base_ref[0] + 2 * step + l
            solid = level < roof_ref[:, cols]
            out_ref[l, :, cols] = jnp.where(solid, 0.0, w_ref[l, :, cols] - slope[l * 128:(l + 1) * 128])


def x_inverse(base, y, w, roof):
    return pl.pallas_call(
        x_inverse_kernel, grid=(4,),
        out_shape=jax.ShapeDtypeStruct((LEV, ROWS, N), F32),
        in_specs=[SM, pl.BlockSpec((NPX, 2, ROWS, 128), lambda g: (0, g, 0, 0)),
                  pl.BlockSpec((2, ROWS, N), lambda g: (g, 0, 0)),
                  pl.BlockSpec((ROWS, N), lambda g: (0, 0))] + table_specs(),
        out_specs=pl.BlockSpec((2, ROWS, N), lambda g: (g, 0, 0)),
        compiler_params=params(40), name="x_inverse",
    )(base, y, w, roof, *tables(True))


def swap(x, axes):
    return lax.all_to_all(x, axes, split_axis=0, concat_axis=0, tiled=True)


def body(horiz_div, w_star, air_temp, roof_level, facet_cells, facet_temp, net_radiation,
         heat_capacity, drag_coef, heat_coef):
    ix, iy = lax.axis_index("px"), lax.axis_index("py")
    owner = jnp.concatenate(
        [v.reshape(OWNERS, 1, SLOT) for v in (facet_temp, drag_coef, heat_coef, jnp.zeros_like(heat_coef))],
        axis=2)
    arrived = swap(owner, ("px", "py")).reshape(OWNERS, 128)
    cells = facet_cells[0]
    safe = jnp.maximum(cells, 0)
    row = safe >> 10
    addr = (row >> 3) * 64 + ((safe >> 7) & 7) * 8 + (row & 7)
    ids = facet_cells.reshape(OWNERS, SLOT)
    w2, a2 = w_star.reshape(1024, 1024), air_temp.reshape(1024, 1024)
    wc, tc = gather_cells(addr, ids, w2, a2)
    w_corr, theta, flux = scatter_fluxes(addr, ids, wc, tc, arrived, w2, a2)
    flux_back = swap(flux.reshape(OWNERS, 1, SLOT), ("px", "py")).reshape(1, OWNERS * SLOT)
    temp_new = facet_temp + (net_radiation - flux_back - 0.5 * facet_temp) / heat_capacity
    w_corr = w_corr.reshape(LEV, ROWS, N)
    halo = lax.ppermute(w_corr[:1], "py", [(j, j - 1) for j in range(1, NPY)])

    eig = jnp.asarray(EIGEN.astype(np.float32))
    eig_x = lax.dynamic_slice_in_dim(eig, ix * 128, 128)
    eig_y = lax.dynamic_slice_in_dim(eig, iy * 64, 64)
    lam = eig[:, None] + eig_x[None, :]
    lam_mine = eig_y[:, None] + eig_x[None, :]

    xs = swap(x_forward(horiz_div, w_corr, halo), "px")
    r, al = y_forward(xs, lam)
    pu = swap(ladder(swap(al, "py"), lam_mine), "py")
    ys = swap(y_inverse(r, pu, lam), "px")
    base = (iy * LEV).astype(jnp.int32).reshape(1)
    w_new = x_inverse(base, ys, w_corr, roof_level)
    return w_new, theta.reshape(LEV, ROWS, N), temp_new


def solution(mesh):
    field, facet = P("py", "px", None), P(("px", "py"), None)
    return jax.shard_map(
        body, mesh=mesh,
        in_specs=(field, field, field, P("px", None)) + (facet,) * 6,
        out_specs=(field, field, facet), check_vma=False)
```

```python
import functools
import math

import jax
import jax.numpy as jnp
import numpy as np
from jax import lax
from jax.experimental import pallas as pl
from jax.experimental.pallas import tpu as pltpu
from jax.sharding import PartitionSpec as P

N = 1024
NPX, NPY = 8, 16
LEV, ROWS = 8, 128
OWNERS, SLOT = 128, 32
MIB = 1 << 20
F32, BF16 = jnp.float32, jnp.bfloat16


def mode_table():
    classes = [np.arange(0, 513, 4), np.arange(2, 513, 4), np.arange(1, 512, 2)]
    n = np.arange(N)
    cols, waves = [], []
    for ks in classes:
        for k in ks:
            edge = k == 0 or k == N // 2
            norm = math.sqrt((1.0 if edge else 2.0) / N)
            cols.append(norm * np.cos(2 * np.pi * ((n * k) % N) / N))
            waves.append(k)
        for k in ks:
            if k == 0 or k == N // 2:
                continue
            cols.append(math.sqrt(2.0 / N) * np.sin(2 * np.pi * ((n * k) % N) / N))
            waves.append(k)
    table = np.stack(cols, axis=1)
    eigen = -4.0 * np.sin(np.pi * np.array(waves) / N) ** 2
    return table, eigen


def split_np(a):
    a = a.astype(np.float32)
    hi = a.astype(jnp.bfloat16)
    lo = (a - hi.astype(np.float32)).astype(jnp.bfloat16)
    return hi, lo


TABLE, EIGEN = mode_table()
T_EE = TABLE[:256, :256]
T_EO = TABLE[:256, 256:512]
T_OD = TABLE[:512, 512:]


def split(v):
    hi = v.astype(BF16)
    return hi, (v - hi.astype(F32)).astype(BF16)


def dot3(ah, al, bh, bl):
    d = functools.partial(jnp.dot, preferred_element_type=F32)
    return d(ah, bh) + (d(al, bh) + d(ah, bl))


def params(mb, sem=None):
    return pltpu.CompilerParams(vmem_limit_bytes=mb * MIB)


VM = pl.BlockSpec(memory_space=pltpu.VMEM)
SM = pl.BlockSpec(memory_space=pltpu.SMEM)


def load_tiles(w_ref, a_ref, wt, tt):
    def one(i, c):
        for half in range(2):
            tr = 2 * i + half
            for ct in range(8):
                wt[pl.ds(pl.multiple_of(tr * 64 + ct * 8, 8), 8), :] = w_ref[
                    pl.ds(pl.multiple_of(tr * 8, 8), 8), ct * 128:(ct + 1) * 128]
        for ct in range(8):
            v = a_ref[pl.ds(pl.multiple_of(i * 16, 16), 16), ct * 128:(ct + 1) * 128].astype(F32)
            tt[pl.ds(pl.multiple_of(i * 128 + ct * 8, 8), 8), :] = v[:8]
            tt[pl.ds(pl.multiple_of(i * 128 + 64 + ct * 8, 8), 8), :] = v[8:]
        return c
    lax.fori_loop(0, 64, one, 0)


def gather_kernel(addr, ids_ref, w_ref, a_ref, wc_ref, tc_ref, wt, tt, gw, gt):
    load_tiles(w_ref, a_ref, wt, tt)

    def one(o, c):
        for s in range(SLOT):
            a = addr[o * SLOT + s]
            gw[pl.ds(s * OWNERS + o, 1), :] = wt[pl.ds(a, 1), :]
            gt[pl.ds(s * OWNERS + o, 1), :] = tt[pl.ds(a, 1), :]
        return c
    lax.fori_loop(0, OWNERS, one, 0)
    ids = ids_ref[...]
    lane = lax.broadcasted_iota(jnp.int32, (OWNERS, 128), 1)
    slot = lax.broadcasted_iota(jnp.int32, (OWNERS, SLOT), 1)
    wc = jnp.zeros((OWNERS, SLOT), F32)
    tc = jnp.zeros((OWNERS, SLOT), F32)
    for s in range(SLOT):
        col = ids[:, s:s + 1]
        hit = lane == jnp.where(col >= 0, col & 127, -1)
        rows = slice(s * OWNERS, (s + 1) * OWNERS)
        wv = jnp.sum(jnp.where(hit, gw[rows, :], 0.0), axis=1, keepdims=True)
        tv = jnp.sum(jnp.where(hit, gt[rows, :], 0.0), axis=1, keepdims=True)
        wc = jnp.where(slot == s, wv, wc)
        tc = jnp.where(slot == s, tv, tc)
    wc_ref[...] = wc
    tc_ref[...] = tc


def gather_cells(addr, ids, w2, a2):
    out = jax.ShapeDtypeStruct((OWNERS, SLOT), F32)
    return pl.pallas_call(
        gather_kernel, out_shape=(out, out), in_specs=[SM, VM, VM, VM], out_specs=(VM, VM),
        scratch_shapes=[pltpu.VMEM((8192, 128), F32), pltpu.VMEM((8192, 128), F32),
                        pltpu.VMEM((4096, 128), F32), pltpu.VMEM((4096, 128), F32)],
        compiler_params=params(40), name="facet_gather",
    )(addr, ids, w2, a2)


def scatter_kernel(addr, ids_ref, wc_ref, tc_ref, od_ref, w_ref, a_ref,
                   wo_ref, th_ref, heat_ref, wt, tt, cw, ct_):
    load_tiles(w_ref, a_ref, wt, tt)
    ids = ids_ref[...]
    wc, tc = wc_ref[...], tc_ref[...]
    ft, drag, heat = od_ref[:, 0:32], od_ref[:, 32:64], od_ref[:, 64:96]
    speed = jnp.sqrt(wc * wc + 0.25)
    stress = drag * speed * wc
    flux = heat * speed * (ft - tc)
    heat_ref[...] = flux
    lane = lax.broadcasted_iota(jnp.int32, (OWNERS, 128), 1)
    for s in range(SLOT):
        col = ids[:, s:s + 1]
        hit = lane == jnp.where(col >= 0, col & 127, -1)
        rows = slice(s * OWNERS, (s + 1) * OWNERS)
        cw[rows, :] = jnp.where(hit, -stress[:, s:s + 1], 0.0)
        ct_[rows, :] = jnp.where(hit, flux[:, s:s + 1], 0.0)

    def one(o, c):
        for s in range(SLOT):
            a = addr[o * SLOT + s]
            wt[pl.ds(a, 1), :] = wt[pl.ds(a, 1), :] + cw[pl.ds(s * OWNERS + o, 1), :]
            tt[pl.ds(a, 1), :] = tt[pl.ds(a, 1), :] + ct_[pl.ds(s * OWNERS + o, 1), :]
        return c
    lax.fori_loop(0, OWNERS, one, 0)

    def put(i, c):
        for half in range(2):
            tr = 2 * i + half
            for ct in range(8):
                wo_ref[pl.ds(pl.multiple_of(tr * 8, 8), 8), ct * 128:(ct + 1) * 128] = wt[
                    pl.ds(pl.multiple_of(tr * 64 + ct * 8, 8), 8), :]
        for ct in range(8):
            v0 = tt[pl.ds(pl.multiple_of(i * 128 + ct * 8, 8), 8), :]
            v1 = tt[pl.ds(pl.multiple_of(i * 128 + 64 + ct * 8, 8), 8), :]
            th_ref[pl.ds(pl.multiple_of(i * 16, 16), 16), ct * 128:(ct + 1) * 128] = (
                jnp.concatenate([v0, v1], axis=0).astype(BF16))
        return c
    lax.fori_loop(0, 64, put, 0)


def scatter_fluxes(addr, ids, wc, tc, od, w2, a2):
    return pl.pallas_call(
        scatter_kernel,
        out_shape=(jax.ShapeDtypeStruct((1024, 1024), F32), jax.ShapeDtypeStruct((1024, 1024), BF16),
                   jax.ShapeDtypeStruct((OWNERS, SLOT), F32)),
        in_specs=[SM, VM, VM, VM, VM, VM, VM], out_specs=(VM, VM, VM),
        scratch_shapes=[pltpu.VMEM((8192, 128), F32), pltpu.VMEM((8192, 128), F32),
                        pltpu.VMEM((4096, 128), F32), pltpu.VMEM((4096, 128), F32)],
        compiler_params=params(48), name="facet_scatter",
    )(addr, ids, wc, tc, od, w2, a2)


BLK = 2 * ROWS + 2 * LEV


def z_basis():
    k, m = np.arange(LEV)[:, None], np.arange(LEV)[None, :]
    q = math.sqrt(4 / 17) * np.sin(np.pi * (2 * m + 1) * (k + 1) / 17)
    theta = -4.0 * np.sin(np.pi * (2 * np.arange(LEV) + 1) / 34) ** 2
    return q, theta


def y_basis():
    i = np.arange(ROWS) + 1
    s = math.sqrt(2 / 129) * np.sin(np.pi * (np.outer(i, i) % 258) / 129)
    mu = -4.0 * np.sin(np.pi * i / 258) ** 2
    return s, mu


Q, THETA = z_basis()
DQ = Q - np.concatenate([np.zeros((1, LEV)), Q[:-1]])
SINE, MU = y_basis()
EDGE = np.concatenate([TABLE[0::ROWS], TABLE[ROWS - 1::ROWS]])


def pack(transposed):
    parts = [split_np(t.T if transposed else t) for t in (T_EE, T_EO, T_OD)]
    (eh, el), (oh, ol), (dh, dl) = parts
    return np.concatenate([dh, dl, np.concatenate([np.concatenate([eh, oh], 1), np.concatenate([el, ol], 1)])])


TAB, TAB_T = pack(False), pack(True)
SINE2 = np.concatenate(split_np(SINE))
EDGE_F = np.concatenate(split_np(EDGE.T))
EDGE_B = np.concatenate(split_np(EDGE))
LAM_X = np.broadcast_to(EIGEN.astype(np.float32), (8, N)).copy()
COLS = np.stack([np.broadcast_to(v[:, None], (ROWS, 128)) for v in (MU, SINE[:, 0], SINE[:, 127])]).astype(np.float32)


def tab_parts(t):
    return ((t[1024:1280, :256], t[1280:1536, :256]), (t[1024:1280, 256:], t[1280:1536, 256:]),
            (t[:512], t[512:1024]))


def combine(coefs, vs):
    out = None
    for c, v in zip(coefs, vs):
        t = float(c) * v
        out = t if out is None else out + t
    return out


def tile(i, size=8):
    return pl.ds(pl.multiple_of(i * size, size), size)


def block_forward_kernel(h_ref, w_ref, wn_ref, halo_ref, tab, sine, lx, cols, out_ref, g_ref, r2, a0, a7):
    step = pl.program_id(0)
    up = jnp.where(step == 3, halo_ref[0], wn_ref[0])
    r0 = h_ref[0] + w_ref[1] - w_ref[0]
    r1 = h_ref[1] + up - w_ref[1]
    r = jnp.concatenate([r0, r1], axis=0)
    s, d = r[:, :512] + r[:, 512:], r[:, :512] - r[:, 512:]
    ee, eo = s[:, :256] + s[:, 256:], s[:, :256] - s[:, 256:]
    te, to, td = tab_parts(tab)
    sh, sl = sine[:128, :], sine[128:, :]
    for v, t, c0 in ((ee, te, 0), (eo, to, 256), (d, td, 512)):
        res = dot3(*split(v), t[0], t[1])
        for l in range(2):
            r2[2 * step + l, :, c0:c0 + res.shape[1]] = dot3(sh, sl, *split(res[l * 128:(l + 1) * 128]))

    @pl.when(step == 3)
    def _():
        def lanes(lt, c):
            ln = tile(lt, 128)
            lam = lx[:, ln]

            def inner(bt, acc):
                rows = tile(bt)
                rs = [r2[k, rows, ln] for k in range(LEV)]
                mu, s0, s1 = cols[0, rows, :], cols[1, rows, :], cols[2, rows, :]
                base = lam + mu
                ps = []
                for m in range(LEV):
                    p = combine(Q[:, m], rs) / (base + float(THETA[m]))
                    g_ref[m, rows, ln] = p
                    ps.append(p)
                a0[rows, ln] = combine(Q[0], ps)
                a7[rows, ln] = combine(Q[7], ps)
                return tuple(acc[m] + s0 * ps[m] for m in range(LEV)) + tuple(
                    acc[LEV + m] + s1 * ps[m] for m in range(LEV))
            acc = lax.fori_loop(0, ROWS // 8, inner, tuple(jnp.zeros((8, 128), F32) for _ in range(16)))
            for e in range(2):
                sums = [jnp.sum(acc[e * LEV + m], axis=0, keepdims=True) for m in range(LEV)]
                out_ref[lt, 2 * ROWS + e * LEV:2 * ROWS + (e + 1) * LEV, :] = jnp.concatenate(
                    [combine(Q[k], sums) for k in range(LEV)], axis=0)
            return c
        lax.fori_loop(0, NPX, lanes, 0)
        for f, a in ((0, a0), (1, a7)):
            res = dot3(sh, sl, *split(a[...]))
            for b in range(NPX):
                out_ref[b, f * ROWS:(f + 1) * ROWS, :] = res[:, b * 128:(b + 1) * 128]


def fixed(shape):
    return pl.BlockSpec(shape, lambda g: (0,) * len(shape))


def block_forward(h, w, halo):
    return pl.pallas_call(
        block_forward_kernel, grid=(4,),
        out_shape=(jax.ShapeDtypeStruct((NPX, BLK, 128), F32), jax.ShapeDtypeStruct((LEV, ROWS, N), F32)),
        in_specs=[pl.BlockSpec((2, 128, 1024), lambda g: (g, 0, 0)),
                  pl.BlockSpec((2, 128, 1024), lambda g: (g, 0, 0)),
                  pl.BlockSpec((1, 128, 1024), lambda g: (jnp.minimum(2 * g + 2, 7), 0, 0)),
                  fixed((1, 128, 1024)), fixed((1536, 512)), fixed((256, 128)), fixed((8, N)), fixed((3, ROWS, 128))],
        out_specs=(fixed((NPX, BLK, 128)), fixed((LEV, ROWS, N))),
        scratch_shapes=[pltpu.VMEM((LEV, ROWS, N), F32), pltpu.VMEM((ROWS, N), F32), pltpu.VMEM((ROWS, N), F32)],
        compiler_params=params(48), name="block_forward",
    )(h, w, w, halo, jnp.asarray(TAB), jnp.asarray(SINE2), jnp.asarray(LAM_X), jnp.asarray(COLS))


def slab_polys(lam):
    phi = [None] * 9
    phi[8] = jnp.ones_like(lam)
    delta = -lam
    phi[7] = phi[8] + delta
    for k in range(6, -1, -1):
        delta = delta - lam * phi[k + 1]
        phi[k] = phi[k + 1] + delta
    theta = [jnp.ones_like(lam), 2.0 - lam]
    for k in range(2, 8):
        theta.append((2.0 - lam) * theta[k - 1] - theta[k - 2])
    return phi, theta, delta


def y_forward_kernel(x_ref, lam_ref, tab, edge, s_ref, al_ref, pp, sr):
    x = jnp.concatenate([x_ref[:, :ROWS], x_ref[:, ROWS:2 * ROWS]], axis=-1).reshape(N, 256)
    s, d = x[:512] + x[512:], x[:512] - x[512:]
    ee, eo = s[:256] + s[256:], s[:256] - s[256:]
    te, to, td = tab_parts(tab)
    for v, t, k0 in ((ee, te, 0), (eo, to, 256), (d, td, 512)):
        res = dot3(t[0], t[1], *split(v))
        pp[k0:k0 + res.shape[0], :] = res
    for i in range(NPX):
        for k in range(LEV):
            sr[i:i + 1, k * 128:(k + 1) * 128] = x_ref[(i + 7) % 8, 2 * ROWS + LEV + k:2 * ROWS + LEV + k + 1, :]
            sr[8 + i:9 + i, k * 128:(k + 1) * 128] = x_ref[(i + 1) % 8, 2 * ROWS + k:2 * ROWS + k + 1, :]
    sh, sl = split(sr[...])

    def spread(i, c):
        lo = tile(i, 256)
        s_ref[lo, :] = dot3(edge[lo, :], edge[pl.ds(pl.multiple_of(N + i * 256, 256), 256), :], sh, sl)
        return c
    lax.fori_loop(0, 4, spread, 0)

    def one(t, c):
        rows = tile(t, 16)
        phi, theta, _ = slab_polys(lam_ref[rows, :])
        inv = 1.0 / phi[0]
        b0 = b7 = None
        for k in range(LEV):
            sk = s_ref[rows, k * 128:(k + 1) * 128]
            b0 = phi[k + 1] * sk if k == 0 else b0 + phi[k + 1] * sk
            b7 = sk if k == 0 else b7 + theta[k] * sk
        inner = tile(t % 4, 16)
        al_ref[t // 4, 0, inner, :] = pp[rows, :128] + b0 * inv
        al_ref[t // 4, 1, inner, :] = pp[rows, 128:] + b7 * inv
        return c
    lax.fori_loop(0, 64, one, 0)


def y_forward(x, lam):
    return pl.pallas_call(
        y_forward_kernel,
        out_shape=(jax.ShapeDtypeStruct((N, N), F32), jax.ShapeDtypeStruct((NPY, 2, 64, 128), F32)),
        in_specs=[VM] * 4, out_specs=(VM, VM),
        scratch_shapes=[pltpu.VMEM((N, 256), F32), pltpu.VMEM((16, N), F32)],
        compiler_params=params(40), name="y_forward",
    )(x, lam, jnp.asarray(TAB_T), jnp.asarray(EDGE_F))


def ladder_kernel(al_ref, lam_ref, out_ref):
    for t in range(8):
        rows = slice(t * 8, (t + 1) * 8)
        phi, theta, delta = slab_polys(lam_ref[rows, :])
        inv = 1.0 / phi[0]
        n07, n77, c = inv, theta[7] * inv, delta * inv
        A = [None] * 17
        B = [None] * 17
        e = [None] * 17
        A[16] = jnp.zeros_like(inv)
        B[16] = jnp.full_like(inv, -2.0)
        for j in range(15, -1, -1):
            g, q = al_ref[j, 0, rows, :], al_ref[j, 1, rows, :]
            e[j + 1] = 1.0 / (1.0 - n77 * B[j + 1])
            be = B[j + 1] * e[j + 1]
            A[j] = g + n07 * (A[j + 1] + be * (q + n77 * A[j + 1]))
            B[j] = n07 * n07 * be - c
        p = -A[0] / B[0]
        for j in range(16):
            out_ref[j, 0, rows, :] = p
            p = (al_ref[j, 1, rows, :] + n77 * A[j + 1] + n07 * p) * e[j + 1]
            out_ref[j, 1, rows, :] = A[j + 1] + B[j + 1] * p


def ladder(al, lam):
    return pl.pallas_call(
        ladder_kernel, out_shape=jax.ShapeDtypeStruct((NPY, 2, 64, 128), F32),
        in_specs=[VM, VM], out_specs=VM, compiler_params=params(16), name="ladder",
    )(al, lam)


def y_inverse_kernel(s_ref, pu_ref, lam_ref, x_ref, tab, edge, out_ref, ph, pl_):
    def one(t, c):
        rows = tile(t, 16)
        inner = tile(t % 4, 16)
        low, top = pu_ref[t // 4, 0, inner, :], pu_ref[t // 4, 1, inner, :]
        lam = lam_ref[rows, :]
        cs = [None] * 8
        fs = [None] * 8
        cs[7] = 1.0 / (1.0 - lam)
        fs[7] = s_ref[rows, 7 * 128:] + top
        for k in range(6, -1, -1):
            cs[k] = 1.0 / (2.0 - lam - cs[k + 1])
            fs[k] = s_ref[rows, k * 128:(k + 1) * 128] + cs[k + 1] * fs[k + 1]
        prev = low
        for k in range(8):
            prev = cs[k] * (fs[k] + prev)
            ph[rows, k * 128:(k + 1) * 128], pl_[rows, k * 128:(k + 1) * 128] = split(prev)
        return c
    lax.fori_loop(0, 64, one, 0)
    edges = dot3(edge[:16, :], edge[16:, :], ph[...], pl_[...])
    for i in range(NPX):
        below, above = (i + 7) % 8, (i + 1) % 8
        for k in range(LEV):
            cols = slice(k * 128, (k + 1) * 128)
            lo = 2 * ROWS + k
            hi = 2 * ROWS + LEV + k
            out_ref[i, lo:lo + 1, :] = edges[8 + below:9 + below, cols] + x_ref[below, hi:hi + 1, :]
            out_ref[i, hi:hi + 1, :] = edges[above:above + 1, cols] + x_ref[above, lo:lo + 1, :]
    pu = jnp.concatenate([pu_ref[:, 0], pu_ref[:, 1]], axis=-1).reshape(N, 256)
    te, to, td = tab_parts(tab)
    t0 = dot3(te[0], te[1], *split(pu[:256]))
    t1 = dot3(to[0], to[1], *split(pu[256:512]))
    d = dot3(td[0], td[1], *split(pu[512:]))
    ev = (t0 + t1, t0 - t1)
    for i in range(4):
        base = ev[i // 2][(i % 2) * 128:(i % 2 + 1) * 128]
        odd = d[i * 128:(i + 1) * 128]
        for l in range(2):
            cols = slice(l * 128, (l + 1) * 128)
            out_ref[i, l * ROWS:(l + 1) * ROWS, :] = base[:, cols] + odd[:, cols]
            out_ref[i + 4, l * ROWS:(l + 1) * ROWS, :] = base[:, cols] - odd[:, cols]


def y_inverse(s, pu, lam, x):
    return pl.pallas_call(
        y_inverse_kernel, out_shape=jax.ShapeDtypeStruct((NPX, BLK, 128), F32),
        in_specs=[VM] * 6, out_specs=VM,
        scratch_shapes=[pltpu.VMEM((N, N), BF16), pltpu.VMEM((N, N), BF16)],
        compiler_params=params(40), name="y_inverse",
    )(s, pu, lam, x, jnp.asarray(TAB), jnp.asarray(EDGE_B))


def block_inverse_kernel(base_ref, y_ref, g_ref, w_ref, roof_ref, tab, sine, lx, cols, out_ref, slope, sp, su):
    step = pl.program_id(0)
    sh, sl = sine[:128, :], sine[128:, :]

    @pl.when(step == 0)
    def _():
        for f, dst in ((0, sp), (1, su)):
            v = jnp.concatenate([y_ref[b, f * ROWS:(f + 1) * ROWS] for b in range(NPX)], axis=1)
            dst[...] = dot3(sh, sl, *split(v))

        def lanes(lt, c):
            ln = tile(lt, 128)
            lam = lx[:, ln]
            ql, qh = [], []
            for e, dst in ((0, ql), (1, qh)):
                rows = [y_ref[lt, 2 * ROWS + e * LEV + k:2 * ROWS + e * LEV + k + 1, :] for k in range(LEV)]
                for m in range(LEV):
                    dst.append(jnp.broadcast_to(combine(Q[:, m], rows), (8, 128)))

            def inner(bt, cc):
                rows = tile(bt)
                mu, s0, s1 = cols[0, rows, :], cols[1, rows, :], cols[2, rows, :]
                base = lam + mu
                low, top = sp[rows, ln], su[rows, ln]
                ps = []
                for m in range(LEV):
                    f = (float(Q[0, m]) * low + float(Q[7, m]) * top) + (s0 * ql[m] + s1 * qh[m])
                    ps.append(g_ref[m, rows, ln] - f / (base + float(THETA[m])))
                for k in range(LEV):
                    v = combine(DQ[k], ps)
                    slope[k, rows, ln] = v - low if k == 0 else v
                return cc
            lax.fori_loop(0, ROWS // 8, inner, 0)
            return c
        lax.fori_loop(0, NPX, lanes, 0)

    v = jnp.concatenate([dot3(sh, sl, *split(slope[2 * step + l])) for l in range(2)], axis=0)
    te, to, td = tab_parts(tab)
    t0 = dot3(*split(v[:, :256]), te[0], te[1])
    t1 = dot3(*split(v[:, 256:512]), to[0], to[1])
    d = dot3(*split(v[:, 512:]), td[0], td[1])
    s = jnp.concatenate([t0 + t1, t0 - t1], axis=1)
    for half, res in ((0, s + d), (1, s - d)):
        cs = slice(half * 512, (half + 1) * 512)
        for l in range(2):
            level = base_ref[0] + 2 * step + l
            solid = level < roof_ref[:, cs]
            out_ref[l, :, cs] = jnp.where(solid, 0.0, w_ref[l, :, cs] - res[l * 128:(l + 1) * 128])


def block_inverse(base, y, g, w, roof):
    return pl.pallas_call(
        block_inverse_kernel, grid=(4,),
        out_shape=jax.ShapeDtypeStruct((LEV, ROWS, N), F32),
        in_specs=[SM, fixed((NPX, BLK, 128)), fixed((LEV, ROWS, N)),
                  pl.BlockSpec((2, ROWS, N), lambda g: (g, 0, 0)), fixed((ROWS, N)),
                  fixed((1536, 512)), fixed((256, 128)), fixed((8, N)), fixed((3, ROWS, 128))],
        out_specs=pl.BlockSpec((2, ROWS, N), lambda g: (g, 0, 0)),
        scratch_shapes=[pltpu.VMEM((LEV, ROWS, N), F32), pltpu.VMEM((ROWS, N), F32), pltpu.VMEM((ROWS, N), F32)],
        compiler_params=params(48), name="block_inverse",
    )(base, y, g, w, roof, jnp.asarray(TAB_T), jnp.asarray(SINE2), jnp.asarray(LAM_X), jnp.asarray(COLS))


def swap(x, axes):
    return lax.all_to_all(x, axes, split_axis=0, concat_axis=0, tiled=True)


def body(horiz_div, w_star, air_temp, roof_level, facet_cells, facet_temp, net_radiation,
         heat_capacity, drag_coef, heat_coef):
    ix, iy = lax.axis_index("px"), lax.axis_index("py")
    owner = jnp.concatenate(
        [v.reshape(OWNERS, 1, SLOT) for v in (facet_temp, drag_coef, heat_coef, jnp.zeros_like(heat_coef))],
        axis=2)
    arrived = swap(owner, ("px", "py")).reshape(OWNERS, 128)
    cells = facet_cells[0]
    safe = jnp.maximum(cells, 0)
    row = safe >> 10
    addr = (row >> 3) * 64 + ((safe >> 7) & 7) * 8 + (row & 7)
    ids = facet_cells.reshape(OWNERS, SLOT)
    w2, a2 = w_star.reshape(1024, 1024), air_temp.reshape(1024, 1024)
    wc, tc = gather_cells(addr, ids, w2, a2)
    w_corr, theta, flux = scatter_fluxes(addr, ids, wc, tc, arrived, w2, a2)
    flux_back = swap(flux.reshape(OWNERS, 1, SLOT), ("px", "py")).reshape(1, OWNERS * SLOT)
    temp_new = facet_temp + (net_radiation - flux_back - 0.5 * facet_temp) / heat_capacity
    w_corr = w_corr.reshape(LEV, ROWS, N)
    halo = lax.ppermute(w_corr[:1], "py", [(j, j - 1) for j in range(1, NPY)])

    eig = jnp.asarray(EIGEN.astype(np.float32))
    eig_x = lax.dynamic_slice_in_dim(eig, ix * 128, 128)
    eig_y = lax.dynamic_slice_in_dim(eig, iy * 64, 64)
    lam = eig[:, None] + eig_x[None, :]
    lam_mine = eig_y[:, None] + eig_x[None, :]

    sent, g = block_forward(horiz_div, w_corr, halo)
    xs = swap(sent, "px")
    s, al = y_forward(xs, lam)
    pu = swap(ladder(swap(al, "py"), lam_mine), "py")
    ys = swap(y_inverse(s, pu, lam, xs), "px")
    base = (iy * LEV).astype(jnp.int32).reshape(1)
    w_new = block_inverse(base, ys, g, w_corr, roof_level)
    return w_new, theta.reshape(LEV, ROWS, N), temp_new


def solution(mesh):
    field, facet = P("py", "px", None), P(("px", "py"), None)
    return jax.shard_map(
        body, mesh=mesh,
        in_specs=(field, field, field, P("px", None)) + (facet,) * 6,
        out_specs=(field, field, facet), check_vma=False)
```

```python
import functools
import math

import jax
import jax.numpy as jnp
import numpy as np
from jax import lax
from jax.experimental import pallas as pl
from jax.experimental.pallas import tpu as pltpu
from jax.sharding import PartitionSpec as P

N = 1024
NPX, NPY = 8, 16
LEV, ROWS = 8, 128
OWNERS, SLOT = 128, 32
MIB = 1 << 20
F32, BF16 = jnp.float32, jnp.bfloat16


def mode_table():
    classes = [np.arange(0, 513, 4), np.arange(2, 513, 4), np.arange(1, 512, 2)]
    n = np.arange(N)
    cols, waves = [], []
    for ks in classes:
        for k in ks:
            edge = k == 0 or k == N // 2
            norm = math.sqrt((1.0 if edge else 2.0) / N)
            cols.append(norm * np.cos(2 * np.pi * ((n * k) % N) / N))
            waves.append(k)
        for k in ks:
            if k == 0 or k == N // 2:
                continue
            cols.append(math.sqrt(2.0 / N) * np.sin(2 * np.pi * ((n * k) % N) / N))
            waves.append(k)
    table = np.stack(cols, axis=1)
    eigen = -4.0 * np.sin(np.pi * np.array(waves) / N) ** 2
    return table, eigen


def split_np(a):
    a = a.astype(np.float32)
    hi = a.astype(jnp.bfloat16)
    lo = (a - hi.astype(np.float32)).astype(jnp.bfloat16)
    return hi, lo


TABLE, EIGEN = mode_table()
T_EE = TABLE[:256, :256]
T_EO = TABLE[:256, 256:512]
T_OD = TABLE[:512, 512:]


def split(v):
    hi = v.astype(BF16)
    return hi, (v - hi.astype(F32)).astype(BF16)


def dot3(ah, al, bh, bl):
    d = functools.partial(jnp.dot, preferred_element_type=F32)
    return d(ah, bh) + (d(al, bh) + d(ah, bl))


def params(mb, sem=None):
    return pltpu.CompilerParams(vmem_limit_bytes=mb * MIB)


VM = pl.BlockSpec(memory_space=pltpu.VMEM)
SM = pl.BlockSpec(memory_space=pltpu.SMEM)


def pack_kernel(ft, dr, he, ce, od, ids, addr):
    zero = jnp.zeros((32, 32), F32)
    none = jnp.zeros((32, 96), jnp.int32)
    for q in range(4):
        c = slice(q * 32, (q + 1) * 32)
        od[pl.ds(q, 32, stride=4), :] = jnp.concatenate([ft[:, c], dr[:, c], he[:, c], zero], axis=1)
        ids[pl.ds(q, 32, stride=4), :] = jnp.concatenate([ce[:, c], none], axis=1)
    safe = jnp.maximum(ce[...], 0)
    row = safe >> 10
    addr[...] = (row >> 3) * 64 + ((safe >> 7) & 7) * 8 + (row & 7)


def pack_owner(ft, dr, he, ce):
    full = jax.ShapeDtypeStruct((OWNERS, 128), F32)
    return pl.pallas_call(
        pack_kernel, out_shape=(full, jax.ShapeDtypeStruct((OWNERS, 128), jnp.int32),
                                jax.ShapeDtypeStruct((32, 128), jnp.int32)),
        in_specs=[VM] * 4, out_specs=(VM,) * 3, compiler_params=params(16), name="pack_owner",
    )(ft, dr, he, ce)


def load_w(w_ref, wt):
    def one(tr, c):
        for ct in range(8):
            wt[tile(tr * 8 + ct), :] = w_ref[tile(tr), ct * 128:(ct + 1) * 128]
        return c
    lax.fori_loop(0, 128, one, 0)


def load_temp(a_ref, tt):
    def one(i, c):
        for ct in range(8):
            v = a_ref[tile(i, 16), ct * 128:(ct + 1) * 128].astype(F32)
            tt[tile(i * 16 + ct), :] = v[:8]
            tt[tile(i * 16 + 8 + ct), :] = v[8:]
        return c
    lax.fori_loop(0, 64, one, 0)


def gather_rows(addr, src, buf):
    def one(o, c):
        for s in range(SLOT):
            buf[pl.ds(s * OWNERS + o, 1), :] = src[pl.ds(addr[o * SLOT + s], 1), :]
        return c
    lax.fori_loop(0, OWNERS, one, 0)


def hits(ids, s, lane):
    col = ids[:, s:s + 1]
    return lane == jnp.where(col >= 0, col & 127, -1)


def pick(ids, buf):
    lane = lax.broadcasted_iota(jnp.int32, (OWNERS, 128), 1)
    out = jnp.zeros((OWNERS, 128), F32)
    for s in range(SLOT):
        v = jnp.where(hits(ids, s, lane), buf[s * OWNERS:(s + 1) * OWNERS, :], 0.0)
        out = jnp.where(lane == s, jnp.sum(v, axis=1, keepdims=True), out)
    return out


def spread_rows(ids, vals, buf):
    lane = lax.broadcasted_iota(jnp.int32, (OWNERS, 128), 1)
    for s in range(SLOT):
        buf[s * OWNERS:(s + 1) * OWNERS, :] = jnp.where(hits(ids, s, lane), vals[:, s:s + 1], 0.0)


def clear(accs):
    def one(i, c):
        for a in accs:
            for j in range(8):
                a[tile(i * 8 + j), :] = jnp.zeros((8, 128), F32)
        return c
    lax.fori_loop(0, 128, one, 0)


def add_rows(addr, accs, buf):
    width = len(accs)

    def one(o, c):
        for s in range(0, SLOT, width):
            at = [addr[o * SLOT + s + j] for j in range(width)]
            new = [accs[j][pl.ds(at[j], 1), :] + buf[pl.ds((s + j) * OWNERS + o, 1), :] for j in range(width)]
            for j in range(width):
                accs[j][pl.ds(at[j], 1), :] = new[j]
        return c
    lax.fori_loop(0, OWNERS, one, 0)


def total(accs, rows):
    return (accs[0][rows, :] + accs[1][rows, :]) + (accs[2][rows, :] + accs[3][rows, :])


def gather_kernel(addr, ids_ref, w_ref, wc_ref, wt, buf):
    load_w(w_ref, wt)
    gather_rows(addr, wt, buf)
    wc_ref[...] = pick(ids_ref[...], buf)


def gather_w(addr, ids, w2):
    return pl.pallas_call(
        gather_kernel, out_shape=jax.ShapeDtypeStruct((OWNERS, 128), F32), in_specs=[SM, VM, VM], out_specs=VM,
        scratch_shapes=[pltpu.VMEM((8192, 128), F32), pltpu.VMEM((4096, 128), F32)],
        compiler_params=params(32), name="facet_gather",
    )(addr, ids, w2)


def scatter_w_kernel(addr, ids_ref, wc_ref, od_ref, w_ref, wo_ref, acc0, acc1, acc2, acc3, buf):
    accs = (acc0, acc1, acc2, acc3)
    load_w(w_ref, acc0)
    clear(accs[1:])
    wc = wc_ref[:, :SLOT]
    stress = od_ref[:, 32:64] * jnp.sqrt(wc * wc + 0.25) * wc
    spread_rows(ids_ref[...], -stress, buf)
    add_rows(addr, accs, buf)

    def put(tr, c):
        for ct in range(8):
            wo_ref[tile(tr), ct * 128:(ct + 1) * 128] = total(accs, tile(tr * 8 + ct))
        return c
    lax.fori_loop(0, 128, put, 0)


FOUR = [pltpu.VMEM((8192, 128), F32)] * 4 + [pltpu.VMEM((4096, 128), F32)]


def scatter_w(addr, ids, wc, od, w2):
    return pl.pallas_call(
        scatter_w_kernel, out_shape=jax.ShapeDtypeStruct((1024, 1024), F32),
        in_specs=[SM, VM, VM, VM, VM], out_specs=VM, scratch_shapes=FOUR,
        compiler_params=params(40), name="scatter_w",
    )(addr, ids, wc, od, w2)


def heat_kernel(addr, shift, after, ids_ref, wc_ref, od_ref, a_ref, th_ref, fl_ref, acc0, acc1, acc2, acc3, buf, turned):
    accs = (acc0, acc1, acc2, acc3)
    load_temp(a_ref, acc0)
    gather_rows(addr, acc0, buf)
    ids = ids_ref[...]
    tc = pick(ids, buf)[:, :SLOT]
    clear(accs[1:])
    wc = wc_ref[:, :SLOT]
    flux = od_ref[:, 64:96] * jnp.sqrt(wc * wc + 0.25) * (od_ref[:, :32] - tc)
    spread_rows(ids, flux, buf)
    wide = jnp.concatenate([flux, jnp.zeros((OWNERS, 96), F32)], axis=1)
    turned[...] = pltpu.roll(wide, shift[0], 1)
    for j in range(NPY):
        fl_ref[j] = turned[pl.ds(j, 8, stride=16), :]
    add_rows(addr, accs, buf)

    def put(i, c):
        for ct in range(8):
            v0 = total(accs, tile(i * 16 + ct))
            v1 = total(accs, tile(i * 16 + 8 + ct))
            th_ref[tile(i, 16), ct * 128:(ct + 1) * 128] = jnp.concatenate([v0, v1], axis=0).astype(BF16)
        return c
    lax.fori_loop(0, 64, put, 0)


def heat_cells(addr, shift, after, ids, wc, od, a2):
    return pl.pallas_call(
        heat_kernel,
        out_shape=(jax.ShapeDtypeStruct((1024, 1024), BF16), jax.ShapeDtypeStruct((NPY, 8, 128), F32)),
        in_specs=[SM, SM, pl.BlockSpec(memory_space=pl.ANY), VM, VM, VM, VM], out_specs=(VM, VM),
        scratch_shapes=FOUR + [pltpu.VMEM((OWNERS, 128), F32)],
        cost_estimate=pl.CostEstimate(flops=0, bytes_accessed=60 * MIB, transcendentals=0),
        compiler_params=params(40), name="heat_cells",
    )(addr, shift, after, ids, wc, od, a2)


BLK = 2 * ROWS + 2 * LEV
BACK = BLK + 8


def z_basis():
    k, m = np.arange(LEV)[:, None], np.arange(LEV)[None, :]
    q = math.sqrt(4 / 17) * np.sin(np.pi * (2 * m + 1) * (k + 1) / 17)
    theta = -4.0 * np.sin(np.pi * (2 * np.arange(LEV) + 1) / 34) ** 2
    return q, theta


def y_basis():
    i = np.arange(ROWS) + 1
    s = math.sqrt(2 / 129) * np.sin(np.pi * (np.outer(i, i) % 258) / 129)
    mu = -4.0 * np.sin(np.pi * i / 258) ** 2
    return s, mu


Q, THETA = z_basis()
DQ = Q - np.concatenate([np.zeros((1, LEV)), Q[:-1]])
SINE, MU = y_basis()
EDGE = np.concatenate([TABLE[0::ROWS], TABLE[ROWS - 1::ROWS]])


def pack(transposed):
    parts = [split_np(t.T if transposed else t) for t in (T_EE, T_EO, T_OD)]
    (eh, el), (oh, ol), (dh, dl) = parts
    return np.concatenate([dh, dl, np.concatenate([np.concatenate([eh, oh], 1), np.concatenate([el, ol], 1)])])


TAB, TAB_T = pack(False), pack(True)
SINE2 = np.concatenate(split_np(SINE))
EDGE_F = np.concatenate(split_np(EDGE.T))
EDGE_B = np.concatenate(split_np(EDGE))
LAM_X = np.broadcast_to(EIGEN.astype(np.float32), (8, N)).copy()
COLS = np.stack([np.broadcast_to(v[:, None], (ROWS, 128)) for v in (MU, SINE[:, 0], SINE[:, 127])]).astype(np.float32)


def tab_parts(t):
    return ((t[1024:1280, :256], t[1280:1536, :256]), (t[1024:1280, 256:], t[1280:1536, 256:]),
            (t[:512], t[512:1024]))


def combine(coefs, vs):
    out = None
    for c, v in zip(coefs, vs):
        t = float(c) * v
        out = t if out is None else out + t
    return out


def tile(i, size=8):
    return pl.ds(pl.multiple_of(i * size, size), size)


def fixed(shape):
    return pl.BlockSpec(shape, lambda g: (0,) * len(shape))


def slab_polys(lam):
    phi = [None] * 9
    phi[8] = jnp.ones_like(lam)
    delta = -lam
    phi[7] = phi[8] + delta
    for k in range(6, -1, -1):
        delta = delta - lam * phi[k + 1]
        phi[k] = phi[k + 1] + delta
    theta = [jnp.ones_like(lam), 2.0 - lam]
    for k in range(2, 8):
        theta.append((2.0 - lam) * theta[k - 1] - theta[k - 2])
    return phi, theta, delta


def inverse_of(v):
    r = pl.reciprocal(v, approx=True)
    r = r * (2.0 - v * r)
    return r * (2.0 - v * r)


def x_modes(v, tab):
    s, d = v[:, :512] + v[:, 512:], v[:, :512] - v[:, 512:]
    te, to, td = tab_parts(tab)
    return ((0, dot3(*split(s[:, :256] + s[:, 256:]), *te)), (256, dot3(*split(s[:, :256] - s[:, 256:]), *to)),
            (512, dot3(*split(d), *td)))


def block_modes_kernel(h_ref, w_ref, wn_ref, tab, sine, out_ref):
    up = jnp.where(pl.program_id(0) == 3, 0.0, wn_ref[0])
    r = jnp.concatenate([h_ref[0] + w_ref[1] - w_ref[0], h_ref[1] + up - w_ref[1]], axis=0)
    for c0, res in x_modes(r, tab):
        for l in range(2):
            out_ref[l, :, c0:c0 + res.shape[1]] = dot3(
                sine[:128, :], sine[128:, :], *split(res[l * 128:(l + 1) * 128]))


def block_modes(h, w):
    two = pl.BlockSpec((2, ROWS, N), lambda g: (g, 0, 0))
    return pl.pallas_call(
        block_modes_kernel, grid=(4,), out_shape=jax.ShapeDtypeStruct((LEV, ROWS, N), F32),
        in_specs=[two, two, pl.BlockSpec((1, ROWS, N), lambda g: (jnp.minimum(2 * g + 2, 7), 0, 0)),
                  fixed((1536, 512)), fixed((256, 128))],
        out_specs=two, compiler_params=params(32), name="block_modes",
        cost_estimate=pl.CostEstimate(flops=0, bytes_accessed=25 * MIB, transcendentals=0),
    )(h, w, w, jnp.asarray(TAB), jnp.asarray(SINE2))


def block_solve_kernel(r_ref, halo_ref, tab, sine, lx, cols, out_ref, g_ref, hx, a07):
    lt = pl.program_id(0)
    sh, sl = sine[:128, :], sine[128:, :]

    @pl.when(lt == 0)
    def _():
        for c0, res in x_modes(halo_ref[...], tab):
            res = dot3(sh, sl, *split(res))
            for b in range(res.shape[1] // 128):
                hx[c0 // 128 + b] = res[:, b * 128:(b + 1) * 128]
    lam = lx[...]

    def inner(bt, acc):
        rows = tile(bt)
        rs = [r_ref[k, rows, :] for k in range(LEV)]
        rs[7] = rs[7] + hx[lt, rows, :]
        mu, s0, s1 = cols[0, rows, :], cols[1, rows, :], cols[2, rows, :]
        base = lam + mu
        ps = []
        for m in range(LEV):
            p = combine(Q[:, m], rs) * inverse_of(base + float(THETA[m]))
            g_ref[m, rows, :] = p
            ps.append(p)
        a07[rows, :128] = combine(Q[0], ps)
        a07[rows, 128:] = combine(Q[7], ps)
        return tuple(acc[m] + s0 * ps[m] for m in range(LEV)) + tuple(
            acc[LEV + m] + s1 * ps[m] for m in range(LEV))
    acc = lax.fori_loop(0, ROWS // 8, inner, tuple(jnp.zeros((8, 128), F32) for _ in range(16)))
    for e in range(2):
        sums = [jnp.sum(acc[e * LEV + m], axis=0, keepdims=True) for m in range(LEV)]
        out_ref[0, 2 * ROWS + e * LEV:2 * ROWS + (e + 1) * LEV, :] = jnp.concatenate(
            [combine(Q[k], sums) for k in range(LEV)], axis=0)
    res = dot3(sh, sl, *split(a07[...]))
    out_ref[0, :ROWS, :] = res[:, :128]
    out_ref[0, ROWS:2 * ROWS, :] = res[:, 128:]


def block_solve(r, halo):
    col = pl.BlockSpec((LEV, ROWS, 128), lambda g: (0, 0, g))
    return pl.pallas_call(
        block_solve_kernel, grid=(NPX,),
        out_shape=(jax.ShapeDtypeStruct((NPX, BLK, 128), F32), jax.ShapeDtypeStruct((LEV, ROWS, N), F32)),
        in_specs=[col, fixed((ROWS, N)), fixed((1536, 512)), fixed((256, 128)),
                  pl.BlockSpec((8, 128), lambda g: (0, g)), fixed((3, ROWS, 128))],
        out_specs=(pl.BlockSpec((1, BLK, 128), lambda g: (g, 0, 0)), col),
        scratch_shapes=[pltpu.VMEM((NPX, ROWS, 128), F32), pltpu.VMEM((ROWS, 256), F32)],
        compiler_params=params(32), name="block_solve",
    )(r, halo, jnp.asarray(TAB), jnp.asarray(SINE2), jnp.asarray(LAM_X), jnp.asarray(COLS))


def edge_rows(x_ref, sr):
    for i in range(NPX):
        for k in range(LEV):
            cs = slice(k * 128, (k + 1) * 128)
            sr[i:i + 1, cs] = x_ref[(i + 7) % 8, 2 * ROWS + LEV + k:2 * ROWS + LEV + k + 1, :]
            sr[8 + i:9 + i, cs] = x_ref[(i + 1) % 8, 2 * ROWS + k:2 * ROWS + k + 1, :]
    return split(sr[...])


def edge_modes(edge, t, sh, sl):
    return dot3(edge[tile(t, 128), :], edge[pl.ds(pl.multiple_of(N + t * 128, 128), 128), :], sh, sl)


def y_forward_kernel(x_ref, lam_ref, tab, edge, al_ref, pp, sr, st):
    x = jnp.concatenate([x_ref[:, :ROWS], x_ref[:, ROWS:2 * ROWS]], axis=-1).reshape(N, 256)
    s, d = x[:512] + x[512:], x[:512] - x[512:]
    ee, eo = s[:256] + s[256:], s[:256] - s[256:]
    te, to, td = tab_parts(tab)
    for v, t, k0 in ((ee, te, 0), (eo, to, 256), (d, td, 512)):
        res = dot3(*t, *split(v))
        pp[k0:k0 + res.shape[0], :] = res
    sh, sl = edge_rows(x_ref, sr)

    def some(t, c):
        st[...] = edge_modes(edge, t, sh, sl)
        for q in range(8):
            part = slice(q * 16, (q + 1) * 16)
            rows = pl.ds(pl.multiple_of(t * 128 + q * 16, 16), 16)
            phi, theta, _ = slab_polys(lam_ref[rows, :])
            inv = inverse_of(phi[0])
            b0 = b7 = None
            for k in range(LEV):
                sk = st[part, k * 128:(k + 1) * 128]
                b0 = phi[k + 1] * sk if k == 0 else b0 + phi[k + 1] * sk
                b7 = sk if k == 0 else b7 + theta[k] * sk
            j, at = 2 * t + q // 4, (q % 4) * 16
            al_ref[j, at:at + 16, :] = pp[rows, :128] + b0 * inv
            al_ref[j, 64 + at:80 + at, :] = pp[rows, 128:] + b7 * inv
        return c
    lax.fori_loop(0, 8, some, 0)


def y_forward(x, lam):
    return pl.pallas_call(
        y_forward_kernel, grid=(1,),
        out_shape=jax.ShapeDtypeStruct((NPY, 128, 128), F32),
        in_specs=[fixed((NPX, BLK, 128)), fixed((N, 128)), fixed((1536, 512)), fixed((2 * N, 16))],
        out_specs=fixed((NPY, 128, 128)),
        scratch_shapes=[pltpu.VMEM((N, 256), F32), pltpu.VMEM((16, N), F32), pltpu.VMEM((128, N), F32)],
        compiler_params=params(40), name="y_forward",
    )(x, lam, jnp.asarray(TAB_T), jnp.asarray(EDGE_F))


def ladder_kernel(al_ref, lam_ref, fl_ref, out_ref):
    for j in range(NPY):
        out_ref[j, 128:, :] = fl_ref[j]

    def some(t, c):
        rows, tops = tile(t), pl.ds(pl.multiple_of(64 + t * 8, 8), 8)
        phi, theta, delta = slab_polys(lam_ref[rows, :])
        inv = 1.0 / phi[0]
        n07, n77, cc = inv, theta[7] * inv, delta * inv
        A = [None] * 17
        B = [None] * 17
        e = [None] * 17
        A[16] = jnp.zeros_like(inv)
        B[16] = jnp.full_like(inv, -2.0)
        for j in range(15, -1, -1):
            g, q = al_ref[j, rows, :], al_ref[j, tops, :]
            e[j + 1] = inverse_of(1.0 - n77 * B[j + 1])
            be = B[j + 1] * e[j + 1]
            A[j] = g + n07 * (A[j + 1] + be * (q + n77 * A[j + 1]))
            B[j] = n07 * n07 * be - cc
        p = -A[0] / B[0]
        for j in range(16):
            out_ref[j, rows, :] = p
            p = (al_ref[j, tops, :] + n77 * A[j + 1] + n07 * p) * e[j + 1]
            out_ref[j, tops, :] = A[j + 1] + B[j + 1] * p
        return c
    lax.fori_loop(0, 8, some, 0)


def ladder(al, lam, fl):
    return pl.pallas_call(
        ladder_kernel, grid=(1,), out_shape=jax.ShapeDtypeStruct((NPY, 136, 128), F32),
        in_specs=[fixed((NPY, 128, 128)), fixed((64, 128)), fixed((NPY, 8, 128))],
        out_specs=fixed((NPY, 136, 128)), compiler_params=params(16), name="ladder",
    )(al, lam, fl)


def y_inverse_kernel(x_ref, pu_ref, lam_ref, tab, edge_f, edge_b, out_ref, sr, st, ph, pl_):
    sh, sl = edge_rows(x_ref, sr)

    def some(t, c):
        st[...] = edge_modes(edge_f, t, sh, sl)
        for q in range(8):
            part = slice(q * 16, (q + 1) * 16)
            rows = pl.ds(pl.multiple_of(t * 128 + q * 16, 16), 16)
            j, at = 2 * t + q // 4, (q % 4) * 16
            low, top = pu_ref[j, at:at + 16, :], pu_ref[j, 64 + at:80 + at, :]
            lam = lam_ref[rows, :]
            cs = [None] * 8
            fs = [None] * 8
            cs[7] = inverse_of(1.0 - lam)
            fs[7] = st[part, 7 * 128:] + top
            for k in range(6, -1, -1):
                cs[k] = inverse_of(2.0 - lam - cs[k + 1])
                fs[k] = st[part, k * 128:(k + 1) * 128] + cs[k + 1] * fs[k + 1]
            prev = low
            for k in range(8):
                prev = cs[k] * (fs[k] + prev)
                ph[rows, k * 128:(k + 1) * 128], pl_[rows, k * 128:(k + 1) * 128] = split(prev)
        return c
    lax.fori_loop(0, 8, some, 0)
    edges = dot3(edge_b[:16, :], edge_b[16:, :], ph[...], pl_[...])
    for i in range(NPX):
        below, above = (i + 7) % 8, (i + 1) % 8
        for k in range(LEV):
            cols = slice(k * 128, (k + 1) * 128)
            lo = 2 * ROWS + k
            hi = 2 * ROWS + LEV + k
            out_ref[i, lo:lo + 1, :] = edges[8 + below:9 + below, cols] + x_ref[below, hi:hi + 1, :]
            out_ref[i, hi:hi + 1, :] = edges[above:above + 1, cols] + x_ref[above, lo:lo + 1, :]
    for q in range(4):
        flux = (pu_ref[4 * q, 128:, :] + pu_ref[4 * q + 1, 128:, :]) + (
            pu_ref[4 * q + 2, 128:, :] + pu_ref[4 * q + 3, 128:, :])
        for i in range(NPX):
            out_ref[i, BLK + q:BLK + q + 1, :] = flux[i:i + 1, :]
            out_ref[i, BLK + 4 + q:BLK + 5 + q, :] = jnp.zeros((1, 128), F32)
    pu = jnp.concatenate([pu_ref[:, :64], pu_ref[:, 64:128]], axis=-1).reshape(N, 256)
    te, to, td = tab_parts(tab)
    t0 = dot3(*te, *split(pu[:256]))
    t1 = dot3(*to, *split(pu[256:512]))
    d = dot3(*td, *split(pu[512:]))
    ev = (t0 + t1, t0 - t1)
    for i in range(4):
        base = ev[i // 2][(i % 2) * 128:(i % 2 + 1) * 128]
        odd = d[i * 128:(i + 1) * 128]
        for l in range(2):
            cols = slice(l * 128, (l + 1) * 128)
            out_ref[i, l * ROWS:(l + 1) * ROWS, :] = base[:, cols] + odd[:, cols]
            out_ref[i + 4, l * ROWS:(l + 1) * ROWS, :] = base[:, cols] - odd[:, cols]


def y_inverse(x, pu, lam):
    return pl.pallas_call(
        y_inverse_kernel, grid=(1,), out_shape=jax.ShapeDtypeStruct((NPX, BACK, 128), F32),
        in_specs=[fixed((NPX, BLK, 128)), fixed((NPY, 136, 128)), fixed((N, 128)), fixed((1536, 512)),
                  fixed((2 * N, 16)), fixed((32, N))],
        out_specs=fixed((NPX, BACK, 128)),
        scratch_shapes=[pltpu.VMEM((16, N), F32), pltpu.VMEM((128, N), F32),
                        pltpu.VMEM((N, N), BF16), pltpu.VMEM((N, N), BF16)],
        compiler_params=params(40), name="y_inverse",
    )(x, pu, lam, jnp.asarray(TAB), jnp.asarray(EDGE_F), jnp.asarray(EDGE_B))


def block_inverse_kernel(base_ref, y_ref, g_ref, w_ref, roof_ref, tab, sine, lx, cols, ft, nr, hc,
                         out_ref, nt_ref, field, wv, spu, fb):
    step = pl.program_id(0)
    sh, sl = sine[:128, :], sine[128:, :]

    @pl.when(step < NPX)
    def _():
        fb[step] = y_ref[0, BLK:, :]
        spu[...] = dot3(sh, sl, *split(jnp.concatenate([y_ref[0, :ROWS, :], y_ref[0, ROWS:2 * ROWS, :]], axis=1)))
        lam = lx[...]
        ql, qh = [], []
        for e, dst in ((0, ql), (1, qh)):
            rows = [y_ref[0, 2 * ROWS + e * LEV + k:2 * ROWS + e * LEV + k + 1, :] for k in range(LEV)]
            for m in range(LEV):
                dst.append(jnp.broadcast_to(combine(Q[:, m], rows), (8, 128)))

        def inner(bt, c):
            rows = tile(bt)
            mu, s0, s1 = cols[0, rows, :], cols[1, rows, :], cols[2, rows, :]
            base = lam + mu
            low, top = spu[rows, :128], spu[rows, 128:]
            ps = []
            for m in range(LEV):
                f = (float(Q[0, m]) * low + float(Q[7, m]) * top) + (s0 * ql[m] + s1 * qh[m])
                ps.append(g_ref[m, rows, :] - f * inverse_of(base + float(THETA[m])))
            for k in range(LEV):
                v = combine(DQ[k], ps)
                wv[rows, k * 128:(k + 1) * 128] = v - low if k == 0 else v
            return c
        lax.fori_loop(0, ROWS // 8, inner, 0)
        res = dot3(sh, sl, *split(wv[...]))
        for k in range(LEV):
            field[k, :, tile(step, 128)] = res[:, k * 128:(k + 1) * 128]

    @pl.when(step >= NPX)
    def _():
        pair = step - NPX
        v = jnp.concatenate([field[2 * pair], field[2 * pair + 1]], axis=0)
        te, to, td = tab_parts(tab)
        t0 = dot3(*split(v[:, :256]), *te)
        t1 = dot3(*split(v[:, 256:512]), *to)
        d = dot3(*split(v[:, 512:]), *td)
        s = jnp.concatenate([t0 + t1, t0 - t1], axis=1)
        for half, res in ((0, s + d), (1, s - d)):
            cs = slice(half * 512, (half + 1) * 512)
            for l in range(2):
                solid = base_ref[0] + 2 * pair + l < roof_ref[:, cs]
                out_ref[l, :, cs] = jnp.where(solid, 0.0, w_ref[l, :, cs] - res[l * 128:(l + 1) * 128])

    @pl.when(step == NPX + 3)
    def _():
        flux = jnp.concatenate([fb[i, :4, :] for i in range(NPX)], axis=0)
        nt_ref[...] = ft[...] + (nr[...] - flux - 0.5 * ft[...]) / hc[...]


def block_inverse(base, y, g, w, roof, ft, nr, hc):
    late = pl.BlockSpec((2, ROWS, N), lambda t: (jnp.maximum(t - NPX, 0), 0, 0))
    return pl.pallas_call(
        block_inverse_kernel, grid=(NPX + 4,),
        out_shape=(jax.ShapeDtypeStruct((LEV, ROWS, N), F32), jax.ShapeDtypeStruct((32, 128), F32)),
        in_specs=[SM, pl.BlockSpec((1, BACK, 128), lambda t: (jnp.minimum(t, NPX - 1), 0, 0)),
                  pl.BlockSpec((LEV, ROWS, 128), lambda t: (0, 0, jnp.minimum(t, NPX - 1))),
                  late, fixed((ROWS, N)), fixed((1536, 512)), fixed((256, 128)),
                  pl.BlockSpec((8, 128), lambda t: (0, jnp.minimum(t, NPX - 1))), fixed((3, ROWS, 128)),
                  fixed((32, 128)), fixed((32, 128)), fixed((32, 128))],
        out_specs=(late, fixed((32, 128))),
        scratch_shapes=[pltpu.VMEM((LEV, ROWS, N), F32), pltpu.VMEM((ROWS, N), F32), pltpu.VMEM((ROWS, 256), F32),
                        pltpu.VMEM((NPX, 8, 128), F32)],
        compiler_params=params(40), name="block_inverse",
    )(base, y, g, w, roof, jnp.asarray(TAB_T), jnp.asarray(SINE2), jnp.asarray(LAM_X), jnp.asarray(COLS), ft, nr, hc)


def swap(x, axes):
    return lax.all_to_all(x, axes, split_axis=0, concat_axis=0, tiled=True)


def body(horiz_div, w_star, air_temp, roof_level, facet_cells, facet_temp, net_radiation,
         heat_capacity, drag_coef, heat_coef):
    ix, iy = lax.axis_index("px"), lax.axis_index("py")
    ft, nr, hc, dr, he, ce = [
        v.reshape(32, 128) for v in (facet_temp, net_radiation, heat_capacity, drag_coef, heat_coef, facet_cells)]
    owner, ids, addr = pack_owner(ft, dr, he, ce)
    od = swap(owner.reshape(OWNERS, 1, 128), ("px", "py")).reshape(OWNERS, 128)
    addr = addr.reshape(OWNERS * SLOT)
    w2, a2 = w_star.reshape(1024, 1024), air_temp.reshape(1024, 1024)
    wc = gather_w(addr, ids, w2)
    w_corr = scatter_w(addr, ids, wc, od, w2)
    halo = lax.ppermute(w_corr[:ROWS], "py", [(j, j - 1) for j in range(1, NPY)])
    w_corr = w_corr.reshape(LEV, ROWS, N)

    eig = jnp.asarray(EIGEN.astype(np.float32))
    eig_x = lax.dynamic_slice_in_dim(eig, ix * 128, 128)
    eig_y = lax.dynamic_slice_in_dim(eig, iy * 64, 64)
    lam = eig[:, None] + eig_x[None, :]
    lam_mine = eig_y[:, None] + eig_x[None, :]

    sent, g = block_solve(block_modes(horiz_div, w_corr), halo)
    xs = swap(sent, "px")
    shift = ((iy % 4) * SLOT).astype(jnp.int32).reshape(1)
    theta, fl = heat_cells(addr, shift, sent, ids, wc, od, a2)
    al = y_forward(xs, lam)
    pu = swap(ladder(swap(al, "py"), lam_mine, fl), "py")
    ys = swap(y_inverse(xs, pu, lam), "px")
    base = (iy * LEV).astype(jnp.int32).reshape(1)
    w_new, temp_new = block_inverse(base, ys, g, w_corr, roof_level, ft, nr, hc)
    return w_new, theta.reshape(LEV, ROWS, N), temp_new.reshape(1, OWNERS * SLOT)


def solution(mesh):
    field, facet = P("py", "px", None), P(("px", "py"), None)
    return jax.shard_map(
        body, mesh=mesh,
        in_specs=(field, field, field, P("px", None)) + (facet,) * 6,
        out_specs=(field, field, facet), check_vma=False)
```

```python
import functools
import math

import jax
import jax.numpy as jnp
import numpy as np
from jax import lax
from jax.experimental import pallas as pl
from jax.experimental.pallas import tpu as pltpu
from jax.sharding import PartitionSpec as P

N = 1024
NPX, NPY = 8, 16
LEV, ROWS = 8, 128
OWNERS, SLOT = 128, 32
MIB = 1 << 20
VMEM_MIB = 58
F32, BF16 = jnp.float32, jnp.bfloat16


def mode_table():
    classes = [np.arange(0, 513, 4), np.arange(2, 513, 4), np.arange(1, 512, 2)]
    n = np.arange(N)
    cols, waves = [], []
    for ks in classes:
        for k in ks:
            edge = k == 0 or k == N // 2
            norm = math.sqrt((1.0 if edge else 2.0) / N)
            cols.append(norm * np.cos(2 * np.pi * ((n * k) % N) / N))
            waves.append(k)
        for k in ks:
            if k == 0 or k == N // 2:
                continue
            cols.append(math.sqrt(2.0 / N) * np.sin(2 * np.pi * ((n * k) % N) / N))
            waves.append(k)
    table = np.stack(cols, axis=1)
    eigen = -4.0 * np.sin(np.pi * np.array(waves) / N) ** 2
    return table, eigen


def split_np(a):
    a = a.astype(np.float32)
    hi = a.astype(jnp.bfloat16)
    lo = (a - hi.astype(np.float32)).astype(jnp.bfloat16)
    return hi, lo


TABLE, EIGEN = mode_table()
T_EE = TABLE[:256, :256]
T_EO = TABLE[:256, 256:512]
T_OD = TABLE[:512, 512:]


def split(v):
    hi = v.astype(BF16)
    return hi, (v - hi.astype(F32)).astype(BF16)


def dot3(ah, al, bh, bl):
    d = functools.partial(jnp.dot, preferred_element_type=F32)
    return d(ah, bh) + (d(al, bh) + d(ah, bl))


def params(mb, sem=None):
    return pltpu.CompilerParams(vmem_limit_bytes=mb * MIB)


TOKEN = jax.ShapeDtypeStruct((8, 128), F32)
VM = pl.BlockSpec(memory_space=pltpu.VMEM)
SM = pl.BlockSpec(memory_space=pltpu.SMEM)


def pack_kernel(ft, dr, he, ce, od, ids, addr):
    zero = jnp.zeros((32, 32), F32)
    none = jnp.zeros((32, 96), jnp.int32)
    for q in range(4):
        c = slice(q * 32, (q + 1) * 32)
        od[pl.ds(q, 32, stride=4), :] = jnp.concatenate([ft[:, c], dr[:, c], he[:, c], zero], axis=1)
        ids[pl.ds(q, 32, stride=4), :] = jnp.concatenate([ce[:, c], none], axis=1)
    safe = jnp.maximum(ce[...], 0)
    row = safe >> 10
    addr[...] = (row >> 3) * 64 + ((safe >> 7) & 7) * 8 + (row & 7)


def pack_owner(ft, dr, he, ce):
    full = jax.ShapeDtypeStruct((OWNERS, 128), F32)
    return pl.pallas_call(
        pack_kernel, out_shape=(full, jax.ShapeDtypeStruct((OWNERS, 128), jnp.int32),
                                jax.ShapeDtypeStruct((32, 128), jnp.int32)),
        in_specs=[VM] * 4, out_specs=(VM,) * 3, compiler_params=params(VMEM_MIB), name="pack_owner",
    )(ft, dr, he, ce)


def load_w(w_ref, wt):
    def one(tr, c):
        for ct in range(8):
            wt[tile(tr * 8 + ct), :] = w_ref[tile(tr), ct * 128:(ct + 1) * 128]
        return c
    lax.fori_loop(0, 128, one, 0)


def load_temp(a_ref, tt):
    def one(i, c):
        for ct in range(8):
            v = a_ref[tile(i, 16), ct * 128:(ct + 1) * 128].astype(F32)
            tt[tile(i * 16 + ct), :] = v[:8]
            tt[tile(i * 16 + 8 + ct), :] = v[8:]
        return c
    lax.fori_loop(0, 64, one, 0)


def gather_rows(addr, src, buf):
    def one(o, c):
        for s in range(SLOT):
            buf[pl.ds(s * OWNERS + o, 1), :] = src[pl.ds(addr[o * SLOT + s], 1), :]
        return c
    lax.fori_loop(0, OWNERS, one, 0)


def hits(ids, s, lane):
    col = ids[:, s:s + 1]
    return lane == jnp.where(col >= 0, col & 127, -1)


def pick(ids, buf):
    lane = lax.broadcasted_iota(jnp.int32, (OWNERS, 128), 1)
    out = jnp.zeros((OWNERS, 128), F32)
    for s in range(SLOT):
        v = jnp.where(hits(ids, s, lane), buf[s * OWNERS:(s + 1) * OWNERS, :], 0.0)
        out = jnp.where(lane == s, jnp.sum(v, axis=1, keepdims=True), out)
    return out


def spread_rows(ids, vals, buf):
    lane = lax.broadcasted_iota(jnp.int32, (OWNERS, 128), 1)
    for s in range(SLOT):
        buf[s * OWNERS:(s + 1) * OWNERS, :] = jnp.where(hits(ids, s, lane), vals[:, s:s + 1], 0.0)


def clear(accs):
    def one(i, c):
        for a in accs:
            for j in range(8):
                a[tile(i * 8 + j), :] = jnp.zeros((8, 128), F32)
        return c
    lax.fori_loop(0, 128, one, 0)


def add_rows(addr, accs, buf):
    width = len(accs)

    def one(o, c):
        for s in range(0, SLOT, width):
            at = [addr[o * SLOT + s + j] for j in range(width)]
            new = [accs[j][pl.ds(at[j], 1), :] + buf[pl.ds((s + j) * OWNERS + o, 1), :] for j in range(width)]
            for j in range(width):
                accs[j][pl.ds(at[j], 1), :] = new[j]
        return c
    lax.fori_loop(0, OWNERS, one, 0)


def total(accs, rows):
    return (accs[0][rows, :] + accs[1][rows, :]) + (accs[2][rows, :] + accs[3][rows, :])


def gather_kernel(addr, ids_ref, w_ref, wc_ref, wt, buf):
    load_w(w_ref, wt)
    gather_rows(addr, wt, buf)
    wc_ref[...] = pick(ids_ref[...], buf)


def gather_w(addr, ids, w2):
    return pl.pallas_call(
        gather_kernel, out_shape=jax.ShapeDtypeStruct((OWNERS, 128), F32), in_specs=[SM, VM, VM], out_specs=VM,
        scratch_shapes=[pltpu.VMEM((8192, 128), F32), pltpu.VMEM((4096, 128), F32)],
        compiler_params=params(VMEM_MIB), name="facet_gather",
    )(addr, ids, w2)


def scatter_w_kernel(addr, ids_ref, wc_ref, od_ref, w_ref, wo_ref, acc0, acc1, acc2, acc3, buf):
    accs = (acc0, acc1, acc2, acc3)
    load_w(w_ref, acc0)
    clear(accs[1:])
    wc = wc_ref[:, :SLOT]
    stress = od_ref[:, 32:64] * jnp.sqrt(wc * wc + 0.25) * wc
    spread_rows(ids_ref[...], -stress, buf)
    add_rows(addr, accs, buf)

    def put(tr, c):
        for ct in range(8):
            wo_ref[tile(tr), ct * 128:(ct + 1) * 128] = total(accs, tile(tr * 8 + ct))
        return c
    lax.fori_loop(0, 128, put, 0)


FOUR = [pltpu.VMEM((8192, 128), F32)] * 4 + [pltpu.VMEM((4096, 128), F32)]


def scatter_w(addr, ids, wc, od, w2):
    return pl.pallas_call(
        scatter_w_kernel, out_shape=jax.ShapeDtypeStruct((1024, 1024), F32),
        in_specs=[SM, VM, VM, VM, VM], out_specs=VM, scratch_shapes=FOUR,
        compiler_params=params(VMEM_MIB), name="scatter_w",
    )(addr, ids, wc, od, w2)


def flux_kernel(addr, tok_in, ids_ref, wc_ref, od_ref, a_ref, flux_ref, fl_ref, tok_ref, tt, buf, turned):
    load_temp(a_ref, tt)
    gather_rows(addr, tt, buf)
    tc = pick(ids_ref[...], buf)[:, :SLOT]
    wc = wc_ref[:, :SLOT]
    flux = od_ref[:, 64:96] * jnp.sqrt(wc * wc + 0.25) * (od_ref[:, :32] - tc)
    wide = jnp.concatenate([flux, jnp.zeros((OWNERS, 96), F32)], axis=1)
    flux_ref[...] = wide
    turned[...] = pltpu.roll(wide, (lax.axis_index("py") % 4) * SLOT, 1)
    for j in range(NPY):
        fl_ref[j] = turned[pl.ds(j, 8, stride=16), :]
    tok_ref[...] = tok_in[...]


def heat_flux(addr, tok, ids, wc, od, a2):
    return pl.pallas_call(
        flux_kernel,
        out_shape=(jax.ShapeDtypeStruct((OWNERS, 128), F32), jax.ShapeDtypeStruct((NPY, 8, 128), F32), TOKEN),
        in_specs=[SM] + [VM] * 5, out_specs=(VM,) * 3,
        scratch_shapes=[pltpu.VMEM((8192, 128), F32), pltpu.VMEM((4096, 128), F32), pltpu.VMEM((OWNERS, 128), F32)],
        cost_estimate=pl.CostEstimate(flops=0, bytes_accessed=25 * MIB, transcendentals=0),
        compiler_params=params(VMEM_MIB), name="heat_flux",
    )(addr, tok, ids, wc, od, a2)


def theta_kernel(addr, tok_in, ids_ref, flux_ref, a_ref, th_ref, tok_ref, acc0, acc1, acc2, acc3, buf):
    accs = (acc0, acc1, acc2, acc3)
    load_temp(a_ref, acc0)
    clear(accs[1:])
    spread_rows(ids_ref[...], flux_ref[...], buf)
    add_rows(addr, accs, buf)

    def put(i, c):
        for ct in range(8):
            v0 = total(accs, tile(i * 16 + ct))
            v1 = total(accs, tile(i * 16 + 8 + ct))
            th_ref[tile(i, 16), ct * 128:(ct + 1) * 128] = jnp.concatenate([v0, v1], axis=0).astype(BF16)
        return c
    lax.fori_loop(0, 64, put, 0)
    tok_ref[...] = tok_in[...]


def new_theta(addr, tok, ids, flux, a2):
    return pl.pallas_call(
        theta_kernel, out_shape=(jax.ShapeDtypeStruct((1024, 1024), BF16), TOKEN),
        in_specs=[SM] + [VM] * 4, out_specs=(VM, VM), scratch_shapes=FOUR,
        cost_estimate=pl.CostEstimate(flops=0, bytes_accessed=40 * MIB, transcendentals=0),
        compiler_params=params(VMEM_MIB), name="new_theta",
    )(addr, tok, ids, flux, a2)


BLK = 2 * ROWS + 2 * LEV
BACK = BLK + 8


def z_basis():
    k, m = np.arange(LEV)[:, None], np.arange(LEV)[None, :]
    q = math.sqrt(4 / 17) * np.sin(np.pi * (2 * m + 1) * (k + 1) / 17)
    theta = -4.0 * np.sin(np.pi * (2 * np.arange(LEV) + 1) / 34) ** 2
    return q, theta


def y_basis():
    i = np.arange(ROWS) + 1
    s = math.sqrt(2 / 129) * np.sin(np.pi * (np.outer(i, i) % 258) / 129)
    mu = -4.0 * np.sin(np.pi * i / 258) ** 2
    return s, mu


Q, THETA = z_basis()
DQ = Q - np.concatenate([np.zeros((1, LEV)), Q[:-1]])
SINE, MU = y_basis()
EDGE = np.concatenate([TABLE[0::ROWS], TABLE[ROWS - 1::ROWS]])


def pack(transposed):
    parts = [split_np(t.T if transposed else t) for t in (T_EE, T_EO, T_OD)]
    (eh, el), (oh, ol), (dh, dl) = parts
    return np.concatenate([dh, dl, np.concatenate([np.concatenate([eh, oh], 1), np.concatenate([el, ol], 1)])])


TAB, TAB_T = pack(False), pack(True)
SINE2 = np.concatenate(split_np(SINE))
EDGE_F = np.concatenate(split_np(EDGE.T))
EDGE_B = np.concatenate(split_np(EDGE))
LAM_Y = np.broadcast_to(EIGEN.astype(np.float32)[:, None], (N, 128)).copy()
LAM_X = np.broadcast_to(EIGEN.astype(np.float32), (8, N)).copy()
COLS = np.stack([np.broadcast_to(v[:, None], (ROWS, 128)) for v in (MU, SINE[:, 0], SINE[:, 127])]).astype(np.float32)


def tab_parts(t):
    return ((t[1024:1280, :256], t[1280:1536, :256]), (t[1024:1280, 256:], t[1280:1536, 256:]),
            (t[:512], t[512:1024]))


def combine(coefs, vs):
    out = None
    for c, v in zip(coefs, vs):
        t = float(c) * v
        out = t if out is None else out + t
    return out


def tile(i, size=8):
    return pl.ds(pl.multiple_of(i * size, size), size)


def fixed(shape):
    return pl.BlockSpec(shape, lambda g: (0,) * len(shape))


def slab_polys(lam):
    phi = [None] * 9
    phi[8] = jnp.ones_like(lam)
    delta = -lam
    phi[7] = phi[8] + delta
    for k in range(6, -1, -1):
        delta = delta - lam * phi[k + 1]
        phi[k] = phi[k + 1] + delta
    theta = [jnp.ones_like(lam), 2.0 - lam]
    for k in range(2, 8):
        theta.append((2.0 - lam) * theta[k - 1] - theta[k - 2])
    return phi, theta, delta


def inverse_of(v):
    r = pl.reciprocal(v, approx=True)
    r = r * (2.0 - v * r)
    return r * (2.0 - v * r)


def x_modes(v, tab):
    s, d = v[:, :512] + v[:, 512:], v[:, :512] - v[:, 512:]
    te, to, td = tab_parts(tab)
    return ((0, dot3(*split(s[:, :256] + s[:, 256:]), *te)), (256, dot3(*split(s[:, :256] - s[:, 256:]), *to)),
            (512, dot3(*split(d), *td)))


def block_forward_kernel(h_ref, w_ref, wn_ref, tab, sine, lx, cols, out_ref, g_ref, tok_ref, r2, hx, a07):
    step = pl.program_id(0)
    sh, sl = sine[:128, :], sine[128:, :]

    @pl.when(step == 0)
    def _():
        tok_ref[...] = jnp.zeros((8, 128), F32)
        lifted = (lax.axis_index("py") > 0).astype(F32)
        for c0, res in x_modes(w_ref[0] * lifted, tab):
            for b in range(res.shape[1] // 128):
                hx[c0 // 128 + b] = res[:, b * 128:(b + 1) * 128]

    @pl.when(step < 4)
    def _():
        up = jnp.where(step == 3, 0.0, wn_ref[0])
        r = jnp.concatenate([h_ref[0] + w_ref[1] - w_ref[0], h_ref[1] + up - w_ref[1]], axis=0)
        for c0, res in x_modes(r, tab):
            for l in range(2):
                v = dot3(sh, sl, *split(res[l * 128:(l + 1) * 128]))
                for b in range(res.shape[1] // 128):
                    r2[c0 // 128 + b, 2 * step + l] = v[:, b * 128:(b + 1) * 128]

    @pl.when(step >= 4)
    def _():
        lt = step - 4
        lam = lx[...]

        def inner(bt, acc):
            rows = tile(bt)
            rs = [r2[lt, k, rows, :] for k in range(LEV)]
            mu, s0, s1 = cols[0, rows, :], cols[1, rows, :], cols[2, rows, :]
            base = lam + mu
            ps = []
            for m in range(LEV):
                p = combine(Q[:, m], rs) * inverse_of(base + float(THETA[m]))
                g_ref[m, rows, :] = p
                ps.append(p)
            a07[rows, :128] = combine(Q[0], ps)
            a07[rows, 128:] = combine(Q[7], ps)
            return tuple(acc[m] + s0 * ps[m] for m in range(LEV)) + tuple(
                acc[LEV + m] + s1 * ps[m] for m in range(LEV))
        acc = lax.fori_loop(0, ROWS // 8, inner, tuple(jnp.zeros((8, 128), F32) for _ in range(16)))
        for e in range(2):
            sums = [jnp.sum(acc[e * LEV + m], axis=0, keepdims=True) for m in range(LEV)]
            out_ref[0, 2 * ROWS + e * LEV:2 * ROWS + (e + 1) * LEV, :] = jnp.concatenate(
                [combine(Q[k], sums) for k in range(LEV)], axis=0)
        res = dot3(sh, sl, *split(a07[...]))
        out_ref[0, :ROWS, :] = res[:, :128] - hx[lt]
        out_ref[0, ROWS:2 * ROWS, :] = res[:, 128:]


def block_forward(h, w):
    two = pl.BlockSpec((2, ROWS, N), lambda g: (jnp.minimum(g, 3), 0, 0))
    return pl.pallas_call(
        block_forward_kernel, grid=(4 + NPX,),
        out_shape=(jax.ShapeDtypeStruct((NPX, BLK, 128), F32), jax.ShapeDtypeStruct((LEV, ROWS, N), F32), TOKEN),
        in_specs=[two, two, pl.BlockSpec((1, ROWS, N), lambda g: (jnp.minimum(2 * g + 2, 7), 0, 0)),
                  fixed((1536, 512)), fixed((256, 128)),
                  pl.BlockSpec((8, 128), lambda g: (0, jnp.maximum(g - 4, 0))), fixed((3, ROWS, 128))],
        out_specs=(pl.BlockSpec((1, BLK, 128), lambda g: (jnp.maximum(g - 4, 0), 0, 0)),
                   pl.BlockSpec((LEV, ROWS, 128), lambda g: (0, 0, jnp.maximum(g - 4, 0))), fixed((8, 128))),
        scratch_shapes=[pltpu.VMEM((NPX, LEV, ROWS, 128), F32), pltpu.VMEM((NPX, ROWS, 128), F32),
                        pltpu.VMEM((ROWS, 256), F32)],
        compiler_params=params(VMEM_MIB), name="block_forward",
    )(h, w, w, jnp.asarray(TAB), jnp.asarray(SINE2), jnp.asarray(LAM_X), jnp.asarray(COLS))


def lam_row(lx):
    return lx[0:1, pl.ds(pl.multiple_of(lax.axis_index("px") * 128, 128), 128)]


def edge_rows(x_ref, sr):
    for i in range(NPX):
        for k in range(LEV):
            cs = slice(k * 128, (k + 1) * 128)
            sr[i:i + 1, cs] = x_ref[(i + 7) % 8, 2 * ROWS + LEV + k:2 * ROWS + LEV + k + 1, :]
            sr[8 + i:9 + i, cs] = x_ref[(i + 1) % 8, 2 * ROWS + k:2 * ROWS + k + 1, :]
    return split(sr[...])


def edge_modes(edge, t, sh, sl):
    return dot3(edge[tile(t, 128), :], edge[pl.ds(pl.multiple_of(N + t * 128, 128), 128), :], sh, sl)


def y_forward_kernel(x_ref, tok, lx, ly, tab, edge, al_ref, pp, sr, st):
    x = jnp.concatenate([x_ref[:, :ROWS], x_ref[:, ROWS:2 * ROWS]], axis=-1).reshape(N, 256)
    s, d = x[:512] + x[512:], x[:512] - x[512:]
    ee, eo = s[:256] + s[256:], s[:256] - s[256:]
    te, to, td = tab_parts(tab)
    for v, t, k0 in ((ee, te, 0), (eo, to, 256), (d, td, 512)):
        res = dot3(*t, *split(v))
        pp[k0:k0 + res.shape[0], :] = res
    sh, sl = edge_rows(x_ref, sr)
    lam_x = lam_row(lx)

    def some(t, c):
        st[...] = edge_modes(edge, t, sh, sl)
        for q in range(8):
            part = slice(q * 16, (q + 1) * 16)
            rows = pl.ds(pl.multiple_of(t * 128 + q * 16, 16), 16)
            phi, theta, _ = slab_polys(ly[rows, :] + lam_x)
            inv = inverse_of(phi[0])
            b0 = b7 = None
            for k in range(LEV):
                sk = st[part, k * 128:(k + 1) * 128]
                b0 = phi[k + 1] * sk if k == 0 else b0 + phi[k + 1] * sk
                b7 = sk if k == 0 else b7 + theta[k] * sk
            j, at = 2 * t + q // 4, (q % 4) * 16
            al_ref[j, at:at + 16, :] = pp[rows, :128] + b0 * inv
            al_ref[j, 64 + at:80 + at, :] = pp[rows, 128:] + b7 * inv
        return c
    lax.fori_loop(0, 8, some, 0)


def y_forward(x, tok):
    return pl.pallas_call(
        y_forward_kernel, grid=(1,),
        out_shape=jax.ShapeDtypeStruct((NPY, 128, 128), F32),
        in_specs=[fixed((NPX, BLK, 128)), fixed((8, 128)), fixed((8, N)), fixed((N, 128)), fixed((1536, 512)),
                  fixed((2 * N, 16))],
        out_specs=fixed((NPY, 128, 128)),
        scratch_shapes=[pltpu.VMEM((N, 256), F32), pltpu.VMEM((16, N), F32), pltpu.VMEM((128, N), F32)],
        compiler_params=params(VMEM_MIB), name="y_forward",
    )(x, tok, jnp.asarray(LAM_X), jnp.asarray(LAM_Y), jnp.asarray(TAB_T), jnp.asarray(EDGE_F))


def ladder_kernel(al_ref, lx, ly, fl_ref, out_ref):
    for j in range(NPY):
        out_ref[j, 128:, :] = fl_ref[j]

    lam_x = lam_row(lx)
    mine = lax.axis_index("py") * 64
    for t in range(8):
        rows, tops = slice(t * 8, (t + 1) * 8), slice(64 + t * 8, 72 + t * 8)
        phi, theta, delta = slab_polys(ly[pl.ds(pl.multiple_of(mine + t * 8, 8), 8), :] + lam_x)
        inv = 1.0 / phi[0]
        n07, n77, cc = inv, theta[7] * inv, delta * inv
        A = [None] * 17
        B = [None] * 17
        e = [None] * 17
        A[16] = jnp.zeros_like(inv)
        B[16] = jnp.full_like(inv, -2.0)
        for j in range(15, -1, -1):
            g, q = al_ref[j, rows, :], al_ref[j, tops, :]
            e[j + 1] = inverse_of(1.0 - n77 * B[j + 1])
            be = B[j + 1] * e[j + 1]
            A[j] = g + n07 * (A[j + 1] + be * (q + n77 * A[j + 1]))
            B[j] = n07 * n07 * be - cc
        p = -A[0] / B[0]
        for j in range(16):
            out_ref[j, rows, :] = p
            p = (al_ref[j, tops, :] + n77 * A[j + 1] + n07 * p) * e[j + 1]
            out_ref[j, tops, :] = A[j + 1] + B[j + 1] * p


def ladder(al, fl):
    return pl.pallas_call(
        ladder_kernel, grid=(1,), out_shape=jax.ShapeDtypeStruct((NPY, 136, 128), F32),
        in_specs=[fixed((NPY, 128, 128)), fixed((8, N)), fixed((N, 128)), fixed((NPY, 8, 128))],
        out_specs=fixed((NPY, 136, 128)), compiler_params=params(VMEM_MIB), name="ladder",
    )(al, jnp.asarray(LAM_X), jnp.asarray(LAM_Y), fl)


def y_inverse_kernel(x_ref, pu_ref, lx, ly, tab, edge_f, edge_b, out_ref, tok_ref, sr, st, ph, pl_):
    tok_ref[...] = jnp.zeros((8, 128), F32)
    sh, sl = edge_rows(x_ref, sr)
    lam_x = lam_row(lx)

    def some(t, c):
        st[...] = edge_modes(edge_f, t, sh, sl)
        for q in range(8):
            part = slice(q * 16, (q + 1) * 16)
            rows = pl.ds(pl.multiple_of(t * 128 + q * 16, 16), 16)
            j, at = 2 * t + q // 4, (q % 4) * 16
            low, top = pu_ref[j, at:at + 16, :], pu_ref[j, 64 + at:80 + at, :]
            lam = ly[rows, :] + lam_x
            cs = [None] * 8
            fs = [None] * 8
            cs[7] = inverse_of(1.0 - lam)
            fs[7] = st[part, 7 * 128:] + top
            for k in range(6, -1, -1):
                cs[k] = inverse_of(2.0 - lam - cs[k + 1])
                fs[k] = st[part, k * 128:(k + 1) * 128] + cs[k + 1] * fs[k + 1]
            prev = low
            for k in range(8):
                prev = cs[k] * (fs[k] + prev)
                ph[rows, k * 128:(k + 1) * 128], pl_[rows, k * 128:(k + 1) * 128] = split(prev)
        return c
    lax.fori_loop(0, 8, some, 0)
    edges = dot3(edge_b[:16, :], edge_b[16:, :], ph[...], pl_[...])
    for i in range(NPX):
        below, above = (i + 7) % 8, (i + 1) % 8
        for k in range(LEV):
            cols = slice(k * 128, (k + 1) * 128)
            lo = 2 * ROWS + k
            hi = 2 * ROWS + LEV + k
            out_ref[i, lo:lo + 1, :] = edges[8 + below:9 + below, cols] + x_ref[below, hi:hi + 1, :]
            out_ref[i, hi:hi + 1, :] = edges[above:above + 1, cols] + x_ref[above, lo:lo + 1, :]
    for q in range(4):
        flux = (pu_ref[4 * q, 128:, :] + pu_ref[4 * q + 1, 128:, :]) + (
            pu_ref[4 * q + 2, 128:, :] + pu_ref[4 * q + 3, 128:, :])
        for i in range(NPX):
            out_ref[i, BLK + q:BLK + q + 1, :] = flux[i:i + 1, :]
            out_ref[i, BLK + 4 + q:BLK + 5 + q, :] = jnp.zeros((1, 128), F32)
    pu = jnp.concatenate([pu_ref[:, :64], pu_ref[:, 64:128]], axis=-1).reshape(N, 256)
    te, to, td = tab_parts(tab)
    t0 = dot3(*te, *split(pu[:256]))
    t1 = dot3(*to, *split(pu[256:512]))
    d = dot3(*td, *split(pu[512:]))
    ev = (t0 + t1, t0 - t1)
    for i in range(4):
        base = ev[i // 2][(i % 2) * 128:(i % 2 + 1) * 128]
        odd = d[i * 128:(i + 1) * 128]
        for l in range(2):
            cols = slice(l * 128, (l + 1) * 128)
            out_ref[i, l * ROWS:(l + 1) * ROWS, :] = base[:, cols] + odd[:, cols]
            out_ref[i + 4, l * ROWS:(l + 1) * ROWS, :] = base[:, cols] - odd[:, cols]


def y_inverse(x, pu):
    return pl.pallas_call(
        y_inverse_kernel, grid=(1,), out_shape=(jax.ShapeDtypeStruct((NPX, BACK, 128), F32), TOKEN),
        in_specs=[fixed((NPX, BLK, 128)), fixed((NPY, 136, 128)), fixed((8, N)), fixed((N, 128)), fixed((1536, 512)),
                  fixed((2 * N, 16)), fixed((32, N))],
        out_specs=(fixed((NPX, BACK, 128)), fixed((8, 128))),
        scratch_shapes=[pltpu.VMEM((16, N), F32), pltpu.VMEM((128, N), F32),
                        pltpu.VMEM((N, N), BF16), pltpu.VMEM((N, N), BF16)],
        compiler_params=params(VMEM_MIB), name="y_inverse",
    )(x, pu, jnp.asarray(LAM_X), jnp.asarray(LAM_Y), jnp.asarray(TAB), jnp.asarray(EDGE_F), jnp.asarray(EDGE_B))


def block_inverse_kernel(y_ref, g_ref, w_ref, roof_ref, tab, sine, lx, cols, ft, nr, hc, tok,
                         out_ref, nt_ref, field, wv, spu, fb):
    step = pl.program_id(0)
    sh, sl = sine[:128, :], sine[128:, :]

    @pl.when(step < NPX)
    def _():
        fb[step] = y_ref[0, BLK:, :]
        spu[...] = dot3(sh, sl, *split(jnp.concatenate([y_ref[0, :ROWS, :], y_ref[0, ROWS:2 * ROWS, :]], axis=1)))
        lam = lx[...]
        ql, qh = [], []
        for e, dst in ((0, ql), (1, qh)):
            rows = [y_ref[0, 2 * ROWS + e * LEV + k:2 * ROWS + e * LEV + k + 1, :] for k in range(LEV)]
            for m in range(LEV):
                dst.append(jnp.broadcast_to(combine(Q[:, m], rows), (8, 128)))

        def inner(bt, c):
            rows = tile(bt)
            mu, s0, s1 = cols[0, rows, :], cols[1, rows, :], cols[2, rows, :]
            base = lam + mu
            low, top = spu[rows, :128], spu[rows, 128:]
            ps = []
            for m in range(LEV):
                f = (float(Q[0, m]) * low + float(Q[7, m]) * top) + (s0 * ql[m] + s1 * qh[m])
                ps.append(g_ref[m, rows, :] - f * inverse_of(base + float(THETA[m])))
            for k in range(LEV):
                v = combine(DQ[k], ps)
                wv[rows, k * 128:(k + 1) * 128] = v - low if k == 0 else v
            return c
        lax.fori_loop(0, ROWS // 8, inner, 0)
        res = dot3(sh, sl, *split(wv[...]))
        for k in range(LEV):
            field[k, :, tile(step, 128)] = res[:, k * 128:(k + 1) * 128]

    @pl.when(step >= NPX)
    def _():
        pair = step - NPX
        v = jnp.concatenate([field[2 * pair], field[2 * pair + 1]], axis=0)
        te, to, td = tab_parts(tab)
        t0 = dot3(*split(v[:, :256]), *te)
        t1 = dot3(*split(v[:, 256:512]), *to)
        d = dot3(*split(v[:, 512:]), *td)
        s = jnp.concatenate([t0 + t1, t0 - t1], axis=1)
        for half, res in ((0, s + d), (1, s - d)):
            cs = slice(half * 512, (half + 1) * 512)
            for l in range(2):
                solid = lax.axis_index("py") * LEV + 2 * pair + l < roof_ref[:, cs]
                out_ref[l, :, cs] = jnp.where(solid, 0.0, w_ref[l, :, cs] - res[l * 128:(l + 1) * 128])

    @pl.when(step == NPX + 3)
    def _():
        flux = jnp.concatenate([fb[i, :4, :] for i in range(NPX)], axis=0)
        nt_ref[...] = ft[...] + (nr[...] - flux - 0.5 * ft[...]) / hc[...]


def block_inverse(y, g, w, roof, ft, nr, hc, tok):
    late = pl.BlockSpec((2, ROWS, N), lambda t: (jnp.maximum(t - NPX, 0), 0, 0))
    return pl.pallas_call(
        block_inverse_kernel, grid=(NPX + 4,),
        out_shape=(jax.ShapeDtypeStruct((LEV, ROWS, N), F32), jax.ShapeDtypeStruct((32, 128), F32)),
        in_specs=[pl.BlockSpec((1, BACK, 128), lambda t: (jnp.minimum(t, NPX - 1), 0, 0)),
                  pl.BlockSpec((LEV, ROWS, 128), lambda t: (0, 0, jnp.minimum(t, NPX - 1))),
                  late, fixed((ROWS, N)), fixed((1536, 512)), fixed((256, 128)),
                  pl.BlockSpec((8, 128), lambda t: (0, jnp.minimum(t, NPX - 1))), fixed((3, ROWS, 128)),
                  fixed((32, 128)), fixed((32, 128)), fixed((32, 128)), fixed((8, 128))],
        out_specs=(late, fixed((32, 128))),
        scratch_shapes=[pltpu.VMEM((LEV, ROWS, N), F32), pltpu.VMEM((ROWS, N), F32), pltpu.VMEM((ROWS, 256), F32),
                        pltpu.VMEM((NPX, 8, 128), F32)],
        compiler_params=params(VMEM_MIB), name="block_inverse",
    )(y, g, w, roof, jnp.asarray(TAB_T), jnp.asarray(SINE2), jnp.asarray(LAM_X), jnp.asarray(COLS), ft, nr, hc, tok)


def swap(x, axes):
    return lax.all_to_all(x, axes, split_axis=0, concat_axis=0, tiled=True)


def body(horiz_div, w_star, air_temp, roof_level, facet_cells, facet_temp, net_radiation,
         heat_capacity, drag_coef, heat_coef):
    ft, nr, hc, dr, he, ce = [
        v.reshape(32, 128) for v in (facet_temp, net_radiation, heat_capacity, drag_coef, heat_coef, facet_cells)]
    owner, ids, addr = pack_owner(ft, dr, he, ce)
    od = swap(owner.reshape(OWNERS, 1, 128), ("px", "py")).reshape(OWNERS, 128)
    addr = addr.reshape(OWNERS * SLOT)
    w2, a2 = w_star.reshape(1024, 1024), air_temp.reshape(1024, 1024)
    wc = gather_w(addr, ids, w2)
    w_corr = scatter_w(addr, ids, wc, od, w2).reshape(LEV, ROWS, N)
    sent, g, tok = block_forward(horiz_div, w_corr)
    xs = swap(sent, "px")
    flux, fl, tok = heat_flux(addr, tok, ids, wc, od, a2)
    pu = swap(ladder(swap(y_forward(xs, tok), "py"), fl), "py")
    back, tok = y_inverse(xs, pu)
    ys = swap(back, "px")
    theta, tok = new_theta(addr, tok, ids, flux, a2)
    w_new, temp_new = block_inverse(ys, g, w_corr, roof_level, ft, nr, hc, tok)
    return w_new, theta.reshape(LEV, ROWS, N), temp_new.reshape(1, OWNERS * SLOT)


def solution(mesh):
    field, facet = P("py", "px", None), P(("px", "py"), None)
    return jax.shard_map(
        body, mesh=mesh,
        in_specs=(field, field, field, P("px", None)) + (facet,) * 6,
        out_specs=(field, field, facet), check_vma=False)
```

```python
import functools
import math

import jax
import jax.numpy as jnp
import numpy as np
from jax import lax
from jax.experimental import pallas as pl
from jax.experimental.pallas import tpu as pltpu
from jax.sharding import PartitionSpec as P

N = 1024
NPX, NPY = 8, 16
LEV, ROWS = 8, 128
OWNERS, SLOT = 128, 32
MIB = 1 << 20
VMEM_MIB = 58
F32, BF16 = jnp.float32, jnp.bfloat16


def mode_table():
    classes = [np.arange(0, 513, 4), np.arange(2, 513, 4), np.arange(1, 512, 2)]
    n = np.arange(N)
    cols, waves = [], []
    for ks in classes:
        for k in ks:
            edge = k == 0 or k == N // 2
            norm = math.sqrt((1.0 if edge else 2.0) / N)
            cols.append(norm * np.cos(2 * np.pi * ((n * k) % N) / N))
            waves.append(k)
        for k in ks:
            if k == 0 or k == N // 2:
                continue
            cols.append(math.sqrt(2.0 / N) * np.sin(2 * np.pi * ((n * k) % N) / N))
            waves.append(k)
    table = np.stack(cols, axis=1)
    eigen = -4.0 * np.sin(np.pi * np.array(waves) / N) ** 2
    return table, eigen


def split_np(a):
    a = a.astype(np.float32)
    hi = a.astype(jnp.bfloat16)
    lo = (a - hi.astype(np.float32)).astype(jnp.bfloat16)
    return hi, lo


TABLE, EIGEN = mode_table()
T_EE = TABLE[:256, :256]
T_EO = TABLE[:256, 256:512]
T_OD = TABLE[:512, 512:]


def split(v):
    hi = v.astype(BF16)
    return hi, (v - hi.astype(F32)).astype(BF16)


def dot3(ah, al, bh, bl):
    d = functools.partial(jnp.dot, preferred_element_type=F32)
    return d(ah, bh) + (d(al, bh) + d(ah, bl))


def params(mb, sem=None):
    return pltpu.CompilerParams(vmem_limit_bytes=mb * MIB)


TOKEN = jax.ShapeDtypeStruct((8, 128), F32)
VM = pl.BlockSpec(memory_space=pltpu.VMEM)
SM = pl.BlockSpec(memory_space=pltpu.SMEM)


def pack_kernel(ft, dr, he, ce, od, ids, addr):
    zero = jnp.zeros((32, 32), F32)
    none = jnp.zeros((32, 96), jnp.int32)
    for q in range(4):
        c = slice(q * 32, (q + 1) * 32)
        od[pl.ds(q, 32, stride=4), :] = jnp.concatenate([ft[:, c], dr[:, c], he[:, c], zero], axis=1)
        ids[pl.ds(q, 32, stride=4), :] = jnp.concatenate([ce[:, c], none], axis=1)
    safe = jnp.maximum(ce[...], 0)
    row = safe >> 10
    addr[...] = (row >> 3) * 64 + ((safe >> 7) & 7) * 8 + (row & 7)


def pack_owner(ft, dr, he, ce):
    full = jax.ShapeDtypeStruct((OWNERS, 128), F32)
    return pl.pallas_call(
        pack_kernel, out_shape=(full, jax.ShapeDtypeStruct((OWNERS, 128), jnp.int32),
                                jax.ShapeDtypeStruct((32, 128), jnp.int32)),
        in_specs=[VM] * 4, out_specs=(VM,) * 3, compiler_params=params(VMEM_MIB), name="pack_owner",
    )(ft, dr, he, ce)


def load_w(w_ref, wt):
    def one(tr, c):
        for ct in range(8):
            wt[tile(tr * 8 + ct), :] = w_ref[tile(tr), ct * 128:(ct + 1) * 128]
        return c
    lax.fori_loop(0, 128, one, 0)


def load_temp(a_ref, tt):
    def one(i, c):
        for ct in range(8):
            v = a_ref[tile(i, 16), ct * 128:(ct + 1) * 128].astype(F32)
            tt[tile(i * 16 + ct), :] = v[:8]
            tt[tile(i * 16 + 8 + ct), :] = v[8:]
        return c
    lax.fori_loop(0, 64, one, 0)


def gather_rows(addr, src, buf):
    def one(o, c):
        for s in range(SLOT):
            buf[pl.ds(s * OWNERS + o, 1), :] = src[pl.ds(addr[o * SLOT + s], 1), :]
        return c
    lax.fori_loop(0, OWNERS, one, 0)


def hits(ids, s, lane):
    col = ids[:, s:s + 1]
    return lane == jnp.where(col >= 0, col & 127, -1)


def pick(ids, buf):
    lane = lax.broadcasted_iota(jnp.int32, (OWNERS, 128), 1)
    out = jnp.zeros((OWNERS, 128), F32)
    for s in range(SLOT):
        v = jnp.where(hits(ids, s, lane), buf[s * OWNERS:(s + 1) * OWNERS, :], 0.0)
        out = jnp.where(lane == s, jnp.sum(v, axis=1, keepdims=True), out)
    return out


def spread_rows(ids, vals, buf):
    lane = lax.broadcasted_iota(jnp.int32, (OWNERS, 128), 1)
    for s in range(SLOT):
        buf[s * OWNERS:(s + 1) * OWNERS, :] = jnp.where(hits(ids, s, lane), vals[:, s:s + 1], 0.0)


def clear(accs):
    def one(i, c):
        for a in accs:
            for j in range(8):
                a[tile(i * 8 + j), :] = jnp.zeros((8, 128), F32)
        return c
    lax.fori_loop(0, 128, one, 0)


def add_rows(addr, accs, buf):
    width = len(accs)

    def one(o, c):
        for s in range(0, SLOT, width):
            at = [addr[o * SLOT + s + j] for j in range(width)]
            new = [accs[j][pl.ds(at[j], 1), :] + buf[pl.ds((s + j) * OWNERS + o, 1), :] for j in range(width)]
            for j in range(width):
                accs[j][pl.ds(at[j], 1), :] = new[j]
        return c
    lax.fori_loop(0, OWNERS, one, 0)


def total(accs, rows):
    return (accs[0][rows, :] + accs[1][rows, :]) + (accs[2][rows, :] + accs[3][rows, :])


def gather_kernel(addr, ids_ref, w_ref, wc_ref, wt, buf):
    load_w(w_ref, wt)
    gather_rows(addr, wt, buf)
    wc_ref[...] = pick(ids_ref[...], buf)


def gather_w(addr, ids, w2):
    return pl.pallas_call(
        gather_kernel, out_shape=jax.ShapeDtypeStruct((OWNERS, 128), F32), in_specs=[SM, VM, VM], out_specs=VM,
        scratch_shapes=[pltpu.VMEM((8192, 128), F32), pltpu.VMEM((4096, 128), F32)],
        compiler_params=params(VMEM_MIB), name="facet_gather",
    )(addr, ids, w2)


FOUR = [pltpu.VMEM((8192, 128), F32)] * 4 + [pltpu.VMEM((4096, 128), F32)]


def flux_kernel(addr, tok_in, ids_ref, wc_ref, od_ref, a_ref, flux_ref, fl_ref, tok_ref, tt, buf, turned):
    load_temp(a_ref, tt)
    gather_rows(addr, tt, buf)
    tc = pick(ids_ref[...], buf)[:, :SLOT]
    wc = wc_ref[:, :SLOT]
    flux = od_ref[:, 64:96] * jnp.sqrt(wc * wc + 0.25) * (od_ref[:, :32] - tc)
    wide = jnp.concatenate([flux, jnp.zeros((OWNERS, 96), F32)], axis=1)
    flux_ref[...] = wide
    turned[...] = pltpu.roll(wide, (lax.axis_index("py") % 4) * SLOT, 1)
    for j in range(NPY):
        fl_ref[j] = turned[pl.ds(j, 8, stride=16), :]
    tok_ref[...] = tok_in[...]


def heat_flux(addr, tok, ids, wc, od, a2):
    return pl.pallas_call(
        flux_kernel,
        out_shape=(jax.ShapeDtypeStruct((OWNERS, 128), F32), jax.ShapeDtypeStruct((NPY, 8, 128), F32), TOKEN),
        in_specs=[SM] + [VM] * 5, out_specs=(VM,) * 3,
        scratch_shapes=[pltpu.VMEM((8192, 128), F32), pltpu.VMEM((4096, 128), F32), pltpu.VMEM((OWNERS, 128), F32)],
        cost_estimate=pl.CostEstimate(flops=0, bytes_accessed=25 * MIB, transcendentals=0),
        compiler_params=params(VMEM_MIB), name="heat_flux",
    )(addr, tok, ids, wc, od, a2)


def theta_kernel(addr, tok_in, ids_ref, flux_ref, a_ref, th_ref, tok_ref, acc0, acc1, acc2, acc3, buf):
    accs = (acc0, acc1, acc2, acc3)
    load_temp(a_ref, acc0)
    clear(accs[1:])
    spread_rows(ids_ref[...], flux_ref[...], buf)
    add_rows(addr, accs, buf)

    def put(i, c):
        for ct in range(8):
            v0 = total(accs, tile(i * 16 + ct))
            v1 = total(accs, tile(i * 16 + 8 + ct))
            th_ref[tile(i, 16), ct * 128:(ct + 1) * 128] = jnp.concatenate([v0, v1], axis=0).astype(BF16)
        return c
    lax.fori_loop(0, 64, put, 0)
    tok_ref[...] = tok_in[...]


def new_theta(addr, tok, ids, flux, a2):
    return pl.pallas_call(
        theta_kernel, out_shape=(jax.ShapeDtypeStruct((1024, 1024), BF16), TOKEN),
        in_specs=[SM] + [VM] * 4, out_specs=(VM, VM), scratch_shapes=FOUR,
        cost_estimate=pl.CostEstimate(flops=0, bytes_accessed=40 * MIB, transcendentals=0),
        compiler_params=params(VMEM_MIB), name="new_theta",
    )(addr, tok, ids, flux, a2)


BLK = 2 * ROWS + 2 * LEV
BACK = BLK + 8


def y_basis():
    i = np.arange(ROWS) + 1
    s = math.sqrt(2 / 129) * np.sin(np.pi * (np.outer(i, i) % 258) / 129)
    mu = -4.0 * np.sin(np.pi * i / 258) ** 2
    return s, mu


SINE, MU = y_basis()
EDGE = np.concatenate([TABLE[0::ROWS], TABLE[ROWS - 1::ROWS]])


def pack(transposed):
    parts = [split_np(t.T if transposed else t) for t in (T_EE, T_EO, T_OD)]
    (eh, el), (oh, ol), (dh, dl) = parts
    return np.concatenate([dh, dl, np.concatenate([np.concatenate([eh, oh], 1), np.concatenate([el, ol], 1)])])


TAB, TAB_T = pack(False), pack(True)
SINE2 = np.concatenate(split_np(SINE))
EDGE_F = np.concatenate(split_np(EDGE.T))
EDGE_B = np.concatenate(split_np(EDGE))
LAM_Y = np.broadcast_to(EIGEN.astype(np.float32)[:, None], (N, 128)).copy()
LAM_X = np.broadcast_to(EIGEN.astype(np.float32), (8, N)).copy()
COLS = np.stack([np.broadcast_to(v[:, None], (ROWS, 128)) for v in (SINE[:, 0], SINE[:, 127])]).astype(np.float32)


def pivots():
    lam = MU[:, None] + EIGEN[None, :]
    c = [1.0 / (1.0 - lam)]
    for _ in range(LEV - 1):
        c.insert(0, 1.0 / (2.0 - lam - c[0]))
    return np.stack(c).astype(np.float32)


PIVOT = pivots()


def tab_parts(t):
    return ((t[1024:1280, :256], t[1280:1536, :256]), (t[1024:1280, 256:], t[1280:1536, 256:]),
            (t[:512], t[512:1024]))


def tile(i, size=8):
    return pl.ds(pl.multiple_of(i * size, size), size)


def fixed(shape):
    return pl.BlockSpec(shape, lambda g: (0,) * len(shape))


def slab_polys(lam):
    phi = [None] * 9
    phi[8] = jnp.ones_like(lam)
    delta = -lam
    phi[7] = phi[8] + delta
    for k in range(6, -1, -1):
        delta = delta - lam * phi[k + 1]
        phi[k] = phi[k + 1] + delta
    theta = [jnp.ones_like(lam), 2.0 - lam]
    for k in range(2, 8):
        theta.append((2.0 - lam) * theta[k - 1] - theta[k - 2])
    return phi, theta, delta


def inverse_of(v):
    r = pl.reciprocal(v, approx=True)
    r = r * (2.0 - v * r)
    return r * (2.0 - v * r)


def x_modes(v, tab):
    s, d = v[:, :512] + v[:, 512:], v[:, :512] - v[:, 512:]
    te, to, td = tab_parts(tab)
    return ((0, dot3(*split(s[:, :256] + s[:, 256:]), *te)), (256, dot3(*split(s[:, :256] - s[:, 256:]), *to)),
            (512, dot3(*split(d), *td)))


STRIP = 32


def fold(v):
    return jnp.sum(v.reshape(STRIP // 8, 8, 128), axis=0)


def eliminate(fs, cs):
    fs = list(fs)
    for k in range(LEV - 2, -1, -1):
        fs[k] = fs[k] + cs[k + 1] * fs[k + 1]
    ps = [cs[0] * fs[0]]
    for k in range(1, LEV):
        ps.append(cs[k] * (fs[k] + ps[k - 1]))
    return ps


def block_forward_kernel(addr, ids_ref, wc_ref, od_ref, w_ref, h_ref, tab, sine, piv, cols,
                         wo_ref, out_ref, r_ref, tok_ref,
                         acc0, acc1, acc2, acc3, buf, wf, r2, hx, a07):
    step = pl.program_id(0)
    sh, sl = sine[:128, :], sine[128:, :]

    @pl.when(step == 0)
    def _():
        tok_ref[...] = jnp.zeros((8, 128), F32)
        accs = (acc0, acc1, acc2, acc3)
        load_w(w_ref, acc0)
        clear(accs[1:])
        wc = wc_ref[:, :SLOT]
        stress = od_ref[:, 32:64] * jnp.sqrt(wc * wc + 0.25) * wc
        spread_rows(ids_ref[...], -stress, buf)
        add_rows(addr, accs, buf)

        def put(tr, c):
            for ct in range(8):
                wf[tr // 16, tile(tr % 16), ct * 128:(ct + 1) * 128] = total(accs, tile(tr * 8 + ct))
            return c
        lax.fori_loop(0, 128, put, 0)
        lifted = (lax.axis_index("py") > 0).astype(F32)
        for c0, res in x_modes(wf[0] * lifted, tab):
            for b in range(res.shape[1] // 128):
                hx[c0 // 128 + b] = res[:, b * 128:(b + 1) * 128]

    @pl.when((step > 0) & (step < 5))
    def _():
        lv = 2 * step - 2
        w0, w1 = wf[lv], wf[lv + 1]
        wo_ref[0] = w0
        wo_ref[1] = w1
        up = jnp.where(step == 4, 0.0, wf[jnp.minimum(lv + 2, LEV - 1)])
        r = jnp.concatenate([h_ref[0] + w1 - w0, h_ref[1] + up - w1], axis=0)
        for c0, res in x_modes(r, tab):
            for l in range(2):
                v = dot3(sh, sl, *split(res[l * 128:(l + 1) * 128]))
                for b in range(res.shape[1] // 128):
                    r2[c0 // 128 + b, lv + l] = v[:, b * 128:(b + 1) * 128]

    @pl.when(step >= 5)
    def _():
        lt = step - 5

        def inner(bt, acc):
            rows = tile(bt, STRIP)
            rs = [r2[lt, k, rows, :] for k in range(LEV)]
            for k in range(LEV):
                r_ref[k, rows, :] = rs[k]
            ps = eliminate(rs, [piv[k, rows, :] for k in range(LEV)])
            s0, s1 = cols[0, rows, :], cols[1, rows, :]
            a07[rows, :128] = ps[0]
            a07[rows, 128:] = ps[7]
            return tuple(acc[k] + fold(s0 * ps[k]) for k in range(LEV)) + tuple(
                acc[LEV + k] + fold(s1 * ps[k]) for k in range(LEV))
        acc = lax.fori_loop(0, ROWS // STRIP, inner, tuple(jnp.zeros((8, 128), F32) for _ in range(16)))
        for e in range(2):
            sums = [jnp.sum(acc[e * LEV + k], axis=0, keepdims=True) for k in range(LEV)]
            out_ref[0, 2 * ROWS + e * LEV:2 * ROWS + (e + 1) * LEV, :] = -jnp.concatenate(sums, axis=0)
        res = dot3(sh, sl, *split(a07[...]))
        out_ref[0, :ROWS, :] = -res[:, :128] - hx[lt]
        out_ref[0, ROWS:2 * ROWS, :] = -res[:, 128:]


def block_forward(addr, ids, wc, od, w2, h):
    two = pl.BlockSpec((2, ROWS, N), lambda g: (jnp.clip(g - 1, 0, 3), 0, 0))
    col = pl.BlockSpec((LEV, ROWS, 128), lambda g: (0, 0, jnp.maximum(g - 5, 0)))
    small = fixed((OWNERS, 128))
    big = jax.ShapeDtypeStruct((LEV, ROWS, N), F32)
    return pl.pallas_call(
        block_forward_kernel, grid=(5 + NPX,),
        out_shape=(big, jax.ShapeDtypeStruct((NPX, BLK, 128), F32), big, TOKEN),
        in_specs=[SM, small, small, small, pl.BlockSpec((N, N), lambda g: (0, 0)), two, fixed((1536, 512)),
                  fixed((256, 128)), col, fixed((2, ROWS, 128))],
        out_specs=(two, pl.BlockSpec((1, BLK, 128), lambda g: (jnp.maximum(g - 5, 0), 0, 0)), col, fixed((8, 128))),
        scratch_shapes=FOUR + [pltpu.VMEM((LEV, ROWS, N), F32), pltpu.VMEM((NPX, LEV, ROWS, 128), F32),
                               pltpu.VMEM((NPX, ROWS, 128), F32), pltpu.VMEM((ROWS, 256), F32)],
        compiler_params=params(VMEM_MIB), name="block_forward",
    )(addr, ids, wc, od, w2, h, jnp.asarray(TAB), jnp.asarray(SINE2), jnp.asarray(PIVOT), jnp.asarray(COLS))


def lam_row(lx):
    return lx[0:1, pl.ds(pl.multiple_of(lax.axis_index("px") * 128, 128), 128)]


def edge_rows(x_ref, sr):
    for i in range(NPX):
        for k in range(LEV):
            cs = slice(k * 128, (k + 1) * 128)
            sr[i:i + 1, cs] = x_ref[(i + 7) % 8, 2 * ROWS + LEV + k:2 * ROWS + LEV + k + 1, :]
            sr[8 + i:9 + i, cs] = x_ref[(i + 1) % 8, 2 * ROWS + k:2 * ROWS + k + 1, :]
    return split(sr[...])


def edge_modes(edge, t, sh, sl):
    return dot3(edge[tile(t, 128), :], edge[pl.ds(pl.multiple_of(N + t * 128, 128), 128), :], sh, sl)


def y_forward_kernel(x_ref, tok, lx, ly, tab, edge, al_ref, pp, sr, st):
    x = jnp.concatenate([x_ref[:, :ROWS], x_ref[:, ROWS:2 * ROWS]], axis=-1).reshape(N, 256)
    s, d = x[:512] + x[512:], x[:512] - x[512:]
    ee, eo = s[:256] + s[256:], s[:256] - s[256:]
    te, to, td = tab_parts(tab)
    for v, t, k0 in ((ee, te, 0), (eo, to, 256), (d, td, 512)):
        res = dot3(*t, *split(v))
        pp[k0:k0 + res.shape[0], :] = res
    sh, sl = edge_rows(x_ref, sr)
    lam_x = lam_row(lx)

    def some(t, c):
        st[...] = edge_modes(edge, t, sh, sl)
        for q in range(8):
            part = slice(q * 16, (q + 1) * 16)
            rows = pl.ds(pl.multiple_of(t * 128 + q * 16, 16), 16)
            phi, theta, _ = slab_polys(ly[rows, :] + lam_x)
            inv = inverse_of(phi[0])
            b0 = b7 = None
            for k in range(LEV):
                sk = st[part, k * 128:(k + 1) * 128]
                b0 = phi[k + 1] * sk if k == 0 else b0 + phi[k + 1] * sk
                b7 = sk if k == 0 else b7 + theta[k] * sk
            j, at = 2 * t + q // 4, (q % 4) * 16
            al_ref[j, at:at + 16, :] = pp[rows, :128] + b0 * inv
            al_ref[j, 64 + at:80 + at, :] = pp[rows, 128:] + b7 * inv
        return c
    lax.fori_loop(0, 8, some, 0)


def y_forward(x, tok):
    return pl.pallas_call(
        y_forward_kernel, grid=(1,),
        out_shape=jax.ShapeDtypeStruct((NPY, 128, 128), F32),
        in_specs=[fixed((NPX, BLK, 128)), fixed((8, 128)), fixed((8, N)), fixed((N, 128)), fixed((1536, 512)),
                  fixed((2 * N, 16))],
        out_specs=fixed((NPY, 128, 128)),
        scratch_shapes=[pltpu.VMEM((N, 256), F32), pltpu.VMEM((16, N), F32), pltpu.VMEM((128, N), F32)],
        compiler_params=params(VMEM_MIB), name="y_forward",
    )(x, tok, jnp.asarray(LAM_X), jnp.asarray(LAM_Y), jnp.asarray(TAB_T), jnp.asarray(EDGE_F))


def ladder_kernel(al_ref, lx, ly, fl_ref, out_ref):
    for j in range(NPY):
        out_ref[j, 128:, :] = fl_ref[j]

    lam_x = lam_row(lx)
    mine = lax.axis_index("py") * 64
    for t in range(8):
        rows, tops = slice(t * 8, (t + 1) * 8), slice(64 + t * 8, 72 + t * 8)
        phi, theta, delta = slab_polys(ly[pl.ds(pl.multiple_of(mine + t * 8, 8), 8), :] + lam_x)
        inv = 1.0 / phi[0]
        n07, n77, cc = inv, theta[7] * inv, delta * inv
        A = [None] * 17
        B = [None] * 17
        e = [None] * 17
        A[16] = jnp.zeros_like(inv)
        B[16] = jnp.full_like(inv, -2.0)
        for j in range(15, -1, -1):
            g, q = al_ref[j, rows, :], al_ref[j, tops, :]
            e[j + 1] = inverse_of(1.0 - n77 * B[j + 1])
            be = B[j + 1] * e[j + 1]
            A[j] = g + n07 * (A[j + 1] + be * (q + n77 * A[j + 1]))
            B[j] = n07 * n07 * be - cc
        p = -A[0] / B[0]
        for j in range(16):
            out_ref[j, rows, :] = p
            p = (al_ref[j, tops, :] + n77 * A[j + 1] + n07 * p) * e[j + 1]
            out_ref[j, tops, :] = A[j + 1] + B[j + 1] * p


def ladder(al, fl):
    return pl.pallas_call(
        ladder_kernel, grid=(1,), out_shape=jax.ShapeDtypeStruct((NPY, 136, 128), F32),
        in_specs=[fixed((NPY, 128, 128)), fixed((8, N)), fixed((N, 128)), fixed((NPY, 8, 128))],
        out_specs=fixed((NPY, 136, 128)), compiler_params=params(VMEM_MIB), name="ladder",
    )(al, jnp.asarray(LAM_X), jnp.asarray(LAM_Y), fl)


def y_inverse_kernel(x_ref, pu_ref, lx, ly, tab, edge_f, edge_b, out_ref, tok_ref, sr, st, ph, pl_):
    tok_ref[...] = jnp.zeros((8, 128), F32)
    sh, sl = edge_rows(x_ref, sr)
    lam_x = lam_row(lx)

    def some(t, c):
        st[...] = edge_modes(edge_f, t, sh, sl)
        for q in range(8):
            part = slice(q * 16, (q + 1) * 16)
            rows = pl.ds(pl.multiple_of(t * 128 + q * 16, 16), 16)
            j, at = 2 * t + q // 4, (q % 4) * 16
            low, top = pu_ref[j, at:at + 16, :], pu_ref[j, 64 + at:80 + at, :]
            lam = ly[rows, :] + lam_x
            cs = [None] * 8
            fs = [None] * 8
            cs[7] = inverse_of(1.0 - lam)
            fs[7] = st[part, 7 * 128:] + top
            for k in range(6, -1, -1):
                cs[k] = inverse_of(2.0 - lam - cs[k + 1])
                fs[k] = st[part, k * 128:(k + 1) * 128] + cs[k + 1] * fs[k + 1]
            prev = low
            for k in range(8):
                prev = cs[k] * (fs[k] + prev)
                ph[rows, k * 128:(k + 1) * 128], pl_[rows, k * 128:(k + 1) * 128] = split(prev)
        return c
    lax.fori_loop(0, 8, some, 0)
    edges = dot3(edge_b[:16, :], edge_b[16:, :], ph[...], pl_[...])
    for i in range(NPX):
        below, above = (i + 7) % 8, (i + 1) % 8
        for k in range(LEV):
            cols = slice(k * 128, (k + 1) * 128)
            lo = 2 * ROWS + k
            hi = 2 * ROWS + LEV + k
            out_ref[i, lo:lo + 1, :] = edges[8 + below:9 + below, cols] + x_ref[below, hi:hi + 1, :]
            out_ref[i, hi:hi + 1, :] = edges[above:above + 1, cols] + x_ref[above, lo:lo + 1, :]
    for q in range(4):
        flux = (pu_ref[4 * q, 128:, :] + pu_ref[4 * q + 1, 128:, :]) + (
            pu_ref[4 * q + 2, 128:, :] + pu_ref[4 * q + 3, 128:, :])
        for i in range(NPX):
            out_ref[i, BLK + q:BLK + q + 1, :] = flux[i:i + 1, :]
            out_ref[i, BLK + 4 + q:BLK + 5 + q, :] = jnp.zeros((1, 128), F32)
    pu = jnp.concatenate([pu_ref[:, :64], pu_ref[:, 64:128]], axis=-1).reshape(N, 256)
    te, to, td = tab_parts(tab)
    t0 = dot3(*te, *split(pu[:256]))
    t1 = dot3(*to, *split(pu[256:512]))
    d = dot3(*td, *split(pu[512:]))
    ev = (t0 + t1, t0 - t1)
    for i in range(4):
        base = ev[i // 2][(i % 2) * 128:(i % 2 + 1) * 128]
        odd = d[i * 128:(i + 1) * 128]
        for l in range(2):
            cols = slice(l * 128, (l + 1) * 128)
            out_ref[i, l * ROWS:(l + 1) * ROWS, :] = base[:, cols] + odd[:, cols]
            out_ref[i + 4, l * ROWS:(l + 1) * ROWS, :] = base[:, cols] - odd[:, cols]


def y_inverse(x, pu):
    return pl.pallas_call(
        y_inverse_kernel, grid=(1,), out_shape=(jax.ShapeDtypeStruct((NPX, BACK, 128), F32), TOKEN),
        in_specs=[fixed((NPX, BLK, 128)), fixed((NPY, 136, 128)), fixed((8, N)), fixed((N, 128)), fixed((1536, 512)),
                  fixed((2 * N, 16)), fixed((32, N))],
        out_specs=(fixed((NPX, BACK, 128)), fixed((8, 128))),
        scratch_shapes=[pltpu.VMEM((16, N), F32), pltpu.VMEM((128, N), F32),
                        pltpu.VMEM((N, N), BF16), pltpu.VMEM((N, N), BF16)],
        compiler_params=params(VMEM_MIB), name="y_inverse",
    )(x, pu, jnp.asarray(LAM_X), jnp.asarray(LAM_Y), jnp.asarray(TAB), jnp.asarray(EDGE_F), jnp.asarray(EDGE_B))


def block_inverse_kernel(y_ref, g_ref, w_ref, roof_ref, tab, sine, piv, cols, ft, nr, hc, tok,
                         out_ref, nt_ref, field, wv, spu, fb):
    step = pl.program_id(0)
    sh, sl = sine[:128, :], sine[128:, :]

    @pl.when(step < NPX)
    def _():
        fb[step] = y_ref[0, BLK:, :]
        spu[...] = dot3(sh, sl, *split(jnp.concatenate([y_ref[0, :ROWS, :], y_ref[0, ROWS:2 * ROWS, :]], axis=1)))
        edge = [y_ref[0, 2 * ROWS + k:2 * ROWS + k + 1, :] for k in range(2 * LEV)]

        def inner(bt, c):
            rows = tile(bt, STRIP)
            s0, s1 = cols[0, rows, :], cols[1, rows, :]
            low, top = spu[rows, :128], spu[rows, 128:]
            fs = [s0 * edge[k] + s1 * edge[LEV + k] - g_ref[k, rows, :] for k in range(LEV)]
            fs[0] = fs[0] + low
            fs[7] = fs[7] + top
            prev = low
            for k, p in enumerate(eliminate(fs, [piv[k, rows, :] for k in range(LEV)])):
                wv[rows, k * 128:(k + 1) * 128] = p - prev
                prev = p
            return c
        lax.fori_loop(0, ROWS // STRIP, inner, 0)
        res = dot3(sh, sl, *split(wv[...]))
        for k in range(LEV):
            field[k, :, tile(step, 128)] = res[:, k * 128:(k + 1) * 128]

    @pl.when(step >= NPX)
    def _():
        pair = step - NPX
        v = jnp.concatenate([field[2 * pair], field[2 * pair + 1]], axis=0)
        te, to, td = tab_parts(tab)
        t0 = dot3(*split(v[:, :256]), *te)
        t1 = dot3(*split(v[:, 256:512]), *to)
        d = dot3(*split(v[:, 512:]), *td)
        s = jnp.concatenate([t0 + t1, t0 - t1], axis=1)
        for half, res in ((0, s + d), (1, s - d)):
            cs = slice(half * 512, (half + 1) * 512)
            for l in range(2):
                solid = lax.axis_index("py") * LEV + 2 * pair + l < roof_ref[:, cs]
                out_ref[l, :, cs] = jnp.where(solid, 0.0, w_ref[l, :, cs] - res[l * 128:(l + 1) * 128])

    @pl.when(step == NPX + 3)
    def _():
        flux = jnp.concatenate([fb[i, :4, :] for i in range(NPX)], axis=0)
        nt_ref[...] = ft[...] + (nr[...] - flux - 0.5 * ft[...]) / hc[...]


def block_inverse(y, g, w, roof, ft, nr, hc, tok):
    late = pl.BlockSpec((2, ROWS, N), lambda t: (jnp.maximum(t - NPX, 0), 0, 0))
    return pl.pallas_call(
        block_inverse_kernel, grid=(NPX + 4,),
        out_shape=(jax.ShapeDtypeStruct((LEV, ROWS, N), F32), jax.ShapeDtypeStruct((32, 128), F32)),
        in_specs=[pl.BlockSpec((1, BACK, 128), lambda t: (jnp.minimum(t, NPX - 1), 0, 0)),
                  pl.BlockSpec((LEV, ROWS, 128), lambda t: (0, 0, jnp.minimum(t, NPX - 1))),
                  late, fixed((ROWS, N)), fixed((1536, 512)), fixed((256, 128)),
                  pl.BlockSpec((LEV, ROWS, 128), lambda t: (0, 0, jnp.minimum(t, NPX - 1))), fixed((2, ROWS, 128)),
                  fixed((32, 128)), fixed((32, 128)), fixed((32, 128)), fixed((8, 128))],
        out_specs=(late, fixed((32, 128))),
        scratch_shapes=[pltpu.VMEM((LEV, ROWS, N), F32), pltpu.VMEM((ROWS, N), F32), pltpu.VMEM((ROWS, 256), F32),
                        pltpu.VMEM((NPX, 8, 128), F32)],
        compiler_params=params(VMEM_MIB), name="block_inverse",
    )(y, g, w, roof, jnp.asarray(TAB_T), jnp.asarray(SINE2), jnp.asarray(PIVOT), jnp.asarray(COLS), ft, nr, hc, tok)


def swap(x, axes):
    return lax.all_to_all(x, axes, split_axis=0, concat_axis=0, tiled=True)


def body(horiz_div, w_star, air_temp, roof_level, facet_cells, facet_temp, net_radiation,
         heat_capacity, drag_coef, heat_coef):
    ft, nr, hc, dr, he, ce = [
        v.reshape(32, 128) for v in (facet_temp, net_radiation, heat_capacity, drag_coef, heat_coef, facet_cells)]
    owner, ids, addr = pack_owner(ft, dr, he, ce)
    od = swap(owner.reshape(OWNERS, 1, 128), ("px", "py")).reshape(OWNERS, 128)
    addr = addr.reshape(OWNERS * SLOT)
    w2, a2 = w_star.reshape(1024, 1024), air_temp.reshape(1024, 1024)
    wc = gather_w(addr, ids, w2)
    w_corr, sent, g, tok = block_forward(addr, ids, wc, od, w2, horiz_div)
    xs = swap(sent, "px")
    flux, fl, tok = heat_flux(addr, tok, ids, wc, od, a2)
    pu = swap(ladder(swap(y_forward(xs, tok), "py"), fl), "py")
    back, tok = y_inverse(xs, pu)
    ys = swap(back, "px")
    theta, tok = new_theta(addr, tok, ids, flux, a2)
    w_new, temp_new = block_inverse(ys, g, w_corr, roof_level, ft, nr, hc, tok)
    return w_new, theta.reshape(LEV, ROWS, N), temp_new.reshape(1, OWNERS * SLOT)


def solution(mesh):
    field, facet = P("py", "px", None), P(("px", "py"), None)
    return jax.shard_map(
        body, mesh=mesh,
        in_specs=(field, field, field, P("px", None)) + (facet,) * 6,
        out_specs=(field, field, facet), check_vma=False)
```

```python
import functools
import math

import jax
import jax.numpy as jnp
import numpy as np
from jax import lax
from jax.experimental import pallas as pl
from jax.experimental.pallas import tpu as pltpu
from jax.sharding import PartitionSpec as P

N = 1024
NPX, NPY = 8, 16
LEV, ROWS = 8, 128
OWNERS, SLOT = 128, 32
MIB = 1 << 20
VMEM_MIB = 50
F32, BF16 = jnp.float32, jnp.bfloat16


def mode_table():
    classes = [np.arange(0, 513, 4), np.arange(2, 513, 4), np.arange(1, 512, 2)]
    n = np.arange(N)
    cols, waves = [], []
    for ks in classes:
        for k in ks:
            edge = k == 0 or k == N // 2
            norm = math.sqrt((1.0 if edge else 2.0) / N)
            cols.append(norm * np.cos(2 * np.pi * ((n * k) % N) / N))
            waves.append(k)
        for k in ks:
            if k == 0 or k == N // 2:
                continue
            cols.append(math.sqrt(2.0 / N) * np.sin(2 * np.pi * ((n * k) % N) / N))
            waves.append(k)
    table = np.stack(cols, axis=1)
    eigen = -4.0 * np.sin(np.pi * np.array(waves) / N) ** 2
    return table, eigen


def split_np(a):
    a = a.astype(np.float32)
    hi = a.astype(jnp.bfloat16)
    lo = (a - hi.astype(np.float32)).astype(jnp.bfloat16)
    return hi, lo


TABLE, EIGEN = mode_table()
T_EE = TABLE[:256, :256]
T_EO = TABLE[:256, 256:512]
T_OD = TABLE[:512, 512:]


def split(v):
    hi = v.astype(BF16)
    return hi, (v - hi.astype(F32)).astype(BF16)


def dot3(ah, al, bh, bl):
    d = functools.partial(jnp.dot, preferred_element_type=F32)
    return d(ah, bh) + (d(al, bh) + d(ah, bl))


def params(mb, sem=None):
    return pltpu.CompilerParams(vmem_limit_bytes=mb * MIB)


TOKEN = jax.ShapeDtypeStruct((8, 128), F32)
VM = pl.BlockSpec(memory_space=pltpu.VMEM)
SM = pl.BlockSpec(memory_space=pltpu.SMEM)


def pack_kernel(ft, dr, he, ce, od, ids, addr):
    zero = jnp.zeros((32, 32), F32)
    none = jnp.zeros((32, 96), jnp.int32)
    for q in range(4):
        c = slice(q * 32, (q + 1) * 32)
        od[pl.ds(q, 32, stride=4), :] = jnp.concatenate([ft[:, c], dr[:, c], he[:, c], zero], axis=1)
        ids[pl.ds(q, 32, stride=4), :] = jnp.concatenate([ce[:, c], none], axis=1)
    safe = jnp.maximum(ce[...], 0)
    row = safe >> 10
    addr[...] = (row >> 3) * 64 + ((safe >> 7) & 7) * 8 + (row & 7)


def pack_owner(ft, dr, he, ce):
    full = jax.ShapeDtypeStruct((OWNERS, 128), F32)
    return pl.pallas_call(
        pack_kernel, out_shape=(full, jax.ShapeDtypeStruct((OWNERS, 128), jnp.int32),
                                jax.ShapeDtypeStruct((32, 128), jnp.int32)),
        in_specs=[VM] * 4, out_specs=(VM,) * 3, compiler_params=params(58), name="pack_owner",
    )(ft, dr, he, ce)


def load_temp(a_ref, tt):
    def one(i, c):
        for ct in range(8):
            v = a_ref[tile(i, 16), ct * 128:(ct + 1) * 128].astype(F32)
            tt[tile(i * 16 + ct), :] = v[:8]
            tt[tile(i * 16 + 8 + ct), :] = v[8:]
        return c
    lax.fori_loop(0, 64, one, 0)


def gather_rows(addr, src, buf):
    def one(o, c):
        for s in range(SLOT):
            buf[pl.ds(s * OWNERS + o, 1), :] = src[pl.ds(addr[o * SLOT + s], 1), :]
        return c
    lax.fori_loop(0, OWNERS, one, 0)


def hits(ids, s, lane):
    col = ids[:, s:s + 1]
    return lane == jnp.where(col >= 0, col & 127, -1)


def pick(ids, buf):
    lane = lax.broadcasted_iota(jnp.int32, (OWNERS, 128), 1)
    out = jnp.zeros((OWNERS, 128), F32)
    for s in range(SLOT):
        v = jnp.where(hits(ids, s, lane), buf[s * OWNERS:(s + 1) * OWNERS, :], 0.0)
        out = jnp.where(lane == s, jnp.sum(v, axis=1, keepdims=True), out)
    return out


def spread_rows(ids, vals, buf):
    lane = lax.broadcasted_iota(jnp.int32, (OWNERS, 128), 1)
    for s in range(SLOT):
        buf[s * OWNERS:(s + 1) * OWNERS, :] = jnp.where(hits(ids, s, lane), vals[:, s:s + 1], 0.0)


def clear(accs):
    def one(i, c):
        for a in accs:
            for j in range(8):
                a[tile(i * 8 + j), :] = jnp.zeros((8, 128), F32)
        return c
    lax.fori_loop(0, 128, one, 0)


def add_rows(addr, accs, buf):
    width = len(accs)

    def one(o, c):
        for s in range(0, SLOT, 2 * width):
            at = [addr[o * SLOT + s + j] for j in range(2 * width)]
            x = [buf[pl.ds((s + j) * OWNERS + o, 1), :] for j in range(2 * width)]
            old = [accs[j % width][pl.ds(at[j], 1), :] for j in range(2 * width)]
            for j in range(width):
                first = old[j] + x[j]
                second = jnp.where(at[j] == at[j + width], first, old[j + width]) + x[j + width]
                accs[j][pl.ds(at[j], 1), :] = first
                accs[j][pl.ds(at[j + width], 1), :] = second
        return c
    lax.fori_loop(0, OWNERS, one, 0)


def total(accs, rows):
    return (accs[0][rows, :] + accs[1][rows, :]) + (accs[2][rows, :] + accs[3][rows, :])


def gather_kernel(addr, ids_ref, w_ref, wc_ref, buf):
    gather_rows(addr, w_ref, buf)
    wc_ref[...] = pick(ids_ref[...], buf)


def gather_w(addr, ids, w2):
    return pl.pallas_call(
        gather_kernel, out_shape=jax.ShapeDtypeStruct((OWNERS, 128), F32), in_specs=[SM, VM, VM], out_specs=VM,
        scratch_shapes=[pltpu.VMEM((4096, 128), F32)],
        compiler_params=params(VMEM_MIB), name="facet_gather",
    )(addr, ids, w2)


FOUR = [pltpu.VMEM((8192, 128), F32)] * 4 + [pltpu.VMEM((4096, 128), F32)]


def flux_kernel(addr, tok_in, ids_ref, wc_ref, od_ref, a_ref, flux_ref, fl_ref, tok_ref, tt, buf, turned):
    load_temp(a_ref, tt)
    gather_rows(addr, tt, buf)
    tc = pick(ids_ref[...], buf)[:, :SLOT]
    wc = wc_ref[:, :SLOT]
    flux = od_ref[:, 64:96] * jnp.sqrt(wc * wc + 0.25) * (od_ref[:, :32] - tc)
    wide = jnp.concatenate([flux, jnp.zeros((OWNERS, 96), F32)], axis=1)
    flux_ref[...] = wide
    turned[...] = pltpu.roll(wide, (lax.axis_index("py") % 4) * SLOT, 1)
    for j in range(NPY):
        fl_ref[j] = turned[pl.ds(j, 8, stride=16), :]
    tok_ref[...] = tok_in[...]


def heat_flux(addr, tok, ids, wc, od, a2):
    return pl.pallas_call(
        flux_kernel,
        out_shape=(jax.ShapeDtypeStruct((OWNERS, 128), F32), jax.ShapeDtypeStruct((NPY, 8, 128), F32), TOKEN),
        in_specs=[SM] + [VM] * 5, out_specs=(VM,) * 3,
        scratch_shapes=[pltpu.VMEM((8192, 128), F32), pltpu.VMEM((4096, 128), F32), pltpu.VMEM((OWNERS, 128), F32)],
        cost_estimate=pl.CostEstimate(flops=0, bytes_accessed=25 * MIB, transcendentals=0),
        compiler_params=params(30), name="heat_flux",
    )(addr, tok, ids, wc, od, a2)


def theta_kernel(addr, tok_in, ids_ref, flux_ref, a_ref, th_ref, tok_ref, acc0, acc1, acc2, acc3, buf):
    accs = (acc0, acc1, acc2, acc3)
    load_temp(a_ref, acc0)
    clear(accs[1:])
    spread_rows(ids_ref[...], flux_ref[...], buf)
    add_rows(addr, accs, buf)

    def put(i, c):
        for ct in range(8):
            v0 = total(accs, tile(i * 16 + ct))
            v1 = total(accs, tile(i * 16 + 8 + ct))
            th_ref[tile(i, 16), ct * 128:(ct + 1) * 128] = jnp.concatenate([v0, v1], axis=0).astype(BF16)
        return c
    lax.fori_loop(0, 64, put, 0)
    tok_ref[...] = tok_in[...]


def new_theta(addr, tok, ids, flux, a2):
    return pl.pallas_call(
        theta_kernel, out_shape=(jax.ShapeDtypeStruct((1024, 1024), BF16), TOKEN),
        in_specs=[SM] + [VM] * 4, out_specs=(VM, VM), scratch_shapes=FOUR,
        cost_estimate=pl.CostEstimate(flops=0, bytes_accessed=40 * MIB, transcendentals=0),
        compiler_params=params(42), name="new_theta",
    )(addr, tok, ids, flux, a2)


BLK = 2 * ROWS + 2 * LEV
BACK = BLK + 8


def y_basis():
    i = np.arange(ROWS) + 1
    s = math.sqrt(2 / 129) * np.sin(np.pi * (np.outer(i, i) % 258) / 129)
    mu = -4.0 * np.sin(np.pi * i / 258) ** 2
    return s, mu


SINE, MU = y_basis()
EDGE = np.concatenate([TABLE[0::ROWS], TABLE[ROWS - 1::ROWS]])


def pack(transposed):
    parts = [split_np(t.T if transposed else t) for t in (T_EE, T_EO, T_OD)]
    (eh, el), (oh, ol), (dh, dl) = parts
    return np.concatenate([dh, dl, np.concatenate([np.concatenate([eh, oh], 1), np.concatenate([el, ol], 1)])])


TAB, TAB_T = pack(False), pack(True)
SINE2 = np.concatenate(split_np(SINE))
EDGE_F = np.concatenate(split_np(EDGE.T))
EDGE_B = np.concatenate(split_np(EDGE))
LAM_Y = np.broadcast_to(EIGEN.astype(np.float32)[:, None], (N, 128)).copy()
LAMS = np.concatenate([LAM_Y, EIGEN.astype(np.float32).reshape(NPX, 128)])
COLS = np.stack([np.broadcast_to(v[:, None], (ROWS, 128)) for v in (SINE[:, 0], SINE[:, 127])]).astype(np.float32)


def pivots():
    lam = MU[:, None] + EIGEN[None, :]
    c = [1.0 / (1.0 - lam)]
    for _ in range(LEV - 1):
        c.insert(0, 1.0 / (2.0 - lam - c[0]))
    return np.stack(c).astype(np.float32)


PIVOT = pivots()


def tab_parts(t):
    return ((t[1024:1280, :256], t[1280:1536, :256]), (t[1024:1280, 256:], t[1280:1536, 256:]),
            (t[:512], t[512:1024]))


def tile(i, size=8):
    return pl.ds(pl.multiple_of(i * size, size), size)


def fixed(shape):
    return pl.BlockSpec(shape, lambda g: (0,) * len(shape))


def slab_polys(lam):
    phi = [None] * 9
    phi[8] = jnp.ones_like(lam)
    delta = -lam
    phi[7] = phi[8] + delta
    for k in range(6, -1, -1):
        delta = delta - lam * phi[k + 1]
        phi[k] = phi[k + 1] + delta
    theta = [jnp.ones_like(lam), 2.0 - lam]
    for k in range(2, 8):
        theta.append((2.0 - lam) * theta[k - 1] - theta[k - 2])
    return phi, theta, delta


def inverse_of(v):
    r = pl.reciprocal(v, approx=True)
    r = r * (2.0 - v * r)
    return r * (2.0 - v * r)


def x_modes(v, tab):
    s, d = v[:, :512] + v[:, 512:], v[:, :512] - v[:, 512:]
    te, to, td = tab_parts(tab)
    return ((0, dot3(*split(s[:, :256] + s[:, 256:]), *te)), (256, dot3(*split(s[:, :256] - s[:, 256:]), *to)),
            (512, dot3(*split(d), *td)))


STRIP = 32


def fold(v):
    return jnp.sum(v.reshape(STRIP // 8, 8, 128), axis=0)


def eliminate(fs, cs):
    fs = list(fs)
    for k in range(LEV - 2, -1, -1):
        fs[k] = fs[k] + cs[k + 1] * fs[k + 1]
    ps = [cs[0] * fs[0]]
    for k in range(1, LEV):
        ps.append(cs[k] * (fs[k] + ps[k - 1]))
    return ps


def block_forward_kernel(addr, ids_ref, wc_ref, od_ref, w_ref, wn_ref, h_ref, tab, sine, piv, cols,
                         wo_ref, out_ref, r_ref, tok_ref,
                         acc0, acc1, acc2, acc3, buf, wf, r2, hx, a07):
    step = pl.program_id(0)
    sh, sl = sine[:128, :], sine[128:, :]

    accs = (acc0, acc1, acc2, acc3)

    def corrected(src, l, level):
        def put(tr, c):
            for ct in range(8):
                cs = slice(ct * 128, (ct + 1) * 128)
                wf[level, tile(tr), cs] = src[l, tile(tr), cs] + total(accs, tile((level * 16 + tr) * 8 + ct))
            return c
        lax.fori_loop(0, 16, put, 0)

    @pl.when(step == 0)
    def _():
        tok_ref[...] = jnp.zeros((8, 128), F32)
        clear(accs)
        wc = wc_ref[:, :SLOT]
        stress = od_ref[:, 32:64] * jnp.sqrt(wc * wc + 0.25) * wc
        spread_rows(ids_ref[...], -stress, buf)
        add_rows(addr, accs, buf)
        corrected(w_ref, 0, 0)
        lifted = (lax.axis_index("py") > 0).astype(F32)
        for c0, res in x_modes(wf[0] * lifted, tab):
            for b in range(res.shape[1] // 128):
                hx[c0 // 128 + b] = res[:, b * 128:(b + 1) * 128]

    @pl.when((step > 0) & (step < 5))
    def _():
        lv = 2 * step - 2
        corrected(w_ref, 1, lv + 1)

        @pl.when(step < 4)
        def _():
            corrected(wn_ref, 0, lv + 2)
        w0, w1 = wf[lv], wf[lv + 1]
        wo_ref[0] = w0
        wo_ref[1] = w1
        up = jnp.where(step == 4, 0.0, wf[jnp.minimum(lv + 2, LEV - 1)])
        r = jnp.concatenate([h_ref[0] + w1 - w0, h_ref[1] + up - w1], axis=0)
        for c0, res in x_modes(r, tab):
            for l in range(2):
                v = dot3(sh, sl, *split(res[l * 128:(l + 1) * 128]))
                for b in range(res.shape[1] // 128):
                    r2[c0 // 128 + b, lv + l] = v[:, b * 128:(b + 1) * 128]

    @pl.when(step >= 5)
    def _():
        lt = step - 5

        def inner(bt, acc):
            rows = tile(bt, STRIP)
            rs = [r2[lt, k, rows, :] for k in range(LEV)]
            for k in range(LEV):
                r_ref[k, rows, :] = rs[k]
            ps = eliminate(rs, [piv[k, rows, :] for k in range(LEV)])
            s0, s1 = cols[0, rows, :], cols[1, rows, :]
            a07[rows, :128] = ps[0]
            a07[rows, 128:] = ps[7]
            return tuple(acc[k] + fold(s0 * ps[k]) for k in range(LEV)) + tuple(
                acc[LEV + k] + fold(s1 * ps[k]) for k in range(LEV))
        acc = lax.fori_loop(0, ROWS // STRIP, inner, tuple(jnp.zeros((8, 128), F32) for _ in range(16)))
        for e in range(2):
            sums = [jnp.sum(acc[e * LEV + k], axis=0, keepdims=True) for k in range(LEV)]
            out_ref[0, 2 * ROWS + e * LEV:2 * ROWS + (e + 1) * LEV, :] = -jnp.concatenate(sums, axis=0)
        res = dot3(sh, sl, *split(a07[...]))
        out_ref[0, :ROWS, :] = -res[:, :128] - hx[lt]
        out_ref[0, ROWS:2 * ROWS, :] = -res[:, 128:]


def block_forward(addr, ids, wc, od, w, h):
    two = pl.BlockSpec((2, ROWS, N), lambda g: (jnp.clip(g - 1, 0, 3), 0, 0))
    col = pl.BlockSpec((LEV, ROWS, 128), lambda g: (0, 0, jnp.maximum(g - 5, 0)))
    small = fixed((OWNERS, 128))
    big = jax.ShapeDtypeStruct((LEV, ROWS, N), F32)
    return pl.pallas_call(
        block_forward_kernel, grid=(5 + NPX,),
        out_shape=(big, jax.ShapeDtypeStruct((NPX, BLK, 128), F32), big, TOKEN),
        in_specs=[SM, small, small, small, two,
                  pl.BlockSpec((1, ROWS, N), lambda g: (jnp.clip(2 * g, 2, 7), 0, 0)), two, fixed((1536, 512)),
                  fixed((256, 128)), col, fixed((2, ROWS, 128))],
        out_specs=(two, pl.BlockSpec((1, BLK, 128), lambda g: (jnp.maximum(g - 5, 0), 0, 0)), col, fixed((8, 128))),
        scratch_shapes=FOUR + [pltpu.VMEM((LEV, ROWS, N), F32), pltpu.VMEM((NPX, LEV, ROWS, 128), F32),
                               pltpu.VMEM((NPX, ROWS, 128), F32), pltpu.VMEM((ROWS, 256), F32)],
        compiler_params=params(VMEM_MIB), name="block_forward",
    )(addr, ids, wc, od, w, w, h, jnp.asarray(TAB), jnp.asarray(SINE2), jnp.asarray(PIVOT), jnp.asarray(COLS))


def lam_row(ly):
    return ly[pl.ds(N + lax.axis_index("px"), 1), :]


def edge_rows(x_ref, sr):
    for i in range(NPX):
        for k in range(LEV):
            cs = slice(k * 128, (k + 1) * 128)
            sr[i:i + 1, cs] = x_ref[(i + 7) % 8, 2 * ROWS + LEV + k:2 * ROWS + LEV + k + 1, :]
            sr[8 + i:9 + i, cs] = x_ref[(i + 1) % 8, 2 * ROWS + k:2 * ROWS + k + 1, :]
    return split(sr[...])


def edge_modes(edge, t, sh, sl):
    return dot3(edge[tile(t, 128), :], edge[pl.ds(pl.multiple_of(N + t * 128, 128), 128), :], sh, sl)


def y_forward_kernel(x_ref, tok, ly, tab, edge, al_ref, pp, sr, st):
    x = jnp.concatenate([x_ref[:, :ROWS], x_ref[:, ROWS:2 * ROWS]], axis=-1).reshape(N, 256)
    s, d = x[:512] + x[512:], x[:512] - x[512:]
    ee, eo = s[:256] + s[256:], s[:256] - s[256:]
    te, to, td = tab_parts(tab)
    for v, t, k0 in ((ee, te, 0), (eo, to, 256), (d, td, 512)):
        res = dot3(*t, *split(v))
        pp[k0:k0 + res.shape[0], :] = res
    sh, sl = edge_rows(x_ref, sr)
    lam_x = lam_row(ly)

    def some(t, c):
        st[...] = edge_modes(edge, t, sh, sl)
        for q in range(8):
            part = slice(q * 16, (q + 1) * 16)
            rows = pl.ds(pl.multiple_of(t * 128 + q * 16, 16), 16)
            phi, theta, _ = slab_polys(ly[rows, :] + lam_x)
            inv = inverse_of(phi[0])
            b0 = b7 = None
            for k in range(LEV):
                sk = st[part, k * 128:(k + 1) * 128]
                b0 = phi[k + 1] * sk if k == 0 else b0 + phi[k + 1] * sk
                b7 = sk if k == 0 else b7 + theta[k] * sk
            j, at = 2 * t + q // 4, (q % 4) * 16
            al_ref[j, at:at + 16, :] = pp[rows, :128] + b0 * inv
            al_ref[j, 64 + at:80 + at, :] = pp[rows, 128:] + b7 * inv
        return c
    lax.fori_loop(0, 8, some, 0)


def y_forward(x, tok):
    return pl.pallas_call(
        y_forward_kernel, grid=(1,),
        out_shape=jax.ShapeDtypeStruct((NPY, 128, 128), F32),
        in_specs=[fixed((NPX, BLK, 128)), fixed((8, 128)), fixed((N + NPX, 128)), fixed((1536, 512)),
                  fixed((2 * N, 16))],
        out_specs=fixed((NPY, 128, 128)),
        scratch_shapes=[pltpu.VMEM((N, 256), F32), pltpu.VMEM((16, N), F32), pltpu.VMEM((128, N), F32)],
        compiler_params=params(VMEM_MIB), name="y_forward",
    )(x, tok, jnp.asarray(LAMS), jnp.asarray(TAB_T), jnp.asarray(EDGE_F))


def ladder_kernel(al_ref, ly, fl_ref, out_ref):
    for j in range(NPY):
        out_ref[j, 128:, :] = fl_ref[j]

    lam_x = lam_row(ly)
    mine = lax.axis_index("py") * 64
    for t in range(8):
        rows, tops = slice(t * 8, (t + 1) * 8), slice(64 + t * 8, 72 + t * 8)
        phi, theta, delta = slab_polys(ly[pl.ds(pl.multiple_of(mine + t * 8, 8), 8), :] + lam_x)
        inv = 1.0 / phi[0]
        n07, n77, cc = inv, theta[7] * inv, delta * inv
        A = [None] * 17
        B = [None] * 17
        e = [None] * 17
        A[16] = jnp.zeros_like(inv)
        B[16] = jnp.full_like(inv, -2.0)
        for j in range(15, -1, -1):
            g, q = al_ref[j, rows, :], al_ref[j, tops, :]
            e[j + 1] = inverse_of(1.0 - n77 * B[j + 1])
            be = B[j + 1] * e[j + 1]
            A[j] = g + n07 * (A[j + 1] + be * (q + n77 * A[j + 1]))
            B[j] = n07 * n07 * be - cc
        p = -A[0] / B[0]
        for j in range(16):
            out_ref[j, rows, :] = p
            p = (al_ref[j, tops, :] + n77 * A[j + 1] + n07 * p) * e[j + 1]
            out_ref[j, tops, :] = A[j + 1] + B[j + 1] * p


def ladder(al, fl):
    return pl.pallas_call(
        ladder_kernel, grid=(1,), out_shape=jax.ShapeDtypeStruct((NPY, 136, 128), F32),
        in_specs=[fixed((NPY, 128, 128)), fixed((N + NPX, 128)), fixed((NPY, 8, 128))],
        out_specs=fixed((NPY, 136, 128)), compiler_params=params(VMEM_MIB), name="ladder",
    )(al, jnp.asarray(LAMS), fl)


def y_inverse_kernel(x_ref, pu_ref, ly, tab, edge_f, edge_b, out_ref, tok_ref, sr, st, ph, pl_):
    tok_ref[...] = jnp.zeros((8, 128), F32)
    sh, sl = edge_rows(x_ref, sr)
    lam_x = lam_row(ly)

    def some(t, c):
        st[...] = edge_modes(edge_f, t, sh, sl)
        for q in range(8):
            part = slice(q * 16, (q + 1) * 16)
            rows = pl.ds(pl.multiple_of(t * 128 + q * 16, 16), 16)
            j, at = 2 * t + q // 4, (q % 4) * 16
            low, top = pu_ref[j, at:at + 16, :], pu_ref[j, 64 + at:80 + at, :]
            lam = ly[rows, :] + lam_x
            cs = [None] * 8
            fs = [None] * 8
            cs[7] = inverse_of(1.0 - lam)
            fs[7] = st[part, 7 * 128:] + top
            for k in range(6, -1, -1):
                cs[k] = inverse_of(2.0 - lam - cs[k + 1])
                fs[k] = st[part, k * 128:(k + 1) * 128] + cs[k + 1] * fs[k + 1]
            prev = low
            for k in range(8):
                prev = cs[k] * (fs[k] + prev)
                ph[rows, k * 128:(k + 1) * 128], pl_[rows, k * 128:(k + 1) * 128] = split(prev)
        return c
    lax.fori_loop(0, 8, some, 0)
    edges = dot3(edge_b[:16, :], edge_b[16:, :], ph[...], pl_[...])
    for i in range(NPX):
        below, above = (i + 7) % 8, (i + 1) % 8
        for k in range(LEV):
            cols = slice(k * 128, (k + 1) * 128)
            lo = 2 * ROWS + k
            hi = 2 * ROWS + LEV + k
            out_ref[i, lo:lo + 1, :] = edges[8 + below:9 + below, cols] + x_ref[below, hi:hi + 1, :]
            out_ref[i, hi:hi + 1, :] = edges[above:above + 1, cols] + x_ref[above, lo:lo + 1, :]
    for q in range(4):
        flux = (pu_ref[4 * q, 128:, :] + pu_ref[4 * q + 1, 128:, :]) + (
            pu_ref[4 * q + 2, 128:, :] + pu_ref[4 * q + 3, 128:, :])
        for i in range(NPX):
            out_ref[i, BLK + q:BLK + q + 1, :] = flux[i:i + 1, :]
            out_ref[i, BLK + 4 + q:BLK + 5 + q, :] = jnp.zeros((1, 128), F32)
    pu = jnp.concatenate([pu_ref[:, :64], pu_ref[:, 64:128]], axis=-1).reshape(N, 256)
    te, to, td = tab_parts(tab)
    t0 = dot3(*te, *split(pu[:256]))
    t1 = dot3(*to, *split(pu[256:512]))
    d = dot3(*td, *split(pu[512:]))
    ev = (t0 + t1, t0 - t1)
    for i in range(4):
        base = ev[i // 2][(i % 2) * 128:(i % 2 + 1) * 128]
        odd = d[i * 128:(i + 1) * 128]
        for l in range(2):
            cols = slice(l * 128, (l + 1) * 128)
            out_ref[i, l * ROWS:(l + 1) * ROWS, :] = base[:, cols] + odd[:, cols]
            out_ref[i + 4, l * ROWS:(l + 1) * ROWS, :] = base[:, cols] - odd[:, cols]


def y_inverse(x, pu):
    return pl.pallas_call(
        y_inverse_kernel, grid=(1,), out_shape=(jax.ShapeDtypeStruct((NPX, BACK, 128), F32), TOKEN),
        in_specs=[fixed((NPX, BLK, 128)), fixed((NPY, 136, 128)), fixed((N + NPX, 128)), fixed((1536, 512)),
                  fixed((2 * N, 16)), fixed((32, N))],
        out_specs=(fixed((NPX, BACK, 128)), fixed((8, 128))),
        scratch_shapes=[pltpu.VMEM((16, N), F32), pltpu.VMEM((128, N), F32),
                        pltpu.VMEM((N, N), BF16), pltpu.VMEM((N, N), BF16)],
        compiler_params=params(VMEM_MIB), name="y_inverse",
    )(x, pu, jnp.asarray(LAMS), jnp.asarray(TAB), jnp.asarray(EDGE_F), jnp.asarray(EDGE_B))


def block_inverse_kernel(y_ref, g_ref, w_ref, roof_ref, tab, sine, piv, cols, ft, nr, hc, tok,
                         out_ref, nt_ref, field, wv, spu, fb):
    step = pl.program_id(0)
    sh, sl = sine[:128, :], sine[128:, :]

    @pl.when(step < NPX)
    def _():
        fb[step] = y_ref[0, BLK:, :]
        spu[...] = dot3(sh, sl, *split(jnp.concatenate([y_ref[0, :ROWS, :], y_ref[0, ROWS:2 * ROWS, :]], axis=1)))
        edge = [y_ref[0, 2 * ROWS + k:2 * ROWS + k + 1, :] for k in range(2 * LEV)]

        def inner(bt, c):
            rows = tile(bt, STRIP)
            s0, s1 = cols[0, rows, :], cols[1, rows, :]
            low, top = spu[rows, :128], spu[rows, 128:]
            fs = [s0 * edge[k] + s1 * edge[LEV + k] - g_ref[k, rows, :] for k in range(LEV)]
            fs[0] = fs[0] + low
            fs[7] = fs[7] + top
            prev = low
            for k, p in enumerate(eliminate(fs, [piv[k, rows, :] for k in range(LEV)])):
                wv[rows, k * 128:(k + 1) * 128] = p - prev
                prev = p
            return c
        lax.fori_loop(0, ROWS // STRIP, inner, 0)
        res = dot3(sh, sl, *split(wv[...]))
        for k in range(LEV):
            field[k, :, tile(step, 128)] = res[:, k * 128:(k + 1) * 128]

    @pl.when(step >= NPX)
    def _():
        pair = step - NPX
        v = jnp.concatenate([field[2 * pair], field[2 * pair + 1]], axis=0)
        te, to, td = tab_parts(tab)
        t0 = dot3(*split(v[:, :256]), *te)
        t1 = dot3(*split(v[:, 256:512]), *to)
        d = dot3(*split(v[:, 512:]), *td)
        s = jnp.concatenate([t0 + t1, t0 - t1], axis=1)
        for half, res in ((0, s + d), (1, s - d)):
            cs = slice(half * 512, (half + 1) * 512)
            for l in range(2):
                solid = lax.axis_index("py") * LEV + 2 * pair + l < roof_ref[:, cs]
                out_ref[l, :, cs] = jnp.where(solid, 0.0, w_ref[l, :, cs] - res[l * 128:(l + 1) * 128])

    @pl.when(step == NPX + 3)
    def _():
        flux = jnp.concatenate([fb[i, :4, :] for i in range(NPX)], axis=0)
        nt_ref[...] = ft[...] + (nr[...] - flux - 0.5 * ft[...]) / hc[...]


def block_inverse(y, g, w, roof, ft, nr, hc, tok):
    late = pl.BlockSpec((2, ROWS, N), lambda t: (jnp.maximum(t - NPX, 0), 0, 0))
    return pl.pallas_call(
        block_inverse_kernel, grid=(NPX + 4,),
        out_shape=(jax.ShapeDtypeStruct((LEV, ROWS, N), F32), jax.ShapeDtypeStruct((32, 128), F32)),
        in_specs=[pl.BlockSpec((1, BACK, 128), lambda t: (jnp.minimum(t, NPX - 1), 0, 0)),
                  pl.BlockSpec((LEV, ROWS, 128), lambda t: (0, 0, jnp.minimum(t, NPX - 1))),
                  late, fixed((ROWS, N)), fixed((1536, 512)), fixed((256, 128)),
                  pl.BlockSpec((LEV, ROWS, 128), lambda t: (0, 0, jnp.minimum(t, NPX - 1))), fixed((2, ROWS, 128)),
                  fixed((32, 128)), fixed((32, 128)), fixed((32, 128)), fixed((8, 128))],
        out_specs=(late, fixed((32, 128))),
        scratch_shapes=[pltpu.VMEM((LEV, ROWS, N), F32), pltpu.VMEM((ROWS, N), F32), pltpu.VMEM((ROWS, 256), F32),
                        pltpu.VMEM((NPX, 8, 128), F32)],
        compiler_params=params(VMEM_MIB), name="block_inverse",
    )(y, g, w, roof, jnp.asarray(TAB_T), jnp.asarray(SINE2), jnp.asarray(PIVOT), jnp.asarray(COLS), ft, nr, hc, tok)


def swap(x, axes):
    return lax.all_to_all(x, axes, split_axis=0, concat_axis=0, tiled=True)


def body(horiz_div, w_star, air_temp, roof_level, facet_cells, facet_temp, net_radiation,
         heat_capacity, drag_coef, heat_coef):
    ft, nr, hc, dr, he, ce = [
        v.reshape(32, 128) for v in (facet_temp, net_radiation, heat_capacity, drag_coef, heat_coef, facet_cells)]
    owner, ids, addr = pack_owner(ft, dr, he, ce)
    od = swap(owner.reshape(OWNERS, 1, 128), ("px", "py")).reshape(OWNERS, 128)
    addr = addr.reshape(OWNERS * SLOT)
    w2, a2 = w_star.reshape(1024, 1024), air_temp.reshape(1024, 1024)
    tiles = w2.reshape(128, 8, 8, 128).transpose(0, 2, 1, 3).reshape(8192, 128)
    wc = gather_w(addr, ids, tiles)
    w_corr, sent, g, tok = block_forward(addr, ids, wc, od, w_star, horiz_div)
    xs = swap(sent, "px")
    flux, fl, tok = heat_flux(addr, tok, ids, wc, od, a2)
    pu = swap(ladder(swap(y_forward(xs, tok), "py"), fl), "py")
    back, tok = y_inverse(xs, pu)
    ys = swap(back, "px")
    theta, tok = new_theta(addr, tok, ids, flux, a2)
    w_new, temp_new = block_inverse(ys, g, w_corr, roof_level, ft, nr, hc, tok)
    return w_new, theta.reshape(LEV, ROWS, N), temp_new.reshape(1, OWNERS * SLOT)


def solution(mesh):
    field, facet = P("py", "px", None), P(("px", "py"), None)
    return jax.shard_map(
        body, mesh=mesh,
        in_specs=(field, field, field, P("px", None)) + (facet,) * 6,
        out_specs=(field, field, facet), check_vma=False)
```

```python
import functools
import math

import jax
import jax.numpy as jnp
import numpy as np
from jax import lax
from jax.experimental import pallas as pl
from jax.experimental.pallas import tpu as pltpu
from jax.sharding import PartitionSpec as P

N = 1024
NPX, NPY = 8, 16
LEV, ROWS = 8, 128
OWNERS, SLOT = 128, 32
MIB = 1 << 20
VMEM_MIB = 50
F32, BF16 = jnp.float32, jnp.bfloat16


def mode_table():
    classes = [np.arange(0, 513, 4), np.arange(2, 513, 4), np.arange(1, 512, 2)]
    n = np.arange(N)
    cols, waves = [], []
    for ks in classes:
        for k in ks:
            edge = k == 0 or k == N // 2
            norm = math.sqrt((1.0 if edge else 2.0) / N)
            cols.append(norm * np.cos(2 * np.pi * ((n * k) % N) / N))
            waves.append(k)
        for k in ks:
            if k == 0 or k == N // 2:
                continue
            cols.append(math.sqrt(2.0 / N) * np.sin(2 * np.pi * ((n * k) % N) / N))
            waves.append(k)
    table = np.stack(cols, axis=1)
    eigen = -4.0 * np.sin(np.pi * np.array(waves) / N) ** 2
    return table, eigen


def split_np(a):
    a = a.astype(np.float32)
    hi = a.astype(jnp.bfloat16)
    lo = (a - hi.astype(np.float32)).astype(jnp.bfloat16)
    return hi, lo


TABLE, EIGEN = mode_table()
T_EE = TABLE[:256, :256]
T_EO = TABLE[:256, 256:512]
T_OD = TABLE[:512, 512:]


def split(v):
    hi = v.astype(BF16)
    return hi, (v - hi.astype(F32)).astype(BF16)


def dot3(ah, al, bh, bl):
    d = functools.partial(jnp.dot, preferred_element_type=F32)
    return d(ah, bh) + (d(al, bh) + d(ah, bl))


def params(mb, sem=None):
    return pltpu.CompilerParams(vmem_limit_bytes=mb * MIB)


TOKEN = jax.ShapeDtypeStruct((8, 128), F32)
VM = pl.BlockSpec(memory_space=pltpu.VMEM)
SM = pl.BlockSpec(memory_space=pltpu.SMEM)


def pack_kernel(ft, dr, he, ce, od, ids, addr):
    zero = jnp.zeros((32, 32), F32)
    none = jnp.zeros((32, 96), jnp.int32)
    for q in range(4):
        c = slice(q * 32, (q + 1) * 32)
        od[pl.ds(q, 32, stride=4), :] = jnp.concatenate([ft[:, c], dr[:, c], he[:, c], zero], axis=1)
        ids[pl.ds(q, 32, stride=4), :] = jnp.concatenate([ce[:, c], none], axis=1)
    safe = jnp.maximum(ce[...], 0)
    row = safe >> 10
    addr[...] = (row >> 3) * 64 + ((safe >> 7) & 7) * 8 + (row & 7)


def pack_owner(ft, dr, he, ce):
    full = jax.ShapeDtypeStruct((OWNERS, 128), F32)
    return pl.pallas_call(
        pack_kernel, out_shape=(full, jax.ShapeDtypeStruct((OWNERS, 128), jnp.int32),
                                jax.ShapeDtypeStruct((32, 128), jnp.int32)),
        in_specs=[VM] * 4, out_specs=(VM,) * 3, compiler_params=params(58), name="pack_owner",
    )(ft, dr, he, ce)


def load_temp(a_ref, tt):
    def one(i, c):
        for ct in range(8):
            v = a_ref[tile(i, 16), ct * 128:(ct + 1) * 128].astype(F32)
            tt[tile(i * 16 + ct), :] = v[:8]
            tt[tile(i * 16 + 8 + ct), :] = v[8:]
        return c
    lax.fori_loop(0, 64, one, 0)


def gather_rows(addr, src, buf):
    def one(o, c):
        for s in range(SLOT):
            buf[pl.ds(s * OWNERS + o, 1), :] = src[pl.ds(addr[o * SLOT + s], 1), :]
        return c
    lax.fori_loop(0, OWNERS, one, 0)


def hits(ids, s, lane):
    col = ids[:, s:s + 1]
    return lane == jnp.where(col >= 0, col & 127, -1)


def pick(ids, buf):
    lane = lax.broadcasted_iota(jnp.int32, (OWNERS, 128), 1)
    out = jnp.zeros((OWNERS, 128), F32)
    for s in range(SLOT):
        v = jnp.where(hits(ids, s, lane), buf[s * OWNERS:(s + 1) * OWNERS, :], 0.0)
        out = jnp.where(lane == s, jnp.sum(v, axis=1, keepdims=True), out)
    return out


def spread_rows(ids, vals, buf):
    lane = lax.broadcasted_iota(jnp.int32, (OWNERS, 128), 1)
    for s in range(SLOT):
        buf[s * OWNERS:(s + 1) * OWNERS, :] = jnp.where(hits(ids, s, lane), vals[:, s:s + 1], 0.0)


def clear(accs):
    def one(i, c):
        for a in accs:
            for j in range(8):
                a[tile(i * 8 + j), :] = jnp.zeros((8, 128), F32)
        return c
    lax.fori_loop(0, 128, one, 0)


def add_rows(addr, accs, buf):
    width = len(accs)

    def one(o, c):
        for s in range(0, SLOT, 2 * width):
            at = [addr[o * SLOT + s + j] for j in range(2 * width)]
            x = [buf[pl.ds((s + j) * OWNERS + o, 1), :] for j in range(2 * width)]
            old = [accs[j % width][pl.ds(at[j], 1), :] for j in range(2 * width)]
            for j in range(width):
                first = old[j] + x[j]
                second = jnp.where(at[j] == at[j + width], first, old[j + width]) + x[j + width]
                accs[j][pl.ds(at[j], 1), :] = first
                accs[j][pl.ds(at[j + width], 1), :] = second
        return c
    lax.fori_loop(0, OWNERS, one, 0)


def total(accs, rows):
    return (accs[0][rows, :] + accs[1][rows, :]) + (accs[2][rows, :] + accs[3][rows, :])


def gather_kernel(addr, ids_ref, w_ref, wc_ref, buf):
    gather_rows(addr, w_ref, buf)
    wc_ref[...] = pick(ids_ref[...], buf)


def gather_w(addr, ids, w2):
    return pl.pallas_call(
        gather_kernel, out_shape=jax.ShapeDtypeStruct((OWNERS, 128), F32), in_specs=[SM, VM, VM], out_specs=VM,
        scratch_shapes=[pltpu.VMEM((4096, 128), F32)],
        compiler_params=params(VMEM_MIB), name="facet_gather",
    )(addr, ids, w2)


FOUR = [pltpu.VMEM((8192, 128), F32)] * 4 + [pltpu.VMEM((4096, 128), F32)]


def flux_kernel(addr, tok_in, ids_ref, wc_ref, od_ref, a_ref, flux_ref, fl_ref, tok_ref, tt, buf, turned):
    load_temp(a_ref, tt)
    gather_rows(addr, tt, buf)
    tc = pick(ids_ref[...], buf)[:, :SLOT]
    wc = wc_ref[:, :SLOT]
    flux = od_ref[:, 64:96] * jnp.sqrt(wc * wc + 0.25) * (od_ref[:, :32] - tc)
    wide = jnp.concatenate([flux, jnp.zeros((OWNERS, 96), F32)], axis=1)
    flux_ref[...] = wide
    turned[...] = pltpu.roll(wide, (lax.axis_index("py") % 4) * SLOT, 1)
    for j in range(NPY):
        fl_ref[j] = turned[pl.ds(j, 8, stride=16), :]
    tok_ref[...] = tok_in[...]


def heat_flux(addr, tok, ids, wc, od, a2):
    return pl.pallas_call(
        flux_kernel,
        out_shape=(jax.ShapeDtypeStruct((OWNERS, 128), F32), jax.ShapeDtypeStruct((NPY, 8, 128), F32), TOKEN),
        in_specs=[SM] + [VM] * 5, out_specs=(VM,) * 3,
        scratch_shapes=[pltpu.VMEM((8192, 128), F32), pltpu.VMEM((4096, 128), F32), pltpu.VMEM((OWNERS, 128), F32)],
        cost_estimate=pl.CostEstimate(flops=0, bytes_accessed=25 * MIB, transcendentals=0),
        compiler_params=params(30), name="heat_flux",
    )(addr, tok, ids, wc, od, a2)


def theta_kernel(addr, tok_in, ids_ref, flux_ref, a_ref, th_ref, tok_ref, acc0, acc1, acc2, acc3, buf):
    accs = (acc0, acc1, acc2, acc3)
    load_temp(a_ref, acc0)
    clear(accs[1:])
    spread_rows(ids_ref[...], flux_ref[...], buf)
    add_rows(addr, accs, buf)

    def put(i, c):
        for ct in range(8):
            v0 = total(accs, tile(i * 16 + ct))
            v1 = total(accs, tile(i * 16 + 8 + ct))
            th_ref[tile(i, 16), ct * 128:(ct + 1) * 128] = jnp.concatenate([v0, v1], axis=0).astype(BF16)
        return c
    lax.fori_loop(0, 64, put, 0)
    tok_ref[...] = tok_in[...]


def new_theta(addr, tok, ids, flux, a2):
    return pl.pallas_call(
        theta_kernel, out_shape=(jax.ShapeDtypeStruct((1024, 1024), BF16), TOKEN),
        in_specs=[SM] + [VM] * 4, out_specs=(VM, VM), scratch_shapes=FOUR,
        cost_estimate=pl.CostEstimate(flops=0, bytes_accessed=40 * MIB, transcendentals=0),
        compiler_params=params(42), name="new_theta",
    )(addr, tok, ids, flux, a2)


BLK = 2 * ROWS + 2 * LEV
BACK = BLK + 8


def y_basis():
    i = np.arange(ROWS) + 1
    s = math.sqrt(2 / 129) * np.sin(np.pi * (np.outer(i, i) % 258) / 129)
    mu = -4.0 * np.sin(np.pi * i / 258) ** 2
    return s, mu


SINE, MU = y_basis()
EDGE = np.concatenate([TABLE[0::ROWS], TABLE[ROWS - 1::ROWS]])


def pack(transposed):
    parts = [split_np(t.T if transposed else t) for t in (T_EE, T_EO, T_OD)]
    (eh, el), (oh, ol), (dh, dl) = parts
    return np.concatenate([dh, dl, np.concatenate([np.concatenate([eh, oh], 1), np.concatenate([el, ol], 1)])])


TAB, TAB_T = pack(False), pack(True)
SINE2 = np.concatenate(split_np(SINE))
EDGE_F = np.concatenate(split_np(EDGE.T))
EDGE_B = np.concatenate(split_np(EDGE))
LAM_Y = np.broadcast_to(EIGEN.astype(np.float32)[:, None], (N, 128)).copy()
LAMS = np.concatenate([LAM_Y, EIGEN.astype(np.float32).reshape(NPX, 128)])
COLS = np.stack([np.broadcast_to(v[:, None], (ROWS, 128)) for v in (SINE[:, 0], SINE[:, 127])]).astype(np.float32)


def pivots():
    lam = MU[:, None] + EIGEN[None, :]
    c = [1.0 / (1.0 - lam)]
    for _ in range(LEV - 1):
        c.insert(0, 1.0 / (2.0 - lam - c[0]))
    return np.stack(c).astype(np.float32)


PIVOT = pivots()


def tab_parts(t):
    return ((t[1024:1280, :256], t[1280:1536, :256]), (t[1024:1280, 256:], t[1280:1536, 256:]),
            (t[:512], t[512:1024]))


def tile(i, size=8):
    return pl.ds(pl.multiple_of(i * size, size), size)


def fixed(shape):
    return pl.BlockSpec(shape, lambda g: (0,) * len(shape))


def slab_polys(lam):
    phi = [None] * 9
    phi[8] = jnp.ones_like(lam)
    delta = -lam
    phi[7] = phi[8] + delta
    for k in range(6, -1, -1):
        delta = delta - lam * phi[k + 1]
        phi[k] = phi[k + 1] + delta
    theta = [jnp.ones_like(lam), 2.0 - lam]
    for k in range(2, 8):
        theta.append((2.0 - lam) * theta[k - 1] - theta[k - 2])
    return phi, theta, delta


def inverse_of(v):
    r = pl.reciprocal(v, approx=True)
    r = r * (2.0 - v * r)
    return r * (2.0 - v * r)


def x_modes(v, tab):
    s, d = v[:, :512] + v[:, 512:], v[:, :512] - v[:, 512:]
    te, to, td = tab_parts(tab)
    return ((0, dot3(*split(s[:, :256] + s[:, 256:]), *te)), (256, dot3(*split(s[:, :256] - s[:, 256:]), *to)),
            (512, dot3(*split(d), *td)))


STRIP = 32


def fold(v):
    return jnp.sum(v.reshape(STRIP // 8, 8, 128), axis=0)


def eliminate(fs, cs):
    fs = list(fs)
    for k in range(LEV - 2, -1, -1):
        fs[k] = fs[k] + cs[k + 1] * fs[k + 1]
    ps = [cs[0] * fs[0]]
    for k in range(1, LEV):
        ps.append(cs[k] * (fs[k] + ps[k - 1]))
    return ps


def block_forward_kernel(addr, ids_ref, wc_ref, od_ref, w_ref, wn_ref, h_ref, tab, sine, piv, cols,
                         wo_ref, out_ref, r_ref, tok_ref,
                         acc0, acc1, acc2, acc3, buf, wf, r2, hx, a07):
    step = pl.program_id(0)
    sh, sl = sine[:128, :], sine[128:, :]

    accs = (acc0, acc1, acc2, acc3)

    def corrected(src, l, level):
        def put(tr, c):
            for ct in range(8):
                cs = slice(ct * 128, (ct + 1) * 128)
                wf[level, tile(tr), cs] = src[l, tile(tr), cs] + total(accs, tile((level * 16 + tr) * 8 + ct))
            return c
        lax.fori_loop(0, 16, put, 0)

    @pl.when(step == 0)
    def _():
        tok_ref[...] = jnp.zeros((8, 128), F32)
        clear(accs)
        wc = wc_ref[:, :SLOT]
        stress = od_ref[:, 32:64] * jnp.sqrt(wc * wc + 0.25) * wc
        spread_rows(ids_ref[...], -stress, buf)
        add_rows(addr, accs, buf)
        corrected(w_ref, 0, 0)
        lifted = (lax.axis_index("py") > 0).astype(F32)
        for c0, res in x_modes(wf[0] * lifted, tab):
            for b in range(res.shape[1] // 128):
                hx[c0 // 128 + b] = res[:, b * 128:(b + 1) * 128]

    @pl.when((step > 0) & (step < 5))
    def _():
        lv = 2 * step - 2
        corrected(w_ref, 1, lv + 1)

        @pl.when(step < 4)
        def _():
            corrected(wn_ref, 0, lv + 2)
        w0, w1 = wf[lv], wf[lv + 1]
        wo_ref[0] = w0
        wo_ref[1] = w1
        up = jnp.where(step == 4, 0.0, wf[jnp.minimum(lv + 2, LEV - 1)])
        r = jnp.concatenate([h_ref[0] + w1 - w0, h_ref[1] + up - w1], axis=0)
        for c0, res in x_modes(r, tab):
            for l in range(2):
                v = dot3(sh, sl, *split(res[l * 128:(l + 1) * 128]))
                for b in range(res.shape[1] // 128):
                    r2[c0 // 128 + b, lv + l] = v[:, b * 128:(b + 1) * 128]

    @pl.when(step >= 5)
    def _():
        for sub in range(2):
            lt = 2 * (step - 5) + sub
            ln = slice(sub * 128, (sub + 1) * 128)

            def inner(bt, acc):
                rows = tile(bt, STRIP)
                rs = [r2[lt, k, rows, :] for k in range(LEV)]
                for k in range(LEV):
                    r_ref[k, rows, ln] = rs[k]
                ps = eliminate(rs, [piv[k, rows, ln] for k in range(LEV)])
                s0, s1 = cols[0, rows, :], cols[1, rows, :]
                a07[rows, sub * 256:sub * 256 + 128] = ps[0]
                a07[rows, sub * 256 + 128:(sub + 1) * 256] = ps[7]
                return tuple(acc[k] + fold(s0 * ps[k]) for k in range(LEV)) + tuple(
                    acc[LEV + k] + fold(s1 * ps[k]) for k in range(LEV))
            acc = lax.fori_loop(0, ROWS // STRIP, inner, tuple(jnp.zeros((8, 128), F32) for _ in range(16)))
            for e in range(2):
                sums = [jnp.sum(acc[e * LEV + k], axis=0, keepdims=True) for k in range(LEV)]
                out_ref[sub, 2 * ROWS + e * LEV:2 * ROWS + (e + 1) * LEV, :] = -jnp.concatenate(sums, axis=0)
        res = dot3(sh, sl, *split(a07[...]))
        for sub in range(2):
            out_ref[sub, :ROWS, :] = -res[:, sub * 256:sub * 256 + 128] - hx[2 * (step - 5) + sub]
            out_ref[sub, ROWS:2 * ROWS, :] = -res[:, sub * 256 + 128:(sub + 1) * 256]


def block_forward(addr, ids, wc, od, w, h):
    two = pl.BlockSpec((2, ROWS, N), lambda g: (jnp.clip(g - 1, 0, 3), 0, 0))
    col = pl.BlockSpec((LEV, ROWS, 256), lambda g: (0, 0, jnp.maximum(g - 5, 0)))
    small = fixed((OWNERS, 128))
    big = jax.ShapeDtypeStruct((LEV, ROWS, N), F32)
    return pl.pallas_call(
        block_forward_kernel, grid=(9,),
        out_shape=(big, jax.ShapeDtypeStruct((NPX, BLK, 128), F32), big, TOKEN),
        in_specs=[SM, small, small, small, two,
                  pl.BlockSpec((1, ROWS, N), lambda g: (jnp.clip(2 * g, 2, 7), 0, 0)), two, fixed((1536, 512)),
                  fixed((256, 128)), col, fixed((2, ROWS, 128))],
        out_specs=(two, pl.BlockSpec((2, BLK, 128), lambda g: (jnp.maximum(g - 5, 0), 0, 0)), col, fixed((8, 128))),
        scratch_shapes=FOUR + [pltpu.VMEM((LEV, ROWS, N), F32), pltpu.VMEM((NPX, LEV, ROWS, 128), F32),
                               pltpu.VMEM((NPX, ROWS, 128), F32), pltpu.VMEM((ROWS, 512), F32)],
        compiler_params=params(VMEM_MIB), name="block_forward",
    )(addr, ids, wc, od, w, w, h, jnp.asarray(TAB), jnp.asarray(SINE2), jnp.asarray(PIVOT), jnp.asarray(COLS))


def lam_row(ly):
    return ly[pl.ds(N + lax.axis_index("px"), 1), :]


def edge_rows(x_ref, sr):
    for i in range(NPX):
        for k in range(LEV):
            cs = slice(k * 128, (k + 1) * 128)
            sr[i:i + 1, cs] = x_ref[(i + 7) % 8, 2 * ROWS + LEV + k:2 * ROWS + LEV + k + 1, :]
            sr[8 + i:9 + i, cs] = x_ref[(i + 1) % 8, 2 * ROWS + k:2 * ROWS + k + 1, :]
    return split(sr[...])


def edge_modes(edge, t, sh, sl):
    return dot3(edge[tile(t, 128), :], edge[pl.ds(pl.multiple_of(N + t * 128, 128), 128), :], sh, sl)


def y_forward_kernel(x_ref, tok, ly, tab, edge, al_ref, pp, sr, st):
    x = jnp.concatenate([x_ref[:, :ROWS], x_ref[:, ROWS:2 * ROWS]], axis=-1).reshape(N, 256)
    s, d = x[:512] + x[512:], x[:512] - x[512:]
    ee, eo = s[:256] + s[256:], s[:256] - s[256:]
    te, to, td = tab_parts(tab)
    for v, t, k0 in ((ee, te, 0), (eo, to, 256), (d, td, 512)):
        res = dot3(*t, *split(v))
        pp[k0:k0 + res.shape[0], :] = res
    sh, sl = edge_rows(x_ref, sr)
    lam_x = lam_row(ly)

    def some(t, c):
        st[...] = edge_modes(edge, t, sh, sl)
        for q in range(8):
            part = slice(q * 16, (q + 1) * 16)
            rows = pl.ds(pl.multiple_of(t * 128 + q * 16, 16), 16)
            phi, theta, _ = slab_polys(ly[rows, :] + lam_x)
            inv = inverse_of(phi[0])
            b0 = b7 = None
            for k in range(LEV):
                sk = st[part, k * 128:(k + 1) * 128]
                b0 = phi[k + 1] * sk if k == 0 else b0 + phi[k + 1] * sk
                b7 = sk if k == 0 else b7 + theta[k] * sk
            j, at = 2 * t + q // 4, (q % 4) * 16
            al_ref[j, at:at + 16, :] = pp[rows, :128] + b0 * inv
            al_ref[j, 64 + at:80 + at, :] = pp[rows, 128:] + b7 * inv
        return c
    lax.fori_loop(0, 8, some, 0)


def y_forward(x, tok):
    return pl.pallas_call(
        y_forward_kernel, grid=(1,),
        out_shape=jax.ShapeDtypeStruct((NPY, 128, 128), F32),
        in_specs=[fixed((NPX, BLK, 128)), fixed((8, 128)), fixed((N + NPX, 128)), fixed((1536, 512)),
                  fixed((2 * N, 16))],
        out_specs=fixed((NPY, 128, 128)),
        scratch_shapes=[pltpu.VMEM((N, 256), F32), pltpu.VMEM((16, N), F32), pltpu.VMEM((128, N), F32)],
        compiler_params=params(VMEM_MIB), name="y_forward",
    )(x, tok, jnp.asarray(LAMS), jnp.asarray(TAB_T), jnp.asarray(EDGE_F))


def ladder_kernel(al_ref, ly, fl_ref, out_ref):
    for j in range(NPY):
        out_ref[j, 128:, :] = fl_ref[j]

    lam_x = lam_row(ly)
    mine = lax.axis_index("py") * 64
    for t in range(8):
        rows, tops = slice(t * 8, (t + 1) * 8), slice(64 + t * 8, 72 + t * 8)
        phi, theta, delta = slab_polys(ly[pl.ds(pl.multiple_of(mine + t * 8, 8), 8), :] + lam_x)
        inv = 1.0 / phi[0]
        n07, n77, cc = inv, theta[7] * inv, delta * inv
        A = [None] * 17
        B = [None] * 17
        e = [None] * 17
        A[16] = jnp.zeros_like(inv)
        B[16] = jnp.full_like(inv, -2.0)
        for j in range(15, -1, -1):
            g, q = al_ref[j, rows, :], al_ref[j, tops, :]
            e[j + 1] = inverse_of(1.0 - n77 * B[j + 1])
            be = B[j + 1] * e[j + 1]
            A[j] = g + n07 * (A[j + 1] + be * (q + n77 * A[j + 1]))
            B[j] = n07 * n07 * be - cc
        p = -A[0] / B[0]
        for j in range(16):
            out_ref[j, rows, :] = p
            p = (al_ref[j, tops, :] + n77 * A[j + 1] + n07 * p) * e[j + 1]
            out_ref[j, tops, :] = A[j + 1] + B[j + 1] * p


def ladder(al, fl):
    return pl.pallas_call(
        ladder_kernel, grid=(1,), out_shape=jax.ShapeDtypeStruct((NPY, 136, 128), F32),
        in_specs=[fixed((NPY, 128, 128)), fixed((N + NPX, 128)), fixed((NPY, 8, 128))],
        out_specs=fixed((NPY, 136, 128)), compiler_params=params(VMEM_MIB), name="ladder",
    )(al, jnp.asarray(LAMS), fl)


def y_inverse_kernel(x_ref, pu_ref, ly, tab, edge_f, edge_b, out_ref, tok_ref, sr, st, ph, pl_):
    tok_ref[...] = jnp.zeros((8, 128), F32)
    sh, sl = edge_rows(x_ref, sr)
    lam_x = lam_row(ly)

    def some(t, c):
        st[...] = edge_modes(edge_f, t, sh, sl)
        for q in range(8):
            part = slice(q * 16, (q + 1) * 16)
            rows = pl.ds(pl.multiple_of(t * 128 + q * 16, 16), 16)
            j, at = 2 * t + q // 4, (q % 4) * 16
            low, top = pu_ref[j, at:at + 16, :], pu_ref[j, 64 + at:80 + at, :]
            lam = ly[rows, :] + lam_x
            cs = [None] * 8
            fs = [None] * 8
            cs[7] = inverse_of(1.0 - lam)
            fs[7] = st[part, 7 * 128:] + top
            for k in range(6, -1, -1):
                cs[k] = inverse_of(2.0 - lam - cs[k + 1])
                fs[k] = st[part, k * 128:(k + 1) * 128] + cs[k + 1] * fs[k + 1]
            prev = low
            for k in range(8):
                prev = cs[k] * (fs[k] + prev)
                ph[rows, k * 128:(k + 1) * 128], pl_[rows, k * 128:(k + 1) * 128] = split(prev)
        return c
    lax.fori_loop(0, 8, some, 0)
    edges = dot3(edge_b[:16, :], edge_b[16:, :], ph[...], pl_[...])
    for i in range(NPX):
        below, above = (i + 7) % 8, (i + 1) % 8
        for k in range(LEV):
            cols = slice(k * 128, (k + 1) * 128)
            lo = 2 * ROWS + k
            hi = 2 * ROWS + LEV + k
            out_ref[i, lo:lo + 1, :] = edges[8 + below:9 + below, cols] + x_ref[below, hi:hi + 1, :]
            out_ref[i, hi:hi + 1, :] = edges[above:above + 1, cols] + x_ref[above, lo:lo + 1, :]
    for q in range(4):
        flux = (pu_ref[4 * q, 128:, :] + pu_ref[4 * q + 1, 128:, :]) + (
            pu_ref[4 * q + 2, 128:, :] + pu_ref[4 * q + 3, 128:, :])
        for i in range(NPX):
            out_ref[i, BLK + q:BLK + q + 1, :] = flux[i:i + 1, :]
            out_ref[i, BLK + 4 + q:BLK + 5 + q, :] = jnp.zeros((1, 128), F32)
    pu = jnp.concatenate([pu_ref[:, :64], pu_ref[:, 64:128]], axis=-1).reshape(N, 256)
    te, to, td = tab_parts(tab)
    t0 = dot3(*te, *split(pu[:256]))
    t1 = dot3(*to, *split(pu[256:512]))
    d = dot3(*td, *split(pu[512:]))
    ev = (t0 + t1, t0 - t1)
    for i in range(4):
        base = ev[i // 2][(i % 2) * 128:(i % 2 + 1) * 128]
        odd = d[i * 128:(i + 1) * 128]
        for l in range(2):
            cols = slice(l * 128, (l + 1) * 128)
            out_ref[i, l * ROWS:(l + 1) * ROWS, :] = base[:, cols] + odd[:, cols]
            out_ref[i + 4, l * ROWS:(l + 1) * ROWS, :] = base[:, cols] - odd[:, cols]


def y_inverse(x, pu):
    return pl.pallas_call(
        y_inverse_kernel, grid=(1,), out_shape=(jax.ShapeDtypeStruct((NPX, BACK, 128), F32), TOKEN),
        in_specs=[fixed((NPX, BLK, 128)), fixed((NPY, 136, 128)), fixed((N + NPX, 128)), fixed((1536, 512)),
                  fixed((2 * N, 16)), fixed((32, N))],
        out_specs=(fixed((NPX, BACK, 128)), fixed((8, 128))),
        scratch_shapes=[pltpu.VMEM((16, N), F32), pltpu.VMEM((128, N), F32),
                        pltpu.VMEM((N, N), BF16), pltpu.VMEM((N, N), BF16)],
        compiler_params=params(VMEM_MIB), name="y_inverse",
    )(x, pu, jnp.asarray(LAMS), jnp.asarray(TAB), jnp.asarray(EDGE_F), jnp.asarray(EDGE_B))


def block_inverse_kernel(y_ref, g_ref, w_ref, roof_ref, tab, sine, piv, cols, ft, nr, hc, tok,
                         out_ref, nt_ref, field, wv, spu, fb):
    step = pl.program_id(0)
    sh, sl = sine[:128, :], sine[128:, :]

    @pl.when(step < 4)
    def _():
        parts = [y_ref[sub, f * ROWS:(f + 1) * ROWS, :] for sub in range(2) for f in range(2)]
        spu[...] = dot3(sh, sl, *split(jnp.concatenate(parts, axis=1)))
        for sub in range(2):
            lt = 2 * step + sub
            ln = slice(sub * 128, (sub + 1) * 128)
            fb[lt] = y_ref[sub, BLK:, :]
            edge = [y_ref[sub, 2 * ROWS + k:2 * ROWS + k + 1, :] for k in range(2 * LEV)]

            def inner(bt, c):
                rows = tile(bt, STRIP)
                s0, s1 = cols[0, rows, :], cols[1, rows, :]
                low = spu[rows, sub * 256:sub * 256 + 128]
                top = spu[rows, sub * 256 + 128:(sub + 1) * 256]
                fs = [s0 * edge[k] + s1 * edge[LEV + k] - g_ref[k, rows, ln] for k in range(LEV)]
                fs[0] = fs[0] + low
                fs[7] = fs[7] + top
                prev = low
                for k, p in enumerate(eliminate(fs, [piv[k, rows, ln] for k in range(LEV)])):
                    wv[sub, rows, k * 128:(k + 1) * 128] = p - prev
                    prev = p
                return c
            lax.fori_loop(0, ROWS // STRIP, inner, 0)
            res = dot3(sh, sl, *split(wv[sub]))
            for k in range(LEV):
                field[k, :, tile(lt, 128)] = res[:, k * 128:(k + 1) * 128]

    @pl.when(step >= 4)
    def _():
        pair = step - 4
        v = jnp.concatenate([field[2 * pair], field[2 * pair + 1]], axis=0)
        te, to, td = tab_parts(tab)
        t0 = dot3(*split(v[:, :256]), *te)
        t1 = dot3(*split(v[:, 256:512]), *to)
        d = dot3(*split(v[:, 512:]), *td)
        s = jnp.concatenate([t0 + t1, t0 - t1], axis=1)
        for half, res in ((0, s + d), (1, s - d)):
            cs = slice(half * 512, (half + 1) * 512)
            for l in range(2):
                solid = lax.axis_index("py") * LEV + 2 * pair + l < roof_ref[:, cs]
                out_ref[l, :, cs] = jnp.where(solid, 0.0, w_ref[l, :, cs] - res[l * 128:(l + 1) * 128])

    @pl.when(step == 7)
    def _():
        flux = jnp.concatenate([fb[i, :4, :] for i in range(NPX)], axis=0)
        nt_ref[...] = ft[...] + (nr[...] - flux - 0.5 * ft[...]) / hc[...]


def block_inverse(y, g, w, roof, ft, nr, hc, tok):
    late = pl.BlockSpec((2, ROWS, N), lambda t: (jnp.maximum(t - 4, 0), 0, 0))
    return pl.pallas_call(
        block_inverse_kernel, grid=(8,),
        out_shape=(jax.ShapeDtypeStruct((LEV, ROWS, N), F32), jax.ShapeDtypeStruct((32, 128), F32)),
        in_specs=[pl.BlockSpec((2, BACK, 128), lambda t: (jnp.minimum(t, 3), 0, 0)),
                  pl.BlockSpec((LEV, ROWS, 256), lambda t: (0, 0, jnp.minimum(t, 3))),
                  late, fixed((ROWS, N)), fixed((1536, 512)), fixed((256, 128)),
                  pl.BlockSpec((LEV, ROWS, 256), lambda t: (0, 0, jnp.minimum(t, 3))), fixed((2, ROWS, 128)),
                  fixed((32, 128)), fixed((32, 128)), fixed((32, 128)), fixed((8, 128))],
        out_specs=(late, fixed((32, 128))),
        scratch_shapes=[pltpu.VMEM((LEV, ROWS, N), F32), pltpu.VMEM((2, ROWS, N), F32), pltpu.VMEM((ROWS, 512), F32),
                        pltpu.VMEM((NPX, 8, 128), F32)],
        compiler_params=params(VMEM_MIB), name="block_inverse",
    )(y, g, w, roof, jnp.asarray(TAB_T), jnp.asarray(SINE2), jnp.asarray(PIVOT), jnp.asarray(COLS), ft, nr, hc, tok)


def swap(x, axes):
    return lax.all_to_all(x, axes, split_axis=0, concat_axis=0, tiled=True)


def body(horiz_div, w_star, air_temp, roof_level, facet_cells, facet_temp, net_radiation,
         heat_capacity, drag_coef, heat_coef):
    ft, nr, hc, dr, he, ce = [
        v.reshape(32, 128) for v in (facet_temp, net_radiation, heat_capacity, drag_coef, heat_coef, facet_cells)]
    owner, ids, addr = pack_owner(ft, dr, he, ce)
    od = swap(owner.reshape(OWNERS, 1, 128), ("px", "py")).reshape(OWNERS, 128)
    addr = addr.reshape(OWNERS * SLOT)
    w2, a2 = w_star.reshape(1024, 1024), air_temp.reshape(1024, 1024)
    tiles = w2.reshape(128, 8, 8, 128).transpose(0, 2, 1, 3).reshape(8192, 128)
    wc = gather_w(addr, ids, tiles)
    w_corr, sent, g, tok = block_forward(addr, ids, wc, od, w_star, horiz_div)
    xs = swap(sent, "px")
    flux, fl, tok = heat_flux(addr, tok, ids, wc, od, a2)
    pu = swap(ladder(swap(y_forward(xs, tok), "py"), fl), "py")
    back, tok = y_inverse(xs, pu)
    ys = swap(back, "px")
    theta, tok = new_theta(addr, tok, ids, flux, a2)
    w_new, temp_new = block_inverse(ys, g, w_corr, roof_level, ft, nr, hc, tok)
    return w_new, theta.reshape(LEV, ROWS, N), temp_new.reshape(1, OWNERS * SLOT)


def solution(mesh):
    field, facet = P("py", "px", None), P(("px", "py"), None)
    return jax.shard_map(
        body, mesh=mesh,
        in_specs=(field, field, field, P("px", None)) + (facet,) * 6,
        out_specs=(field, field, facet), check_vma=False)
```

```python
import functools
import math

import jax
import jax.numpy as jnp
import numpy as np
from jax import lax
from jax.experimental import pallas as pl
from jax.experimental.pallas import tpu as pltpu
from jax.sharding import PartitionSpec as P

N = 1024
NPX, NPY = 8, 16
LEV, ROWS = 8, 128
OWNERS, SLOT = 128, 32
MIB = 1 << 20
VMEM_MIB = 50
F32, BF16 = jnp.float32, jnp.bfloat16


def mode_table():
    classes = [np.arange(0, 513, 4), np.arange(2, 513, 4), np.arange(1, 512, 2)]
    n = np.arange(N)
    cols, waves = [], []
    for ks in classes:
        for k in ks:
            edge = k == 0 or k == N // 2
            norm = math.sqrt((1.0 if edge else 2.0) / N)
            cols.append(norm * np.cos(2 * np.pi * ((n * k) % N) / N))
            waves.append(k)
        for k in ks:
            if k == 0 or k == N // 2:
                continue
            cols.append(math.sqrt(2.0 / N) * np.sin(2 * np.pi * ((n * k) % N) / N))
            waves.append(k)
    table = np.stack(cols, axis=1)
    eigen = -4.0 * np.sin(np.pi * np.array(waves) / N) ** 2
    return table, eigen


def split_np(a):
    a = a.astype(np.float32)
    hi = a.astype(jnp.bfloat16)
    lo = (a - hi.astype(np.float32)).astype(jnp.bfloat16)
    return hi, lo


TABLE, EIGEN = mode_table()
T_EE = TABLE[:256, :256]
T_EO = TABLE[:256, 256:512]
T_OD = TABLE[:512, 512:]


def split(v):
    hi = v.astype(BF16)
    return hi, (v - hi.astype(F32)).astype(BF16)


def dot3(ah, al, bh, bl):
    d = functools.partial(jnp.dot, preferred_element_type=F32)
    return d(ah, bh) + (d(al, bh) + d(ah, bl))


def params(mb, sem=None):
    return pltpu.CompilerParams(vmem_limit_bytes=mb * MIB)


TOKEN = jax.ShapeDtypeStruct((8, 128), F32)
VM = pl.BlockSpec(memory_space=pltpu.VMEM)
SM = pl.BlockSpec(memory_space=pltpu.SMEM)


def pack_kernel(ft, dr, he, ce, od, ids, addr):
    zero = jnp.zeros((32, 32), F32)
    none = jnp.zeros((32, 96), jnp.int32)
    for q in range(4):
        c = slice(q * 32, (q + 1) * 32)
        od[pl.ds(q, 32, stride=4), :] = jnp.concatenate([ft[:, c], dr[:, c], he[:, c], zero], axis=1)
        ids[pl.ds(q, 32, stride=4), :] = jnp.concatenate([ce[:, c], none], axis=1)
    safe = jnp.maximum(ce[...], 0)
    row = safe >> 10
    addr[...] = (row >> 3) * 64 + ((safe >> 7) & 7) * 8 + (row & 7)


def pack_owner(ft, dr, he, ce):
    full = jax.ShapeDtypeStruct((OWNERS, 128), F32)
    return pl.pallas_call(
        pack_kernel, out_shape=(full, jax.ShapeDtypeStruct((OWNERS, 128), jnp.int32),
                                jax.ShapeDtypeStruct((32, 128), jnp.int32)),
        in_specs=[VM] * 4, out_specs=(VM,) * 3, compiler_params=params(58), name="pack_owner",
    )(ft, dr, he, ce)


def load_temp(a_ref, tt):
    def one(i, c):
        for ct in range(8):
            v = a_ref[tile(i, 16), ct * 128:(ct + 1) * 128].astype(F32)
            tt[tile(i * 16 + ct), :] = v[:8]
            tt[tile(i * 16 + 8 + ct), :] = v[8:]
        return c
    lax.fori_loop(0, 64, one, 0)


def gather_rows(addr, src, buf):
    def one(o, c):
        for s in range(SLOT):
            buf[pl.ds(s * OWNERS + o, 1), :] = src[pl.ds(addr[o * SLOT + s], 1), :]
        return c
    lax.fori_loop(0, OWNERS, one, 0)


def hits(ids, s, lane):
    col = ids[:, s:s + 1]
    return lane == jnp.where(col >= 0, col & 127, -1)


def pick(ids, buf):
    lane = lax.broadcasted_iota(jnp.int32, (OWNERS, 128), 1)
    out = jnp.zeros((OWNERS, 128), F32)
    for s in range(SLOT):
        v = jnp.where(hits(ids, s, lane), buf[s * OWNERS:(s + 1) * OWNERS, :], 0.0)
        out = jnp.where(lane == s, jnp.sum(v, axis=1, keepdims=True), out)
    return out


def spread_rows(ids, vals, buf):
    lane = lax.broadcasted_iota(jnp.int32, (OWNERS, 128), 1)
    for s in range(SLOT):
        buf[s * OWNERS:(s + 1) * OWNERS, :] = jnp.where(hits(ids, s, lane), vals[:, s:s + 1], 0.0)


def clear(accs):
    def one(i, c):
        for a in accs:
            for j in range(8):
                a[tile(i * 8 + j), :] = jnp.zeros((8, 128), F32)
        return c
    lax.fori_loop(0, 128, one, 0)


def add_rows(addr, accs, buf):
    width = len(accs)

    def one(o, c):
        for s in range(0, SLOT, 2 * width):
            at = [addr[o * SLOT + s + j] for j in range(2 * width)]
            x = [buf[pl.ds((s + j) * OWNERS + o, 1), :] for j in range(2 * width)]
            old = [accs[j % width][pl.ds(at[j], 1), :] for j in range(2 * width)]
            for j in range(width):
                first = old[j] + x[j]
                second = jnp.where(at[j] == at[j + width], first, old[j + width]) + x[j + width]
                accs[j][pl.ds(at[j], 1), :] = first
                accs[j][pl.ds(at[j + width], 1), :] = second
        return c
    lax.fori_loop(0, OWNERS, one, 0)


def total(accs, rows):
    return (accs[0][rows, :] + accs[1][rows, :]) + (accs[2][rows, :] + accs[3][rows, :])


def gather_kernel(addr, ids_ref, w_ref, wc_ref, buf):
    gather_rows(addr, w_ref, buf)
    wc_ref[...] = pick(ids_ref[...], buf)


def gather_w(addr, ids, w2):
    return pl.pallas_call(
        gather_kernel, out_shape=jax.ShapeDtypeStruct((OWNERS, 128), F32), in_specs=[SM, VM, VM], out_specs=VM,
        scratch_shapes=[pltpu.VMEM((4096, 128), F32)],
        compiler_params=params(VMEM_MIB), name="facet_gather",
    )(addr, ids, w2)


FOUR = [pltpu.VMEM((8192, 128), F32)] * 4 + [pltpu.VMEM((4096, 128), F32)]


def flux_kernel(addr, tok_in, ids_ref, wc_ref, od_ref, a_ref, flux_ref, fl_ref, tok_ref, tt, buf, turned):
    load_temp(a_ref, tt)
    gather_rows(addr, tt, buf)
    tc = pick(ids_ref[...], buf)[:, :SLOT]
    wc = wc_ref[:, :SLOT]
    flux = od_ref[:, 64:96] * jnp.sqrt(wc * wc + 0.25) * (od_ref[:, :32] - tc)
    wide = jnp.concatenate([flux, jnp.zeros((OWNERS, 96), F32)], axis=1)
    flux_ref[...] = wide
    turned[...] = pltpu.roll(wide, (lax.axis_index("py") % 4) * SLOT, 1)
    for j in range(NPY):
        fl_ref[j] = turned[pl.ds(j, 8, stride=16), :]
    tok_ref[...] = tok_in[...]


def heat_flux(addr, tok, ids, wc, od, a2):
    return pl.pallas_call(
        flux_kernel,
        out_shape=(jax.ShapeDtypeStruct((OWNERS, 128), F32), jax.ShapeDtypeStruct((NPY, 8, 128), F32), TOKEN),
        in_specs=[SM] + [VM] * 5, out_specs=(VM,) * 3,
        scratch_shapes=[pltpu.VMEM((8192, 128), F32), pltpu.VMEM((4096, 128), F32), pltpu.VMEM((OWNERS, 128), F32)],
        cost_estimate=pl.CostEstimate(flops=0, bytes_accessed=25 * MIB, transcendentals=0),
        compiler_params=params(30), name="heat_flux",
    )(addr, tok, ids, wc, od, a2)


def theta_kernel(addr, tok_in, ids_ref, flux_ref, a_ref, th_ref, tok_ref, acc0, acc1, acc2, acc3, buf):
    accs = (acc0, acc1, acc2, acc3)
    load_temp(a_ref, acc0)
    clear(accs[1:])
    spread_rows(ids_ref[...], flux_ref[...], buf)
    add_rows(addr, accs, buf)

    def put(i, c):
        for ct in range(8):
            v0 = total(accs, tile(i * 16 + ct))
            v1 = total(accs, tile(i * 16 + 8 + ct))
            th_ref[tile(i, 16), ct * 128:(ct + 1) * 128] = jnp.concatenate([v0, v1], axis=0).astype(BF16)
        return c
    lax.fori_loop(0, 64, put, 0)
    tok_ref[...] = tok_in[...]


def new_theta(addr, tok, ids, flux, a2):
    return pl.pallas_call(
        theta_kernel, out_shape=(jax.ShapeDtypeStruct((1024, 1024), BF16), TOKEN),
        in_specs=[SM] + [VM] * 4, out_specs=(VM, VM), scratch_shapes=FOUR,
        cost_estimate=pl.CostEstimate(flops=0, bytes_accessed=40 * MIB, transcendentals=0),
        compiler_params=params(42), name="new_theta",
    )(addr, tok, ids, flux, a2)


BLK = 2 * ROWS + 2 * LEV
BACK = BLK + 8


def y_basis():
    i = np.arange(ROWS) + 1
    s = math.sqrt(2 / 129) * np.sin(np.pi * (np.outer(i, i) % 258) / 129)
    mu = -4.0 * np.sin(np.pi * i / 258) ** 2
    return s, mu


SINE, MU = y_basis()
EDGE = np.concatenate([TABLE[0::ROWS], TABLE[ROWS - 1::ROWS]])


def pack(transposed):
    parts = [split_np(t.T if transposed else t) for t in (T_EE, T_EO, T_OD)]
    (eh, el), (oh, ol), (dh, dl) = parts
    return np.concatenate([dh, dl, np.concatenate([np.concatenate([eh, oh], 1), np.concatenate([el, ol], 1)])])


TAB, TAB_T = pack(False), pack(True)
SINE2 = np.concatenate(split_np(SINE))
EDGE_F = np.concatenate(split_np(EDGE.T))
EDGE_B = np.concatenate(split_np(EDGE))
LAM_Y = np.broadcast_to(EIGEN.astype(np.float32)[:, None], (N, 128)).copy()
LAMS = np.concatenate([LAM_Y, EIGEN.astype(np.float32).reshape(NPX, 128)])
COLS = np.stack([np.broadcast_to(v[:, None], (ROWS, 128)) for v in (SINE[:, 0], SINE[:, 127])]).astype(np.float32)


def pivots():
    lam = MU[:, None] + EIGEN[None, :]
    c = [1.0 / (1.0 - lam)]
    for _ in range(LEV - 1):
        c.insert(0, 1.0 / (2.0 - lam - c[0]))
    return np.stack(c).astype(np.float32)


PIVOT = pivots()


def tab_parts(t):
    return ((t[1024:1280, :256], t[1280:1536, :256]), (t[1024:1280, 256:], t[1280:1536, 256:]),
            (t[:512], t[512:1024]))


def tile(i, size=8):
    return pl.ds(pl.multiple_of(i * size, size), size)


def fixed(shape):
    return pl.BlockSpec(shape, lambda g: (0,) * len(shape))


def slab_polys(lam):
    phi = [None] * 9
    phi[8] = jnp.ones_like(lam)
    delta = -lam
    phi[7] = phi[8] + delta
    for k in range(6, -1, -1):
        delta = delta - lam * phi[k + 1]
        phi[k] = phi[k + 1] + delta
    theta = [jnp.ones_like(lam), 2.0 - lam]
    for k in range(2, 8):
        theta.append((2.0 - lam) * theta[k - 1] - theta[k - 2])
    return phi, theta, delta


def inverse_of(v):
    r = pl.reciprocal(v, approx=True)
    r = r * (2.0 - v * r)
    return r * (2.0 - v * r)


def x_modes(v, tab):
    s, d = v[:, :512] + v[:, 512:], v[:, :512] - v[:, 512:]
    te, to, td = tab_parts(tab)
    return ((0, dot3(*split(s[:, :256] + s[:, 256:]), *te)), (256, dot3(*split(s[:, :256] - s[:, 256:]), *to)),
            (512, dot3(*split(d), *td)))


STRIP = 32


def fold(v):
    return jnp.sum(v.reshape(STRIP // 8, 8, 128), axis=0)


def eliminate(fs, cs):
    fs = list(fs)
    for k in range(LEV - 2, -1, -1):
        fs[k] = fs[k] + cs[k + 1] * fs[k + 1]
    ps = [cs[0] * fs[0]]
    for k in range(1, LEV):
        ps.append(cs[k] * (fs[k] + ps[k - 1]))
    return ps


def block_forward_kernel(addr, ids_ref, wc_ref, od_ref, w_ref, wn_ref, h_ref, tab, sine, piv, cols,
                         wo_ref, out_ref, r_ref, tok_ref,
                         acc0, acc1, acc2, acc3, buf, wf, r2, hx, a07):
    step = pl.program_id(0)
    sh, sl = sine[:128, :], sine[128:, :]

    accs = (acc0, acc1, acc2, acc3)

    def corrected(src, l, level):
        def put(tr, c):
            for ct in range(8):
                cs = slice(ct * 128, (ct + 1) * 128)
                wf[level, tile(tr), cs] = src[l, tile(tr), cs] + total(accs, tile((level * 16 + tr) * 8 + ct))
            return c
        lax.fori_loop(0, 16, put, 0)

    @pl.when(step == 0)
    def _():
        tok_ref[...] = jnp.zeros((8, 128), F32)
        clear(accs)
        wc = wc_ref[:, :SLOT]
        stress = od_ref[:, 32:64] * jnp.sqrt(wc * wc + 0.25) * wc
        spread_rows(ids_ref[...], -stress, buf)
        add_rows(addr, accs, buf)
        corrected(w_ref, 0, 0)
        lifted = (lax.axis_index("py") > 0).astype(F32)
        for c0, res in x_modes(wf[0] * lifted, tab):
            for b in range(res.shape[1] // 128):
                hx[c0 // 128 + b] = res[:, b * 128:(b + 1) * 128]

    @pl.when((step > 0) & (step < 5))
    def _():
        lv = 2 * step - 2
        corrected(w_ref, 1, lv + 1)

        @pl.when(step < 4)
        def _():
            corrected(wn_ref, 0, lv + 2)
        w0, w1 = wf[lv], wf[lv + 1]
        wo_ref[0] = w0
        wo_ref[1] = w1
        up = jnp.where(step == 4, 0.0, wf[jnp.minimum(lv + 2, LEV - 1)])
        r = jnp.concatenate([h_ref[0] + w1 - w0, h_ref[1] + up - w1], axis=0)
        for c0, res in x_modes(r, tab):
            for l in range(2):
                v = dot3(sh, sl, *split(res[l * 128:(l + 1) * 128]))
                for b in range(res.shape[1] // 128):
                    r2[c0 // 128 + b, lv + l] = v[:, b * 128:(b + 1) * 128]

    @pl.when(step >= 5)
    def _():
        for sub in range(2):
            lt = 2 * (step - 5) + sub
            ln = slice(sub * 128, (sub + 1) * 128)

            def inner(bt, acc):
                rows = tile(bt, STRIP)
                rs = [r2[lt, k, rows, :] for k in range(LEV)]
                for k in range(LEV):
                    r_ref[k, rows, ln] = rs[k]
                ps = eliminate(rs, [piv[k, rows, ln] for k in range(LEV)])
                s0, s1 = cols[0, rows, :], cols[1, rows, :]
                a07[rows, sub * 256:sub * 256 + 128] = ps[0]
                a07[rows, sub * 256 + 128:(sub + 1) * 256] = ps[7]
                return tuple(acc[k] + fold(s0 * ps[k]) for k in range(LEV)) + tuple(
                    acc[LEV + k] + fold(s1 * ps[k]) for k in range(LEV))
            acc = lax.fori_loop(0, ROWS // STRIP, inner, tuple(jnp.zeros((8, 128), F32) for _ in range(16)))
            for e in range(2):
                sums = [jnp.sum(acc[e * LEV + k], axis=0, keepdims=True) for k in range(LEV)]
                out_ref[sub, 2 * ROWS + e * LEV:2 * ROWS + (e + 1) * LEV, :] = -jnp.concatenate(sums, axis=0)
        res = dot3(sh, sl, *split(a07[...]))
        for sub in range(2):
            out_ref[sub, :ROWS, :] = -res[:, sub * 256:sub * 256 + 128] - hx[2 * (step - 5) + sub]
            out_ref[sub, ROWS:2 * ROWS, :] = -res[:, sub * 256 + 128:(sub + 1) * 256]


def block_forward(addr, ids, wc, od, w, h):
    two = pl.BlockSpec((2, ROWS, N), lambda g: (jnp.clip(g - 1, 0, 3), 0, 0))
    col = pl.BlockSpec((LEV, ROWS, 256), lambda g: (0, 0, jnp.maximum(g - 5, 0)))
    small = fixed((OWNERS, 128))
    big = jax.ShapeDtypeStruct((LEV, ROWS, N), F32)
    return pl.pallas_call(
        block_forward_kernel, grid=(9,),
        out_shape=(big, jax.ShapeDtypeStruct((NPX, BLK, 128), F32), big, TOKEN),
        in_specs=[SM, small, small, small, two,
                  pl.BlockSpec((1, ROWS, N), lambda g: (jnp.clip(2 * g, 2, 7), 0, 0)), two, fixed((1536, 512)),
                  fixed((256, 128)), col, fixed((2, ROWS, 128))],
        out_specs=(two, pl.BlockSpec((2, BLK, 128), lambda g: (jnp.maximum(g - 5, 0), 0, 0)), col, fixed((8, 128))),
        scratch_shapes=FOUR + [pltpu.VMEM((LEV, ROWS, N), F32), pltpu.VMEM((NPX, LEV, ROWS, 128), F32),
                               pltpu.VMEM((NPX, ROWS, 128), F32), pltpu.VMEM((ROWS, 512), F32)],
        compiler_params=params(58), name="block_forward",
    )(addr, ids, wc, od, w, w, h, jnp.asarray(TAB), jnp.asarray(SINE2), jnp.asarray(PIVOT), jnp.asarray(COLS))


def lam_row(ly):
    return ly[pl.ds(N + lax.axis_index("px"), 1), :]


def edge_rows(x_ref, sr):
    for i in range(NPX):
        for k in range(LEV):
            cs = slice(k * 128, (k + 1) * 128)
            sr[i:i + 1, cs] = x_ref[(i + 7) % 8, 2 * ROWS + LEV + k:2 * ROWS + LEV + k + 1, :]
            sr[8 + i:9 + i, cs] = x_ref[(i + 1) % 8, 2 * ROWS + k:2 * ROWS + k + 1, :]
    return split(sr[...])


def edge_modes(edge, t, sh, sl):
    return dot3(edge[tile(t, 128), :], edge[pl.ds(pl.multiple_of(N + t * 128, 128), 128), :], sh, sl)


def y_forward_kernel(x_ref, tok, ly, tab, edge, al_ref, pp, sr, st):
    x = jnp.concatenate([x_ref[:, :ROWS], x_ref[:, ROWS:2 * ROWS]], axis=-1).reshape(N, 256)
    s, d = x[:512] + x[512:], x[:512] - x[512:]
    ee, eo = s[:256] + s[256:], s[:256] - s[256:]
    te, to, td = tab_parts(tab)
    for v, t, k0 in ((ee, te, 0), (eo, to, 256), (d, td, 512)):
        res = dot3(*t, *split(v))
        pp[k0:k0 + res.shape[0], :] = res
    sh, sl = edge_rows(x_ref, sr)
    lam_x = lam_row(ly)

    def some(t, c):
        st[...] = edge_modes(edge, t, sh, sl)
        for q in range(8):
            part = slice(q * 16, (q + 1) * 16)
            rows = pl.ds(pl.multiple_of(t * 128 + q * 16, 16), 16)
            phi, theta, _ = slab_polys(ly[rows, :] + lam_x)
            inv = inverse_of(phi[0])
            b0 = b7 = None
            for k in range(LEV):
                sk = st[part, k * 128:(k + 1) * 128]
                b0 = phi[k + 1] * sk if k == 0 else b0 + phi[k + 1] * sk
                b7 = sk if k == 0 else b7 + theta[k] * sk
            j, at = 2 * t + q // 4, (q % 4) * 16
            al_ref[j, at:at + 16, :] = pp[rows, :128] + b0 * inv
            al_ref[j, 64 + at:80 + at, :] = pp[rows, 128:] + b7 * inv
        return c
    lax.fori_loop(0, 8, some, 0)


def y_forward(x, tok):
    return pl.pallas_call(
        y_forward_kernel, grid=(1,),
        out_shape=jax.ShapeDtypeStruct((NPY, 128, 128), F32),
        in_specs=[fixed((NPX, BLK, 128)), fixed((8, 128)), fixed((N + NPX, 128)), fixed((1536, 512)),
                  fixed((2 * N, 16))],
        out_specs=fixed((NPY, 128, 128)),
        scratch_shapes=[pltpu.VMEM((N, 256), F32), pltpu.VMEM((16, N), F32), pltpu.VMEM((128, N), F32)],
        compiler_params=params(VMEM_MIB), name="y_forward",
    )(x, tok, jnp.asarray(LAMS), jnp.asarray(TAB_T), jnp.asarray(EDGE_F))


def ladder_kernel(al_ref, ly, fl_ref, out_ref):
    for j in range(NPY):
        out_ref[j, 128:, :] = fl_ref[j]

    lam_x = lam_row(ly)
    mine = lax.axis_index("py") * 64
    for t in range(8):
        rows, tops = slice(t * 8, (t + 1) * 8), slice(64 + t * 8, 72 + t * 8)
        phi, theta, delta = slab_polys(ly[pl.ds(pl.multiple_of(mine + t * 8, 8), 8), :] + lam_x)
        inv = 1.0 / phi[0]
        n07, n77, cc = inv, theta[7] * inv, delta * inv
        A = [None] * 17
        B = [None] * 17
        e = [None] * 17
        A[16] = jnp.zeros_like(inv)
        B[16] = jnp.full_like(inv, -2.0)
        for j in range(15, -1, -1):
            g, q = al_ref[j, rows, :], al_ref[j, tops, :]
            e[j + 1] = inverse_of(1.0 - n77 * B[j + 1])
            be = B[j + 1] * e[j + 1]
            A[j] = g + n07 * (A[j + 1] + be * (q + n77 * A[j + 1]))
            B[j] = n07 * n07 * be - cc
        p = -A[0] / B[0]
        for j in range(16):
            out_ref[j, rows, :] = p
            p = (al_ref[j, tops, :] + n77 * A[j + 1] + n07 * p) * e[j + 1]
            out_ref[j, tops, :] = A[j + 1] + B[j + 1] * p


def ladder(al, fl):
    return pl.pallas_call(
        ladder_kernel, grid=(1,), out_shape=jax.ShapeDtypeStruct((NPY, 136, 128), F32),
        in_specs=[fixed((NPY, 128, 128)), fixed((N + NPX, 128)), fixed((NPY, 8, 128))],
        out_specs=fixed((NPY, 136, 128)), compiler_params=params(VMEM_MIB), name="ladder",
    )(al, jnp.asarray(LAMS), fl)


def y_inverse_kernel(x_ref, pu_ref, ly, tab, edge_f, edge_b, out_ref, tok_ref, sr, st, ph, pl_):
    tok_ref[...] = jnp.zeros((8, 128), F32)
    sh, sl = edge_rows(x_ref, sr)
    lam_x = lam_row(ly)

    def some(t, c):
        st[...] = edge_modes(edge_f, t, sh, sl)
        for q in range(8):
            part = slice(q * 16, (q + 1) * 16)
            rows = pl.ds(pl.multiple_of(t * 128 + q * 16, 16), 16)
            j, at = 2 * t + q // 4, (q % 4) * 16
            low, top = pu_ref[j, at:at + 16, :], pu_ref[j, 64 + at:80 + at, :]
            lam = ly[rows, :] + lam_x
            cs = [None] * 8
            fs = [None] * 8
            cs[7] = inverse_of(1.0 - lam)
            fs[7] = st[part, 7 * 128:] + top
            for k in range(6, -1, -1):
                cs[k] = inverse_of(2.0 - lam - cs[k + 1])
                fs[k] = st[part, k * 128:(k + 1) * 128] + cs[k + 1] * fs[k + 1]
            prev = low
            for k in range(8):
                prev = cs[k] * (fs[k] + prev)
                ph[rows, k * 128:(k + 1) * 128], pl_[rows, k * 128:(k + 1) * 128] = split(prev)
        return c
    lax.fori_loop(0, 8, some, 0)
    edges = dot3(edge_b[:16, :], edge_b[16:, :], ph[...], pl_[...])
    for i in range(NPX):
        below, above = (i + 7) % 8, (i + 1) % 8
        for k in range(LEV):
            cols = slice(k * 128, (k + 1) * 128)
            lo = 2 * ROWS + k
            hi = 2 * ROWS + LEV + k
            out_ref[i, lo:lo + 1, :] = edges[8 + below:9 + below, cols] + x_ref[below, hi:hi + 1, :]
            out_ref[i, hi:hi + 1, :] = edges[above:above + 1, cols] + x_ref[above, lo:lo + 1, :]
    for q in range(4):
        flux = (pu_ref[4 * q, 128:, :] + pu_ref[4 * q + 1, 128:, :]) + (
            pu_ref[4 * q + 2, 128:, :] + pu_ref[4 * q + 3, 128:, :])
        for i in range(NPX):
            out_ref[i, BLK + q:BLK + q + 1, :] = flux[i:i + 1, :]
            out_ref[i, BLK + 4 + q:BLK + 5 + q, :] = jnp.zeros((1, 128), F32)
    pu = jnp.concatenate([pu_ref[:, :64], pu_ref[:, 64:128]], axis=-1).reshape(N, 256)
    te, to, td = tab_parts(tab)
    t0 = dot3(*te, *split(pu[:256]))
    t1 = dot3(*to, *split(pu[256:512]))
    d = dot3(*td, *split(pu[512:]))
    ev = (t0 + t1, t0 - t1)
    for i in range(4):
        base = ev[i // 2][(i % 2) * 128:(i % 2 + 1) * 128]
        odd = d[i * 128:(i + 1) * 128]
        for l in range(2):
            cols = slice(l * 128, (l + 1) * 128)
            out_ref[i, l * ROWS:(l + 1) * ROWS, :] = base[:, cols] + odd[:, cols]
            out_ref[i + 4, l * ROWS:(l + 1) * ROWS, :] = base[:, cols] - odd[:, cols]


def y_inverse(x, pu):
    return pl.pallas_call(
        y_inverse_kernel, grid=(1,), out_shape=(jax.ShapeDtypeStruct((NPX, BACK, 128), F32), TOKEN),
        in_specs=[fixed((NPX, BLK, 128)), fixed((NPY, 136, 128)), fixed((N + NPX, 128)), fixed((1536, 512)),
                  fixed((2 * N, 16)), fixed((32, N))],
        out_specs=(fixed((NPX, BACK, 128)), fixed((8, 128))),
        scratch_shapes=[pltpu.VMEM((16, N), F32), pltpu.VMEM((128, N), F32),
                        pltpu.VMEM((N, N), BF16), pltpu.VMEM((N, N), BF16)],
        compiler_params=params(VMEM_MIB), name="y_inverse",
    )(x, pu, jnp.asarray(LAMS), jnp.asarray(TAB), jnp.asarray(EDGE_F), jnp.asarray(EDGE_B))


def block_inverse_kernel(y_ref, g_ref, w_ref, roof_ref, tab, sine, piv, cols, ft, nr, hc, tok,
                         out_ref, nt_ref, field, wv, spu, fb):
    step = pl.program_id(0)
    sh, sl = sine[:128, :], sine[128:, :]

    @pl.when(step < 4)
    def _():
        parts = [y_ref[sub, f * ROWS:(f + 1) * ROWS, :] for sub in range(2) for f in range(2)]
        spu[...] = dot3(sh, sl, *split(jnp.concatenate(parts, axis=1)))
        for sub in range(2):
            lt = 2 * step + sub
            ln = slice(sub * 128, (sub + 1) * 128)
            fb[lt] = y_ref[sub, BLK:, :]
            edge = [y_ref[sub, 2 * ROWS + k:2 * ROWS + k + 1, :] for k in range(2 * LEV)]

            def inner(bt, c):
                rows = tile(bt, STRIP)
                s0, s1 = cols[0, rows, :], cols[1, rows, :]
                low = spu[rows, sub * 256:sub * 256 + 128]
                top = spu[rows, sub * 256 + 128:(sub + 1) * 256]
                fs = [s0 * edge[k] + s1 * edge[LEV + k] - g_ref[k, rows, ln] for k in range(LEV)]
                fs[0] = fs[0] + low
                fs[7] = fs[7] + top
                prev = low
                for k, p in enumerate(eliminate(fs, [piv[k, rows, ln] for k in range(LEV)])):
                    wv[sub, rows, k * 128:(k + 1) * 128] = p - prev
                    prev = p
                return c
            lax.fori_loop(0, ROWS // STRIP, inner, 0)
            res = dot3(sh, sl, *split(wv[sub]))
            for k in range(LEV):
                field[k, :, tile(lt, 128)] = res[:, k * 128:(k + 1) * 128]

    @pl.when(step >= 4)
    def _():
        pair = step - 4
        v = jnp.concatenate([field[2 * pair], field[2 * pair + 1]], axis=0)
        te, to, td = tab_parts(tab)
        t0 = dot3(*split(v[:, :256]), *te)
        t1 = dot3(*split(v[:, 256:512]), *to)
        d = dot3(*split(v[:, 512:]), *td)
        s = jnp.concatenate([t0 + t1, t0 - t1], axis=1)
        for half, res in ((0, s + d), (1, s - d)):
            cs = slice(half * 512, (half + 1) * 512)
            for l in range(2):
                solid = lax.axis_index("py") * LEV + 2 * pair + l < roof_ref[:, cs]
                out_ref[l, :, cs] = jnp.where(solid, 0.0, w_ref[l, :, cs] - res[l * 128:(l + 1) * 128])

    @pl.when(step == 7)
    def _():
        flux = jnp.concatenate([fb[i, :4, :] for i in range(NPX)], axis=0)
        nt_ref[...] = ft[...] + (nr[...] - flux - 0.5 * ft[...]) / hc[...]


def block_inverse(y, g, w, roof, ft, nr, hc, tok):
    late = pl.BlockSpec((2, ROWS, N), lambda t: (jnp.maximum(t - 4, 0), 0, 0))
    return pl.pallas_call(
        block_inverse_kernel, grid=(8,),
        out_shape=(jax.ShapeDtypeStruct((LEV, ROWS, N), F32), jax.ShapeDtypeStruct((32, 128), F32)),
        in_specs=[pl.BlockSpec((2, BACK, 128), lambda t: (jnp.minimum(t, 3), 0, 0)),
                  pl.BlockSpec((LEV, ROWS, 256), lambda t: (0, 0, jnp.minimum(t, 3))),
                  late, fixed((ROWS, N)), fixed((1536, 512)), fixed((256, 128)),
                  pl.BlockSpec((LEV, ROWS, 256), lambda t: (0, 0, jnp.minimum(t, 3))), fixed((2, ROWS, 128)),
                  fixed((32, 128)), fixed((32, 128)), fixed((32, 128)), fixed((8, 128))],
        out_specs=(late, fixed((32, 128))),
        scratch_shapes=[pltpu.VMEM((LEV, ROWS, N), F32), pltpu.VMEM((2, ROWS, N), F32), pltpu.VMEM((ROWS, 512), F32),
                        pltpu.VMEM((NPX, 8, 128), F32)],
        compiler_params=params(VMEM_MIB), name="block_inverse",
    )(y, g, w, roof, jnp.asarray(TAB_T), jnp.asarray(SINE2), jnp.asarray(PIVOT), jnp.asarray(COLS), ft, nr, hc, tok)


def swap(x, axes):
    return lax.all_to_all(x, axes, split_axis=0, concat_axis=0, tiled=True)


def body(horiz_div, w_star, air_temp, roof_level, facet_cells, facet_temp, net_radiation,
         heat_capacity, drag_coef, heat_coef):
    ft, nr, hc, dr, he, ce = [
        v.reshape(32, 128) for v in (facet_temp, net_radiation, heat_capacity, drag_coef, heat_coef, facet_cells)]
    owner, ids, addr = pack_owner(ft, dr, he, ce)
    od = swap(owner.reshape(OWNERS, 1, 128), ("px", "py")).reshape(OWNERS, 128)
    addr = addr.reshape(OWNERS * SLOT)
    w2, a2 = w_star.reshape(1024, 1024), air_temp.reshape(1024, 1024)
    tiles = w2.reshape(128, 8, 8, 128).transpose(0, 2, 1, 3).reshape(8192, 128)
    wc = gather_w(addr, ids, tiles)
    w_corr, sent, g, tok = block_forward(addr, ids, wc, od, w_star, horiz_div)
    xs = swap(sent, "px")
    flux, fl, tok = heat_flux(addr, tok, ids, wc, od, a2)
    pu = swap(ladder(swap(y_forward(xs, tok), "py"), fl), "py")
    back, tok = y_inverse(xs, pu)
    ys = swap(back, "px")
    theta, tok = new_theta(addr, tok, ids, flux, a2)
    w_new, temp_new = block_inverse(ys, g, w_corr, roof_level, ft, nr, hc, tok)
    return w_new, theta.reshape(LEV, ROWS, N), temp_new.reshape(1, OWNERS * SLOT)


def solution(mesh):
    field, facet = P("py", "px", None), P(("px", "py"), None)
    return jax.shard_map(
        body, mesh=mesh,
        in_specs=(field, field, field, P("px", None)) + (facet,) * 6,
        out_specs=(field, field, facet), check_vma=False)
```

```python
import functools
import math

import jax
import jax.numpy as jnp
import numpy as np
from jax import lax
from jax.experimental import pallas as pl
from jax.experimental.pallas import tpu as pltpu
from jax.sharding import PartitionSpec as P

N = 1024
NPX, NPY = 8, 16
LEV, ROWS = 8, 128
OWNERS, SLOT = 128, 32
MIB = 1 << 20
VMEM_MIB = 50
F32, BF16 = jnp.float32, jnp.bfloat16


def mode_table():
    classes = [np.arange(0, 513, 4), np.arange(2, 513, 4), np.arange(1, 512, 2)]
    n = np.arange(N)
    cols, waves = [], []
    for ks in classes:
        for k in ks:
            edge = k == 0 or k == N // 2
            norm = math.sqrt((1.0 if edge else 2.0) / N)
            cols.append(norm * np.cos(2 * np.pi * ((n * k) % N) / N))
            waves.append(k)
        for k in ks:
            if k == 0 or k == N // 2:
                continue
            cols.append(math.sqrt(2.0 / N) * np.sin(2 * np.pi * ((n * k) % N) / N))
            waves.append(k)
    table = np.stack(cols, axis=1)
    eigen = -4.0 * np.sin(np.pi * np.array(waves) / N) ** 2
    return table, eigen


def split_np(a):
    a = a.astype(np.float32)
    hi = a.astype(jnp.bfloat16)
    lo = (a - hi.astype(np.float32)).astype(jnp.bfloat16)
    return hi, lo


TABLE, EIGEN = mode_table()
T_EE = TABLE[:256, :256]
T_EO = TABLE[:256, 256:512]
T_OD = TABLE[:512, 512:]


def split(v):
    hi = v.astype(BF16)
    return hi, (v - hi.astype(F32)).astype(BF16)


def dot3(ah, al, bh, bl):
    d = functools.partial(jnp.dot, preferred_element_type=F32)
    return d(ah, bh) + (d(al, bh) + d(ah, bl))


def params(mb, sem=None):
    return pltpu.CompilerParams(vmem_limit_bytes=mb * MIB)


TOKEN = jax.ShapeDtypeStruct((8, 128), F32)
VM = pl.BlockSpec(memory_space=pltpu.VMEM)
SM = pl.BlockSpec(memory_space=pltpu.SMEM)


def pack_kernel(ft, dr, he, ce, od, ids, addr):
    zero = jnp.zeros((32, 32), F32)
    none = jnp.zeros((32, 96), jnp.int32)
    for q in range(4):
        c = slice(q * 32, (q + 1) * 32)
        od[pl.ds(q, 32, stride=4), :] = jnp.concatenate([ft[:, c], dr[:, c], he[:, c], zero], axis=1)
        ids[pl.ds(q, 32, stride=4), :] = jnp.concatenate([ce[:, c], none], axis=1)
    safe = jnp.maximum(ce[...], 0)
    row = safe >> 10
    addr[...] = (row >> 3) * 64 + ((safe >> 7) & 7) * 8 + (row & 7)


def pack_owner(ft, dr, he, ce):
    full = jax.ShapeDtypeStruct((OWNERS, 128), F32)
    return pl.pallas_call(
        pack_kernel, out_shape=(full, jax.ShapeDtypeStruct((OWNERS, 128), jnp.int32),
                                jax.ShapeDtypeStruct((32, 128), jnp.int32)),
        in_specs=[VM] * 4, out_specs=(VM,) * 3, compiler_params=params(58), name="pack_owner",
    )(ft, dr, he, ce)


def load_temp(a_ref, tt):
    def one(i, c):
        for ct in range(8):
            v = a_ref[tile(i, 16), ct * 128:(ct + 1) * 128].astype(F32)
            tt[tile(i * 16 + ct), :] = v[:8]
            tt[tile(i * 16 + 8 + ct), :] = v[8:]
        return c
    lax.fori_loop(0, 64, one, 0)


def gather_rows(addr, src, buf):
    def one(o, c):
        for s in range(SLOT):
            buf[pl.ds(s * OWNERS + o, 1), :] = src[pl.ds(addr[o * SLOT + s], 1), :]
        return c
    lax.fori_loop(0, OWNERS, one, 0)


def hits(ids, s, lane):
    col = ids[:, s:s + 1]
    return lane == jnp.where(col >= 0, col & 127, -1)


def pick(ids, buf):
    lane = lax.broadcasted_iota(jnp.int32, (OWNERS, 128), 1)
    out = jnp.zeros((OWNERS, 128), F32)
    for s in range(SLOT):
        v = jnp.where(hits(ids, s, lane), buf[s * OWNERS:(s + 1) * OWNERS, :], 0.0)
        out = jnp.where(lane == s, jnp.sum(v, axis=1, keepdims=True), out)
    return out


def spread_rows(ids, vals, buf):
    lane = lax.broadcasted_iota(jnp.int32, (OWNERS, 128), 1)
    for s in range(SLOT):
        buf[s * OWNERS:(s + 1) * OWNERS, :] = jnp.where(hits(ids, s, lane), vals[:, s:s + 1], 0.0)


def clear(accs):
    def one(i, c):
        for a in accs:
            for j in range(8):
                a[tile(i * 8 + j), :] = jnp.zeros((8, 128), F32)
        return c
    lax.fori_loop(0, 128, one, 0)


def add_rows(addr, accs, buf):
    width = len(accs)

    def one(o, c):
        for s in range(0, SLOT, 2 * width):
            at = [addr[o * SLOT + s + j] for j in range(2 * width)]
            x = [buf[pl.ds((s + j) * OWNERS + o, 1), :] for j in range(2 * width)]
            old = [accs[j % width][pl.ds(at[j], 1), :] for j in range(2 * width)]
            for j in range(width):
                first = old[j] + x[j]
                second = jnp.where(at[j] == at[j + width], first, old[j + width]) + x[j + width]
                accs[j][pl.ds(at[j], 1), :] = first
                accs[j][pl.ds(at[j + width], 1), :] = second
        return c
    lax.fori_loop(0, OWNERS, one, 0)


def total(accs, rows):
    return (accs[0][rows, :] + accs[1][rows, :]) + (accs[2][rows, :] + accs[3][rows, :])


def gather_kernel(addr, ids_ref, w_ref, wc_ref, buf):
    gather_rows(addr, w_ref, buf)
    wc_ref[...] = pick(ids_ref[...], buf)


def gather_w(addr, ids, w2):
    return pl.pallas_call(
        gather_kernel, out_shape=jax.ShapeDtypeStruct((OWNERS, 128), F32), in_specs=[SM, VM, VM], out_specs=VM,
        scratch_shapes=[pltpu.VMEM((4096, 128), F32)],
        compiler_params=params(VMEM_MIB), name="facet_gather",
    )(addr, ids, w2)


FOUR = [pltpu.VMEM((8192, 128), F32)] * 4 + [pltpu.VMEM((4096, 128), F32)]


def flux_kernel(addr, tok_in, ids_ref, wc_ref, od_ref, a_ref, flux_ref, fl_ref, tok_ref, tt, buf, turned):
    load_temp(a_ref, tt)
    gather_rows(addr, tt, buf)
    tc = pick(ids_ref[...], buf)[:, :SLOT]
    wc = wc_ref[:, :SLOT]
    flux = od_ref[:, 64:96] * jnp.sqrt(wc * wc + 0.25) * (od_ref[:, :32] - tc)
    wide = jnp.concatenate([flux, jnp.zeros((OWNERS, 96), F32)], axis=1)
    flux_ref[...] = wide
    turned[...] = pltpu.roll(wide, (lax.axis_index("py") % 4) * SLOT, 1)
    for j in range(NPY):
        fl_ref[j] = turned[pl.ds(j, 8, stride=16), :]
    tok_ref[...] = tok_in[...]


def heat_flux(addr, tok, ids, wc, od, a2):
    return pl.pallas_call(
        flux_kernel,
        out_shape=(jax.ShapeDtypeStruct((OWNERS, 128), F32), jax.ShapeDtypeStruct((NPY, 8, 128), F32), TOKEN),
        in_specs=[SM] + [VM] * 5, out_specs=(VM,) * 3,
        scratch_shapes=[pltpu.VMEM((8192, 128), F32), pltpu.VMEM((4096, 128), F32), pltpu.VMEM((OWNERS, 128), F32)],
        cost_estimate=pl.CostEstimate(flops=0, bytes_accessed=25 * MIB, transcendentals=0),
        compiler_params=params(30), name="heat_flux",
    )(addr, tok, ids, wc, od, a2)


def theta_kernel(addr, tok_in, ids_ref, flux_ref, a_ref, th_ref, tok_ref, acc0, acc1, acc2, acc3, buf):
    accs = (acc0, acc1, acc2, acc3)
    load_temp(a_ref, acc0)
    clear(accs[1:])
    spread_rows(ids_ref[...], flux_ref[...], buf)
    add_rows(addr, accs, buf)

    def put(i, c):
        for ct in range(8):
            v0 = total(accs, tile(i * 16 + ct))
            v1 = total(accs, tile(i * 16 + 8 + ct))
            th_ref[tile(i, 16), ct * 128:(ct + 1) * 128] = jnp.concatenate([v0, v1], axis=0).astype(BF16)
        return c
    lax.fori_loop(0, 64, put, 0)
    tok_ref[...] = tok_in[...]


def new_theta(addr, tok, ids, flux, a2):
    return pl.pallas_call(
        theta_kernel, out_shape=(jax.ShapeDtypeStruct((1024, 1024), BF16), TOKEN),
        in_specs=[SM] + [VM] * 4, out_specs=(VM, VM), scratch_shapes=FOUR,
        cost_estimate=pl.CostEstimate(flops=0, bytes_accessed=40 * MIB, transcendentals=0),
        compiler_params=params(42), name="new_theta",
    )(addr, tok, ids, flux, a2)


BLK = 2 * ROWS + 2 * LEV
BACK = BLK + 8


def y_basis():
    i = np.arange(ROWS) + 1
    s = math.sqrt(2 / 129) * np.sin(np.pi * (np.outer(i, i) % 258) / 129)
    mu = -4.0 * np.sin(np.pi * i / 258) ** 2
    return s, mu


SINE, MU = y_basis()
EDGE = np.concatenate([TABLE[0::ROWS], TABLE[ROWS - 1::ROWS]])


def pack(transposed):
    parts = [split_np(t.T if transposed else t) for t in (T_EE, T_EO, T_OD)]
    (eh, el), (oh, ol), (dh, dl) = parts
    return np.concatenate([dh, dl, np.concatenate([np.concatenate([eh, oh], 1), np.concatenate([el, ol], 1)])])


TAB, TAB_T = pack(False), pack(True)
SINE2 = np.concatenate(split_np(SINE))
EDGE_F = np.concatenate(split_np(EDGE.T))
EDGE_B = np.concatenate(split_np(EDGE))
LAM_Y = np.broadcast_to(EIGEN.astype(np.float32)[:, None], (N, 128)).copy()
LAMS = np.concatenate([LAM_Y, EIGEN.astype(np.float32).reshape(NPX, 128)])
COLS = np.stack([np.broadcast_to(v[:, None], (ROWS, 128)) for v in (SINE[:, 0], SINE[:, 127])]).astype(np.float32)


def pivots():
    lam = MU[:, None] + EIGEN[None, :]
    c = [1.0 / (1.0 - lam)]
    for _ in range(LEV - 1):
        c.insert(0, 1.0 / (2.0 - lam - c[0]))
    return np.stack(c).astype(np.float32)


PIVOT = pivots()


def tab_parts(t):
    return ((t[1024:1280, :256], t[1280:1536, :256]), (t[1024:1280, 256:], t[1280:1536, 256:]),
            (t[:512], t[512:1024]))


def tile(i, size=8):
    return pl.ds(pl.multiple_of(i * size, size), size)


def fixed(shape):
    return pl.BlockSpec(shape, lambda g: (0,) * len(shape))


def slab_polys(lam):
    phi = [None] * 9
    phi[8] = jnp.ones_like(lam)
    delta = -lam
    phi[7] = phi[8] + delta
    for k in range(6, -1, -1):
        delta = delta - lam * phi[k + 1]
        phi[k] = phi[k + 1] + delta
    theta = [jnp.ones_like(lam), 2.0 - lam]
    for k in range(2, 8):
        theta.append((2.0 - lam) * theta[k - 1] - theta[k - 2])
    return phi, theta, delta


def inverse_of(v):
    r = pl.reciprocal(v, approx=True)
    r = r * (2.0 - v * r)
    return r * (2.0 - v * r)


def x_modes(v, tab):
    s, d = v[:, :512] + v[:, 512:], v[:, :512] - v[:, 512:]
    te, to, td = tab_parts(tab)
    return ((0, dot3(*split(s[:, :256] + s[:, 256:]), *te)), (256, dot3(*split(s[:, :256] - s[:, 256:]), *to)),
            (512, dot3(*split(d), *td)))


STRIP = 16


def fold(v):
    return jnp.sum(v.reshape(STRIP // 8, 8, 128), axis=0)


def eliminate(fs, cs):
    fs = list(fs)
    for k in range(LEV - 2, -1, -1):
        fs[k] = fs[k] + cs[k + 1] * fs[k + 1]
    ps = [cs[0] * fs[0]]
    for k in range(1, LEV):
        ps.append(cs[k] * (fs[k] + ps[k - 1]))
    return ps


def block_forward_kernel(addr, ids_ref, wc_ref, od_ref, w_ref, wn_ref, h_ref, tab, sine, piv, cols,
                         wo_ref, out_ref, r_ref, tok_ref,
                         acc0, acc1, acc2, acc3, buf, wf, r2, hx, a07):
    step = pl.program_id(0)
    sh, sl = sine[:128, :], sine[128:, :]

    accs = (acc0, acc1, acc2, acc3)

    def corrected(src, l, level):
        def put(tr, c):
            for ct in range(8):
                cs = slice(ct * 128, (ct + 1) * 128)
                wf[level, tile(tr), cs] = src[l, tile(tr), cs] + total(accs, tile((level * 16 + tr) * 8 + ct))
            return c
        lax.fori_loop(0, 16, put, 0)

    @pl.when(step == 0)
    def _():
        tok_ref[...] = jnp.zeros((8, 128), F32)
        clear(accs)
        wc = wc_ref[:, :SLOT]
        stress = od_ref[:, 32:64] * jnp.sqrt(wc * wc + 0.25) * wc
        spread_rows(ids_ref[...], -stress, buf)
        add_rows(addr, accs, buf)
        corrected(w_ref, 0, 0)
        lifted = (lax.axis_index("py") > 0).astype(F32)
        for c0, res in x_modes(wf[0] * lifted, tab):
            for b in range(res.shape[1] // 128):
                hx[c0 // 128 + b] = res[:, b * 128:(b + 1) * 128]

    @pl.when((step > 0) & (step < 5))
    def _():
        lv = 2 * step - 2
        corrected(w_ref, 1, lv + 1)

        @pl.when(step < 4)
        def _():
            corrected(wn_ref, 0, lv + 2)
        w0, w1 = wf[lv], wf[lv + 1]
        wo_ref[0] = w0
        wo_ref[1] = w1
        up = jnp.where(step == 4, 0.0, wf[jnp.minimum(lv + 2, LEV - 1)])
        r = jnp.concatenate([h_ref[0] + w1 - w0, h_ref[1] + up - w1], axis=0)
        for c0, res in x_modes(r, tab):
            for l in range(2):
                v = dot3(sh, sl, *split(res[l * 128:(l + 1) * 128]))
                for b in range(res.shape[1] // 128):
                    r2[c0 // 128 + b, lv + l] = v[:, b * 128:(b + 1) * 128]

    @pl.when(step >= 5)
    def _():
        for sub in range(2):
            lt = 2 * (step - 5) + sub
            ln = slice(sub * 128, (sub + 1) * 128)

            def inner(bt, acc):
                rows = tile(bt, STRIP)
                rs = [r2[lt, k, rows, :] for k in range(LEV)]
                for k in range(LEV):
                    r_ref[k, rows, ln] = rs[k]
                ps = eliminate(rs, [piv[k, rows, ln] for k in range(LEV)])
                s0, s1 = cols[0, rows, :], cols[1, rows, :]
                a07[rows, sub * 256:sub * 256 + 128] = ps[0]
                a07[rows, sub * 256 + 128:(sub + 1) * 256] = ps[7]
                return tuple(acc[k] + fold(s0 * ps[k]) for k in range(LEV)) + tuple(
                    acc[LEV + k] + fold(s1 * ps[k]) for k in range(LEV))
            acc = lax.fori_loop(0, ROWS // STRIP, inner, tuple(jnp.zeros((8, 128), F32) for _ in range(16)))
            for e in range(2):
                sums = [jnp.sum(acc[e * LEV + k], axis=0, keepdims=True) for k in range(LEV)]
                out_ref[sub, 2 * ROWS + e * LEV:2 * ROWS + (e + 1) * LEV, :] = -jnp.concatenate(sums, axis=0)
        res = dot3(sh, sl, *split(a07[...]))
        for sub in range(2):
            out_ref[sub, :ROWS, :] = -res[:, sub * 256:sub * 256 + 128] - hx[2 * (step - 5) + sub]
            out_ref[sub, ROWS:2 * ROWS, :] = -res[:, sub * 256 + 128:(sub + 1) * 256]


def block_forward(addr, ids, wc, od, w, h):
    two = pl.BlockSpec((2, ROWS, N), lambda g: (jnp.clip(g - 1, 0, 3), 0, 0))
    col = pl.BlockSpec((LEV, ROWS, 256), lambda g: (0, 0, jnp.maximum(g - 5, 0)))
    small = fixed((OWNERS, 128))
    big = jax.ShapeDtypeStruct((LEV, ROWS, N), F32)
    return pl.pallas_call(
        block_forward_kernel, grid=(9,),
        out_shape=(big, jax.ShapeDtypeStruct((NPX, BLK, 128), F32), big, TOKEN),
        in_specs=[SM, small, small, small, two,
                  pl.BlockSpec((1, ROWS, N), lambda g: (jnp.clip(2 * g, 2, 7), 0, 0)), two, fixed((1536, 512)),
                  fixed((256, 128)), col, fixed((2, ROWS, 128))],
        out_specs=(two, pl.BlockSpec((2, BLK, 128), lambda g: (jnp.maximum(g - 5, 0), 0, 0)), col, fixed((8, 128))),
        scratch_shapes=FOUR + [pltpu.VMEM((LEV, ROWS, N), F32), pltpu.VMEM((NPX, LEV, ROWS, 128), F32),
                               pltpu.VMEM((NPX, ROWS, 128), F32), pltpu.VMEM((ROWS, 512), F32)],
        compiler_params=params(VMEM_MIB), name="block_forward",
    )(addr, ids, wc, od, w, w, h, jnp.asarray(TAB), jnp.asarray(SINE2), jnp.asarray(PIVOT), jnp.asarray(COLS))


def lam_row(ly):
    return ly[pl.ds(N + lax.axis_index("px"), 1), :]


def edge_rows(x_ref, sr):
    for i in range(NPX):
        for k in range(LEV):
            cs = slice(k * 128, (k + 1) * 128)
            sr[i:i + 1, cs] = x_ref[(i + 7) % 8, 2 * ROWS + LEV + k:2 * ROWS + LEV + k + 1, :]
            sr[8 + i:9 + i, cs] = x_ref[(i + 1) % 8, 2 * ROWS + k:2 * ROWS + k + 1, :]
    return split(sr[...])


def edge_modes(edge, t, sh, sl):
    return dot3(edge[tile(t, 128), :], edge[pl.ds(pl.multiple_of(N + t * 128, 128), 128), :], sh, sl)


def y_forward_kernel(x_ref, tok, ly, tab, edge, al_ref, pp, sr, st):
    x = jnp.concatenate([x_ref[:, :ROWS], x_ref[:, ROWS:2 * ROWS]], axis=-1).reshape(N, 256)
    s, d = x[:512] + x[512:], x[:512] - x[512:]
    ee, eo = s[:256] + s[256:], s[:256] - s[256:]
    te, to, td = tab_parts(tab)
    for v, t, k0 in ((ee, te, 0), (eo, to, 256), (d, td, 512)):
        res = dot3(*t, *split(v))
        pp[k0:k0 + res.shape[0], :] = res
    sh, sl = edge_rows(x_ref, sr)
    lam_x = lam_row(ly)

    def some(t, c):
        st[...] = edge_modes(edge, t, sh, sl)
        for q in range(8):
            part = slice(q * 16, (q + 1) * 16)
            rows = pl.ds(pl.multiple_of(t * 128 + q * 16, 16), 16)
            phi, theta, _ = slab_polys(ly[rows, :] + lam_x)
            inv = inverse_of(phi[0])
            b0 = b7 = None
            for k in range(LEV):
                sk = st[part, k * 128:(k + 1) * 128]
                b0 = phi[k + 1] * sk if k == 0 else b0 + phi[k + 1] * sk
                b7 = sk if k == 0 else b7 + theta[k] * sk
            j, at = 2 * t + q // 4, (q % 4) * 16
            al_ref[j, at:at + 16, :] = pp[rows, :128] + b0 * inv
            al_ref[j, 64 + at:80 + at, :] = pp[rows, 128:] + b7 * inv
        return c
    lax.fori_loop(0, 8, some, 0)


def y_forward(x, tok):
    return pl.pallas_call(
        y_forward_kernel, grid=(1,),
        out_shape=jax.ShapeDtypeStruct((NPY, 128, 128), F32),
        in_specs=[fixed((NPX, BLK, 128)), fixed((8, 128)), fixed((N + NPX, 128)), fixed((1536, 512)),
                  fixed((2 * N, 16))],
        out_specs=fixed((NPY, 128, 128)),
        scratch_shapes=[pltpu.VMEM((N, 256), F32), pltpu.VMEM((16, N), F32), pltpu.VMEM((128, N), F32)],
        compiler_params=params(VMEM_MIB), name="y_forward",
    )(x, tok, jnp.asarray(LAMS), jnp.asarray(TAB_T), jnp.asarray(EDGE_F))


def ladder_kernel(al_ref, ly, fl_ref, out_ref):
    for j in range(NPY):
        out_ref[j, 128:, :] = fl_ref[j]

    lam_x = lam_row(ly)
    mine = lax.axis_index("py") * 64
    for t in range(8):
        rows, tops = slice(t * 8, (t + 1) * 8), slice(64 + t * 8, 72 + t * 8)
        phi, theta, delta = slab_polys(ly[pl.ds(pl.multiple_of(mine + t * 8, 8), 8), :] + lam_x)
        inv = 1.0 / phi[0]
        n07, n77, cc = inv, theta[7] * inv, delta * inv
        A = [None] * 17
        B = [None] * 17
        e = [None] * 17
        A[16] = jnp.zeros_like(inv)
        B[16] = jnp.full_like(inv, -2.0)
        for j in range(15, -1, -1):
            g, q = al_ref[j, rows, :], al_ref[j, tops, :]
            e[j + 1] = inverse_of(1.0 - n77 * B[j + 1])
            be = B[j + 1] * e[j + 1]
            A[j] = g + n07 * (A[j + 1] + be * (q + n77 * A[j + 1]))
            B[j] = n07 * n07 * be - cc
        p = -A[0] / B[0]
        for j in range(16):
            out_ref[j, rows, :] = p
            p = (al_ref[j, tops, :] + n77 * A[j + 1] + n07 * p) * e[j + 1]
            out_ref[j, tops, :] = A[j + 1] + B[j + 1] * p


def ladder(al, fl):
    return pl.pallas_call(
        ladder_kernel, grid=(1,), out_shape=jax.ShapeDtypeStruct((NPY, 136, 128), F32),
        in_specs=[fixed((NPY, 128, 128)), fixed((N + NPX, 128)), fixed((NPY, 8, 128))],
        out_specs=fixed((NPY, 136, 128)), compiler_params=params(VMEM_MIB), name="ladder",
    )(al, jnp.asarray(LAMS), fl)


def y_inverse_kernel(x_ref, pu_ref, ly, tab, edge_f, edge_b, out_ref, tok_ref, sr, st, ph, pl_):
    tok_ref[...] = jnp.zeros((8, 128), F32)
    sh, sl = edge_rows(x_ref, sr)
    lam_x = lam_row(ly)

    def some(t, c):
        st[...] = edge_modes(edge_f, t, sh, sl)
        for q in range(8):
            part = slice(q * 16, (q + 1) * 16)
            rows = pl.ds(pl.multiple_of(t * 128 + q * 16, 16), 16)
            j, at = 2 * t + q // 4, (q % 4) * 16
            low, top = pu_ref[j, at:at + 16, :], pu_ref[j, 64 + at:80 + at, :]
            lam = ly[rows, :] + lam_x
            cs = [None] * 8
            fs = [None] * 8
            cs[7] = inverse_of(1.0 - lam)
            fs[7] = st[part, 7 * 128:] + top
            for k in range(6, -1, -1):
                cs[k] = inverse_of(2.0 - lam - cs[k + 1])
                fs[k] = st[part, k * 128:(k + 1) * 128] + cs[k + 1] * fs[k + 1]
            prev = low
            for k in range(8):
                prev = cs[k] * (fs[k] + prev)
                ph[rows, k * 128:(k + 1) * 128], pl_[rows, k * 128:(k + 1) * 128] = split(prev)
        return c
    lax.fori_loop(0, 8, some, 0)
    edges = dot3(edge_b[:16, :], edge_b[16:, :], ph[...], pl_[...])
    for i in range(NPX):
        below, above = (i + 7) % 8, (i + 1) % 8
        for k in range(LEV):
            cols = slice(k * 128, (k + 1) * 128)
            lo = 2 * ROWS + k
            hi = 2 * ROWS + LEV + k
            out_ref[i, lo:lo + 1, :] = edges[8 + below:9 + below, cols] + x_ref[below, hi:hi + 1, :]
            out_ref[i, hi:hi + 1, :] = edges[above:above + 1, cols] + x_ref[above, lo:lo + 1, :]
    for q in range(4):
        flux = (pu_ref[4 * q, 128:, :] + pu_ref[4 * q + 1, 128:, :]) + (
            pu_ref[4 * q + 2, 128:, :] + pu_ref[4 * q + 3, 128:, :])
        for i in range(NPX):
            out_ref[i, BLK + q:BLK + q + 1, :] = flux[i:i + 1, :]
            out_ref[i, BLK + 4 + q:BLK + 5 + q, :] = jnp.zeros((1, 128), F32)
    pu = jnp.concatenate([pu_ref[:, :64], pu_ref[:, 64:128]], axis=-1).reshape(N, 256)
    te, to, td = tab_parts(tab)
    t0 = dot3(*te, *split(pu[:256]))
    t1 = dot3(*to, *split(pu[256:512]))
    d = dot3(*td, *split(pu[512:]))
    ev = (t0 + t1, t0 - t1)
    for i in range(4):
        base = ev[i // 2][(i % 2) * 128:(i % 2 + 1) * 128]
        odd = d[i * 128:(i + 1) * 128]
        for l in range(2):
            cols = slice(l * 128, (l + 1) * 128)
            out_ref[i, l * ROWS:(l + 1) * ROWS, :] = base[:, cols] + odd[:, cols]
            out_ref[i + 4, l * ROWS:(l + 1) * ROWS, :] = base[:, cols] - odd[:, cols]


def y_inverse(x, pu):
    return pl.pallas_call(
        y_inverse_kernel, grid=(1,), out_shape=(jax.ShapeDtypeStruct((NPX, BACK, 128), F32), TOKEN),
        in_specs=[fixed((NPX, BLK, 128)), fixed((NPY, 136, 128)), fixed((N + NPX, 128)), fixed((1536, 512)),
                  fixed((2 * N, 16)), fixed((32, N))],
        out_specs=(fixed((NPX, BACK, 128)), fixed((8, 128))),
        scratch_shapes=[pltpu.VMEM((16, N), F32), pltpu.VMEM((128, N), F32),
                        pltpu.VMEM((N, N), BF16), pltpu.VMEM((N, N), BF16)],
        compiler_params=params(VMEM_MIB), name="y_inverse",
    )(x, pu, jnp.asarray(LAMS), jnp.asarray(TAB), jnp.asarray(EDGE_F), jnp.asarray(EDGE_B))


def block_inverse_kernel(y_ref, g_ref, w_ref, roof_ref, tab, sine, piv, cols, ft, nr, hc, tok,
                         out_ref, nt_ref, field, wv, spu, fb):
    step = pl.program_id(0)
    sh, sl = sine[:128, :], sine[128:, :]

    @pl.when(step < 4)
    def _():
        parts = [y_ref[sub, f * ROWS:(f + 1) * ROWS, :] for sub in range(2) for f in range(2)]
        spu[...] = dot3(sh, sl, *split(jnp.concatenate(parts, axis=1)))
        for sub in range(2):
            lt = 2 * step + sub
            ln = slice(sub * 128, (sub + 1) * 128)
            fb[lt] = y_ref[sub, BLK:, :]
            edge = [y_ref[sub, 2 * ROWS + k:2 * ROWS + k + 1, :] for k in range(2 * LEV)]

            def inner(bt, c):
                rows = tile(bt, STRIP)
                s0, s1 = cols[0, rows, :], cols[1, rows, :]
                low = spu[rows, sub * 256:sub * 256 + 128]
                top = spu[rows, sub * 256 + 128:(sub + 1) * 256]
                fs = [s0 * edge[k] + s1 * edge[LEV + k] - g_ref[k, rows, ln] for k in range(LEV)]
                fs[0] = fs[0] + low
                fs[7] = fs[7] + top
                prev = low
                for k, p in enumerate(eliminate(fs, [piv[k, rows, ln] for k in range(LEV)])):
                    wv[sub, rows, k * 128:(k + 1) * 128] = p - prev
                    prev = p
                return c
            lax.fori_loop(0, ROWS // STRIP, inner, 0)
            res = dot3(sh, sl, *split(wv[sub]))
            for k in range(LEV):
                field[k, :, tile(lt, 128)] = res[:, k * 128:(k + 1) * 128]

    @pl.when(step >= 4)
    def _():
        pair = step - 4
        v = jnp.concatenate([field[2 * pair], field[2 * pair + 1]], axis=0)
        te, to, td = tab_parts(tab)
        t0 = dot3(*split(v[:, :256]), *te)
        t1 = dot3(*split(v[:, 256:512]), *to)
        d = dot3(*split(v[:, 512:]), *td)
        s = jnp.concatenate([t0 + t1, t0 - t1], axis=1)
        for half, res in ((0, s + d), (1, s - d)):
            cs = slice(half * 512, (half + 1) * 512)
            for l in range(2):
                solid = lax.axis_index("py") * LEV + 2 * pair + l < roof_ref[:, cs]
                out_ref[l, :, cs] = jnp.where(solid, 0.0, w_ref[l, :, cs] - res[l * 128:(l + 1) * 128])

    @pl.when(step == 7)
    def _():
        flux = jnp.concatenate([fb[i, :4, :] for i in range(NPX)], axis=0)
        nt_ref[...] = ft[...] + (nr[...] - flux - 0.5 * ft[...]) / hc[...]


def block_inverse(y, g, w, roof, ft, nr, hc, tok):
    late = pl.BlockSpec((2, ROWS, N), lambda t: (jnp.maximum(t - 4, 0), 0, 0))
    return pl.pallas_call(
        block_inverse_kernel, grid=(8,),
        out_shape=(jax.ShapeDtypeStruct((LEV, ROWS, N), F32), jax.ShapeDtypeStruct((32, 128), F32)),
        in_specs=[pl.BlockSpec((2, BACK, 128), lambda t: (jnp.minimum(t, 3), 0, 0)),
                  pl.BlockSpec((LEV, ROWS, 256), lambda t: (0, 0, jnp.minimum(t, 3))),
                  late, fixed((ROWS, N)), fixed((1536, 512)), fixed((256, 128)),
                  pl.BlockSpec((LEV, ROWS, 256), lambda t: (0, 0, jnp.minimum(t, 3))), fixed((2, ROWS, 128)),
                  fixed((32, 128)), fixed((32, 128)), fixed((32, 128)), fixed((8, 128))],
        out_specs=(late, fixed((32, 128))),
        scratch_shapes=[pltpu.VMEM((LEV, ROWS, N), F32), pltpu.VMEM((2, ROWS, N), F32), pltpu.VMEM((ROWS, 512), F32),
                        pltpu.VMEM((NPX, 8, 128), F32)],
        compiler_params=params(VMEM_MIB), name="block_inverse",
    )(y, g, w, roof, jnp.asarray(TAB_T), jnp.asarray(SINE2), jnp.asarray(PIVOT), jnp.asarray(COLS), ft, nr, hc, tok)


def swap(x, axes):
    return lax.all_to_all(x, axes, split_axis=0, concat_axis=0, tiled=True)


def body(horiz_div, w_star, air_temp, roof_level, facet_cells, facet_temp, net_radiation,
         heat_capacity, drag_coef, heat_coef):
    ft, nr, hc, dr, he, ce = [
        v.reshape(32, 128) for v in (facet_temp, net_radiation, heat_capacity, drag_coef, heat_coef, facet_cells)]
    owner, ids, addr = pack_owner(ft, dr, he, ce)
    od = swap(owner.reshape(OWNERS, 1, 128), ("px", "py")).reshape(OWNERS, 128)
    addr = addr.reshape(OWNERS * SLOT)
    w2, a2 = w_star.reshape(1024, 1024), air_temp.reshape(1024, 1024)
    tiles = w2.reshape(128, 8, 8, 128).transpose(0, 2, 1, 3).reshape(8192, 128)
    wc = gather_w(addr, ids, tiles)
    w_corr, sent, g, tok = block_forward(addr, ids, wc, od, w_star, horiz_div)
    xs = swap(sent, "px")
    flux, fl, tok = heat_flux(addr, tok, ids, wc, od, a2)
    pu = swap(ladder(swap(y_forward(xs, tok), "py"), fl), "py")
    back, tok = y_inverse(xs, pu)
    ys = swap(back, "px")
    theta, tok = new_theta(addr, tok, ids, flux, a2)
    w_new, temp_new = block_inverse(ys, g, w_corr, roof_level, ft, nr, hc, tok)
    return w_new, theta.reshape(LEV, ROWS, N), temp_new.reshape(1, OWNERS * SLOT)


def solution(mesh):
    field, facet = P("py", "px", None), P(("px", "py"), None)
    return jax.shard_map(
        body, mesh=mesh,
        in_specs=(field, field, field, P("px", None)) + (facet,) * 6,
        out_specs=(field, field, facet), check_vma=False)
```
